128 devices in a mesh: phase: 2 (over y_lo), dp: 64 (over z, y_hi, x, core).
Axes of the slice: x: 4, y: 4 (y_hi: 2, y_lo: 2; y = y_hi * 2 + y_lo), z: 4, core: 2. Of those that a mesh axis runs over, the one named last changes fastest.
Arguments:
- block_input: bfloat16 [2, 4096, 1536], P(None, 'dp'), may hold values from -6 to 6
- cotangent: bfloat16 [2, 4096, 1536], P(None, 'dp'), may hold values from -6 to 6
- segments: int32 [2, 64, 64], P(None, 'dp'), may hold values from 0 to 3, never falling along the last dimension, each value on 1 to 32 neighbouring positions
- routes: int32 [2, 4096, 6], P(None, 'dp'), may hold values from 0 to 63, all different within a row; in each aligned block of 64 rows (0 to 63, 64 to 127, ..., all dimensions but the last counted through in order) at most 7 rows name the same one
- in_proj: bfloat16 [1536, 6448], P(('phase', 'dp')), may hold values from -0.15625 to 0.15625
- conv_taps: bfloat16 [4, 3328], P(None, ('phase', 'dp')), may hold values from -3 to 3
- conv_bias: bfloat16 [3328], P(('phase', 'dp')), may hold values from -3 to 3
- step_bias: float32 [48], replicated, may hold values from -4 to -1
- decay_log: float32 [48], replicated, may hold values from 0 to 2.7
- skip_weight: float32 [48], replicated, may hold values from 0.5 to 1.5
- norm_gain: bfloat16 [3072], P(('phase', 'dp')), may hold values from 0.5 to 1.5
- out_proj: bfloat16 [3072, 1536], P(('phase', 'dp')), may hold values from -0.109375 to 0.109375
- query_proj: bfloat16 [1536, 1536], P(('phase', 'dp')), may hold values from -0.15625 to 0.15625
- key_value_projection: bfloat16 [1536, 1024], P(('phase', 'dp')), may hold values from -0.15625 to 0.15625
- attn_out_proj: bfloat16 [1536, 1536], P(('phase', 'dp')), may hold values from -0.4375 to 0.4375
- norm_gains: bfloat16 [2, 2, 1536], P('phase', None, 'dp'), may hold values from 0.5 to 1.5
- router: bfloat16 [2, 1536, 64], P('phase', 'dp'), may hold values from -0.078125 to 0.078125
- shared_in: bfloat16 [2, 1536, 2048], P('phase', 'dp'), may hold values from -0.15625 to 0.15625
- shared_out: bfloat16 [2, 1024, 1536], P('phase', 'dp'), may hold values from -0.1875 to 0.1875
- experts_in: bfloat16 [2, 64, 1536, 1024], P('phase', 'dp'), may hold values from -0.15625 to 0.15625
- experts_out: bfloat16 [2, 64, 512, 1536], P('phase', 'dp'), may hold values from -0.5 to 0.5
Outputs:
- phase_outputs: bfloat16 [2, 2, 4096, 1536], P('phase', None, 'dp')
- input_grads: float32 [2, 2, 4096, 1536], P('phase', None, 'dp')
- in_proj_grad: float32 [1536, 6448], P(('phase', 'dp'))
- conv_taps_grad: float32 [4, 3328], P(None, ('phase', 'dp'))
- conv_bias_grad: float32 [3328], P(('phase', 'dp'))
- step_bias_grad: float32 [48], replicated
- decay_log_grad: float32 [48], replicated
- skip_weight_grad: float32 [48], replicated
- norm_gain_grad: float32 [3072], P(('phase', 'dp'))
- out_proj_grad: float32 [3072, 1536], P(('phase', 'dp'))
- query_proj_grad: float32 [1536, 1536], P(('phase', 'dp'))
- keyval_proj_grad: float32 [1536, 1024], P(('phase', 'dp'))
- attn_out_proj_grad: float32 [1536, 1536], P(('phase', 'dp'))
- norm_gains_grad: float32 [2, 2, 1536], P('phase', None, 'dp')
- router_grad: float32 [2, 1536, 64], P('phase', 'dp')
- shared_in_grad: float32 [2, 1536, 2048], P('phase', 'dp')
- shared_out_grad: float32 [2, 1024, 1536], P('phase', 'dp')
- experts_in_grad: float32 [2, 64, 1536, 1024], P('phase', 'dp')
- experts_out_grad: float32 [2, 64, 512, 1536], P('phase', 'dp')
The draws below stay inside these ranges and needn't reach their ends.
Inputs may be any that keep to these rules, and one draw needn't show every extreme that they name: `segments`: never falls along a sequence; each segment has at most 32 tokens. `routes`: in each aligned block of 64 rows (the tokens of one sequence) no expert is named more than 7 times, a bound that some block reaches.
All inputs are finite; a program needn't handle non-finite values.
Results may differ from the reference program's by a relative error of at most 0.03.
Values may be sent and summed in bfloat16 or wider, within the bound.
A program may use at most 512 MiB of HBM per device.

```python
import math
import jax
import jax.numpy as jnp
import numpy as np
from jax import lax

MODEL_WIDTH = 1536
H = 48
P_SIZE = 64
N = 128
KW = 4
QUERY_HEADS = 12
KEY_VALUE_HEADS = 4
HEAD_SIZE = 128
F = 512
FS = 1024
TOPK = 6
SEQ = 64
MB = 2
EXPERTS = 64
CAP = 7
TOKENS = 4096
DI = 3072
CONVW = 3328
NIN = 6448
N_PHASE = 2
N_DP = 64


def levels(rng, shape, split, low, largest):
    loudness, own = 1.0, jax.random.fold_in(rng, 6)
    for axis_at, shards_of in split:
        steps = jnp.exp(jax.random.uniform(jax.random.fold_in(own, axis_at), (shards_of,), jnp.float32, low / len(split), largest / len(split)))
        loudness = loudness * jnp.repeat(steps, shape[axis_at] // shards_of).reshape([-1 if axis == axis_at else 1 for axis in range(len(shape))])
    return loudness


def profile(number_of, total, reach, lean):
    weights = [(1 << 20) // math.isqrt(grade ** lean) + 1 for grade in range(2, number_of + 1)]
    rest, counts = total - reach - (number_of - 1), [1] * (number_of - 1)
    while rest > 0:
        candidates = [i for i in range(number_of - 1) if counts[i] < reach]
        whole, left = sum([weights[i] for i in candidates]), rest
        for i in candidates:
            more = min(reach - counts[i], max(1, left * weights[i] // whole), rest)
            counts[i] = counts[i] + more
            rest = rest - more
    return np.array([reach] + counts)


def uneven_parts(key, number_of, total, most, lean):
    if number_of == 2:
        one = jax.random.randint(key, (), max(1, total - most), min(most, total - 1) + 1)
        return jnp.stack([one, total - one])
    tallies = jnp.asarray(profile(number_of, total, most, lean), jnp.int32)
    couples = (number_of - 1) // 2
    giver, sink = tallies[1:1 + 2 * couples:2], tallies[2:2 + 2 * couples:2]
    slack = jnp.minimum(giver - 1, most - sink)
    passed = jax.random.randint(jax.random.fold_in(key, 1), (couples,), 0, 1 << 20) % (slack + 1)
    tallies = tallies.at[1:1 + 2 * couples:2].set(giver - passed).at[2:2 + 2 * couples:2].set(sink + passed)
    return tallies[jax.random.permutation(jax.random.fold_in(key, 2), number_of)]


def routed_block(key, own, number, rows, count, top, bound, lean):
    order = jax.random.permutation(key, count)
    packed, usual = portions_of(count, rows * top, bound, lean, True), portions_of(count, rows * top, bound, lean, False)
    places = jnp.arange(count)

    def named(sizes, turn):
        used = int((sizes > 0).sum())
        fixed = max(1, used // 4)
        passed = fixed + (places - fixed + turn * (used - fixed)) % max(1, count - fixed)
        return jnp.zeros((count,), jnp.int32).at[order[jnp.where(places < fixed, places, passed)]].set(jnp.asarray(sizes, jnp.int32))

    sizes = jnp.where(number % 4 == 0, named(packed, number // 4), named(usual, number - number // 4 - 1))
    mixed = jax.random.permutation(jax.random.fold_in(own, 3), count)
    giver, sink = mixed[0:count // 2 * 2:2], mixed[1:count // 2 * 2:2]
    slack = jnp.minimum(sizes[giver] - 1, bound - sizes[sink]) // 2
    slack = jnp.where((giver == order[0]) | (sink == order[0]) | (sizes[sink] == 0), 0, jnp.maximum(slack, 0))
    passed = jax.random.randint(jax.random.fold_in(own, 4), (count // 2,), 0, 1 << 20) % (slack + 1)
    sizes = sizes.at[giver].add(-passed).at[sink].add(passed)
    labels = jnp.searchsorted(jnp.cumsum(sizes), jnp.arange(rows * top), side="right").astype(jnp.int32)
    grid = labels.reshape(top, rows).T
    grid = grid[jax.random.permutation(jax.random.fold_in(own, 1), rows)]
    turn = jax.random.randint(jax.random.fold_in(own, 2), (rows, 1), 0, top)
    return jnp.take_along_axis(grid, (jnp.arange(top)[None, :] + turn) % top, axis=1)


def portions_of(count, total, limit, slope, full):
    weights = [(1 << 20) // math.isqrt(standing ** slope) + 1 for standing in range(1, count + 1)]
    largest = limit if full else min(limit, max(-(-total // count), total * weights[0] // sum(weights)))
    least = 1 if total - largest >= count - 1 else 0
    holding, rest = [largest] + [least] * (count - 1), total - largest - least * (count - 1)
    while rest > 0:
        movable = [i for i in range(1, count) if holding[i] < largest] or [i for i in range(1, count) if holding[i] < limit]
        whole, left = sum([weights[i] for i in movable]), rest
        for i in movable:
            more = min(limit - holding[i], max(1, left * weights[i] // whole), rest)
            holding[i] = holding[i] + more
            rest = rest - more
    return np.array(holding)


def bell_draw(rng, extent, scale, limit, split=(), kind=jnp.bfloat16):
    values = scale * jax.random.normal(rng, extent, jnp.float32)
    if split:
        values = values * levels(rng, extent, split, -0.22, 0.18)
    return jnp.clip(values, -limit, limit).astype(kind)


def setup_inputs(seed: int = 0) -> dict:
    seeds = jax.random.split(jax.random.key(seed), 22)
    block_input = bell_draw(seeds[0], (MB, TOKENS, MODEL_WIDTH), 1.0, 6.0, ((1, 64),))
    cotangent = bell_draw(seeds[1], (MB, TOKENS, MODEL_WIDTH), 1.0, 6.0, ((1, 64),))
    segments = jax.vmap(lambda own: jnp.searchsorted(jnp.cumsum(uneven_parts(own, 4, SEQ, SEQ // 2, 0)), jnp.arange(SEQ), side="right"))(jax.random.split(seeds[2], MB * N_DP)).reshape((MB, N_DP, SEQ)).astype(jnp.int32)
    routes_keys = jax.random.split(jax.random.fold_in(seeds[3], 1), MB * TOKENS // SEQ)
    routes_turns = jax.random.permutation(jax.random.fold_in(seeds[3], 3), MB * TOKENS // SEQ)
    routes = jax.vmap(lambda own, number: routed_block(jax.random.fold_in(seeds[3], 2), own, number, SEQ, EXPERTS, TOPK, CAP, 2))(routes_keys, routes_turns).reshape((MB, TOKENS, TOPK))
    in_proj = bell_draw(seeds[4], (MODEL_WIDTH, NIN), MODEL_WIDTH ** -0.5, 0.15625, ((0, 128),))
    conv_taps = bell_draw(seeds[5], (KW, CONVW), KW ** -0.5, 3.0, ((1, 128),))
    conv_bias = bell_draw(seeds[6], (CONVW,), 0.5, 3.0, ((0, 128),))
    step_bias = jnp.clip(jax.random.uniform(seeds[7], (H,), jnp.float32, -4.0, -1.0), -4.0, -1.0)
    decay_log = jnp.clip(jax.random.uniform(seeds[8], (H,), jnp.float32, 0.0, 2.7), 0.0, 2.7)
    skip_weight = jnp.clip(jax.random.uniform(seeds[9], (H,), jnp.float32, 0.5, 1.5), 0.5, 1.5)
    norm_gain = jnp.clip(1.0 + 0.1 * jax.random.normal(seeds[10], (DI,), jnp.float32), 0.5, 1.5).astype(jnp.bfloat16)
    out_proj = bell_draw(seeds[11], (DI, MODEL_WIDTH), DI ** -0.5, 0.109375, ((0, 128),))
    query_proj = bell_draw(seeds[12], (MODEL_WIDTH, QUERY_HEADS * HEAD_SIZE), MODEL_WIDTH ** -0.5, 0.15625, ((0, 128),))
    key_value_projection = bell_draw(seeds[13], (MODEL_WIDTH, 2 * KEY_VALUE_HEADS * HEAD_SIZE), MODEL_WIDTH ** -0.5, 0.15625, ((0, 128),))
    attn_out_proj = bell_draw(seeds[14], (QUERY_HEADS * HEAD_SIZE, MODEL_WIDTH), (QUERY_HEADS * HEAD_SIZE // 8) ** -0.5, 0.4375, ((0, 128),))
    norm_gains = jnp.clip(1.0 + 0.1 * jax.random.normal(seeds[15], (N_PHASE, 2, MODEL_WIDTH), jnp.float32), 0.5, 1.5).astype(jnp.bfloat16)
    router = bell_draw(seeds[16], (N_PHASE, MODEL_WIDTH, EXPERTS), (4 * MODEL_WIDTH) ** -0.5, 0.078125, ((0, 2), (1, 64)))
    shared_in = bell_draw(seeds[17], (N_PHASE, MODEL_WIDTH, 2 * FS), MODEL_WIDTH ** -0.5, 0.15625, ((0, 2), (1, 64)))
    shared_out = bell_draw(seeds[18], (N_PHASE, FS, MODEL_WIDTH), FS ** -0.5, 0.1875, ((0, 2), (1, 64)))
    experts_in = bell_draw(seeds[19], (N_PHASE, EXPERTS, MODEL_WIDTH, 2 * F), MODEL_WIDTH ** -0.5, 0.15625, ((0, 2), (1, 64)))
    experts_out = bell_draw(seeds[20], (N_PHASE, EXPERTS, F, MODEL_WIDTH), (F // 4) ** -0.5, 0.5, ((0, 2), (1, 64)))
    return {"block_input": block_input, "cotangent": cotangent, "segments": segments, "routes": routes, "in_proj": in_proj, "conv_taps": conv_taps, "conv_bias": conv_bias, "step_bias": step_bias, "decay_log": decay_log, "skip_weight": skip_weight, "norm_gain": norm_gain, "out_proj": out_proj, "query_proj": query_proj, "key_value_projection": key_value_projection, "attn_out_proj": attn_out_proj, "norm_gains": norm_gains, "router": router, "shared_in": shared_in, "shared_out": shared_out, "experts_in": experts_in, "experts_out": experts_out}


eps = 1e-05

@jax.custom_vjp
def low(v):
    return lax.optimization_barrier(v.astype(jnp.bfloat16)).astype(jnp.float32)

@jax.custom_vjp
def low_back(v):
    return v

def low_keep(v):
    return (low(v), None)

def low_pass(kept, grad):
    return (grad,)

def back_keep(v):
    return (v, None)

def back_low(kept, grad):
    return (low(grad),)
low.defvjp(low_keep, low_pass)
low_back.defvjp(back_keep, back_low)

def matmul(left, right):
    return jnp.dot(left, right, precision=lax.Precision.HIGHEST, preferred_element_type=jnp.float32)

def rms_scale(value, gain):
    return value * lax.rsqrt(lax.optimization_barrier(jnp.mean(value * value, axis=-1, keepdims=True)) + eps) * gain

def swiglu(value):
    half = value.shape[-1] // 2
    return jax.nn.silu(value[..., :half]) * value[..., half:]

def mamba_core(projected_rows, seg, conv_taps, conv_bias, step_bias, decay_log, skip_weight, norm_gain):
    projected_rows = low_back(projected_rows)
    length_total = projected_rows.shape[0]
    gate_part = projected_rows[:, :DI]
    conv_in = projected_rows[:, DI:DI + CONVW]
    step_raw = projected_rows[:, DI + CONVW:]
    padded = jnp.pad(conv_in, ((KW - 1, 0), (0, 0)))
    seg_pad = jnp.concatenate([jnp.full((KW - 1,), -1, jnp.int32), seg.astype(jnp.int32)])
    conv = jnp.zeros_like(conv_in) + conv_bias[None, :]
    for tap in range(KW):
        same = (seg_pad[tap:tap + length_total] == seg).astype(conv_in.dtype)
        conv = conv + conv_taps[tap][None, :] * padded[tap:tap + length_total] * same[:, None]
    active = jax.nn.silu(conv)
    value_rows = active[:, :DI].reshape(length_total, H, P_SIZE)
    in_state = active[:, DI:DI + N]
    out_state = active[:, DI + N:]
    step = jax.nn.softplus(step_raw + step_bias[None, :])
    total = jnp.cumsum(step * (-jnp.exp(decay_log))[None, :], axis=0)
    position = jnp.arange(length_total, dtype=jnp.int32)
    allowed = (position[:, None] >= position[None, :]) & (seg[:, None] == seg[None, :])
    spread = total.T[:, :, None] - total.T[:, None, :]
    decay = jnp.where(allowed[None], jnp.exp(jnp.minimum(spread, 0.0)), 0.0)
    intersection = matmul(out_state, in_state.T)
    mixing = decay * intersection[None] * step.T[:, None, :]
    result = jnp.einsum('hij,jhp->ihp', mixing, value_rows, precision=lax.Precision.HIGHEST)
    result = result + skip_weight[None, :, None] * value_rows
    gated = result.reshape(length_total, DI) * jax.nn.silu(gate_part)
    return low(rms_scale(gated, norm_gain))

def attend_core(projected_rows, seg):
    projected_rows = low(low_back(projected_rows))
    length_total = projected_rows.shape[0]
    query_width = QUERY_HEADS * HEAD_SIZE
    query_rows = projected_rows[:, :query_width].reshape(length_total, KEY_VALUE_HEADS, QUERY_HEADS // KEY_VALUE_HEADS, HEAD_SIZE)
    key_rows = projected_rows[:, query_width:query_width + KEY_VALUE_HEADS * HEAD_SIZE].reshape(length_total, KEY_VALUE_HEADS, HEAD_SIZE)
    value_rows = projected_rows[:, query_width + KEY_VALUE_HEADS * HEAD_SIZE:].reshape(length_total, KEY_VALUE_HEADS, HEAD_SIZE)
    scores = jnp.einsum('igrd,jgd->grij', query_rows, key_rows, precision=lax.Precision.HIGHEST) * HEAD_SIZE ** (-0.5)
    position = jnp.arange(length_total, dtype=jnp.int32)
    allowed = (position[:, None] >= position[None, :]) & (seg[:, None] == seg[None, :])
    scores = jnp.where(allowed[None, None], scores, -1e+30)
    probs = low(jax.nn.softmax(scores, axis=-1))
    heads = jnp.einsum('grij,jgd->igrd', probs, value_rows, precision=lax.Precision.HIGHEST)
    return low(heads.reshape(length_total, query_width))

def slot_of(block_routes):
    hits = (block_routes[:, None] == jnp.arange(EXPERTS, dtype=jnp.int32)[None, :]).astype(jnp.int32)
    before = jnp.cumsum(hits, axis=0) - hits
    return lax.optimization_barrier(jnp.sum(before * hits, axis=1))

def phase_forward(inp, seg_rows, flat_routes, mixer_fn, gain_rows, router, shared_in, shared_out, experts_in, experts_out):
    rows = inp.reshape(MB * N_DP, SEQ, MODEL_WIDTH)

    def mix_row(pair):
        row, row_seg = pair
        return mixer_fn(low(rms_scale(row, gain_rows[0])), row_seg)
    hidden = rows + lax.map(jax.checkpoint(mix_row), (rows, seg_rows))
    flat = hidden.reshape(MB * TOKENS, MODEL_WIDTH)
    normed = low(rms_scale(flat, gain_rows[1]))
    logits = matmul(normed, router)
    chosen = jnp.take_along_axis(logits, flat_routes, axis=1)
    gates = jax.nn.softmax(chosen, axis=1)
    blocks = flat_routes.reshape(MB * N_DP, SEQ * TOPK)
    slots = jax.vmap(slot_of)(blocks)
    block_ids = jnp.arange(MB * N_DP, dtype=jnp.int32)
    place = (block_ids * CAP)[:, None] + slots
    token = (block_ids * SEQ)[:, None] + (jnp.arange(SEQ * TOPK, dtype=jnp.int32) // TOPK)[None, :]
    source = jnp.zeros((EXPERTS, MB * N_DP * CAP), jnp.int32).at[blocks, place].set(token)

    def run_expert(items):
        src, w_in, w_out = items
        taken = low_back(normed[src])
        both = low_back(matmul(taken, w_in))
        hid = low(swiglu(both))
        return low_back(low(matmul(hid, w_out)))
    answers = lax.map(jax.checkpoint(run_expert), (source, experts_in, experts_out))
    picked = answers[blocks, place].reshape(MB * TOKENS, TOPK, MODEL_WIDTH)
    moe = lax.optimization_barrier(jnp.sum(gates[:, :, None] * picked, axis=1))
    shared_both = low_back(matmul(normed, shared_in))
    shared = low_back(matmul(low(swiglu(shared_both)), shared_out))
    return (flat + moe + shared).reshape(MB, TOKENS, MODEL_WIDTH)

def as_float(value):
    return value.astype(jnp.float32)

def reference(block_input, cotangent, segments, routes, in_proj, conv_taps, conv_bias, step_bias, decay_log, skip_weight, norm_gain, out_proj, query_proj, key_value_projection, attn_out_proj, norm_gains, router, shared_in, shared_out, experts_in, experts_out):
    seg_rows = segments.reshape(MB * N_DP, SEQ).astype(jnp.int32)
    flat_routes = routes.reshape(MB * TOKENS, TOPK).astype(jnp.int32)

    def forward(inp, probe, in_proj, conv_taps, conv_bias, step_bias, decay_log, skip_weight, norm_gain, out_proj, query_proj, key_value_projection, attn_out_proj, norm_gains, router, shared_in, shared_out, experts_in, experts_out):

        def mamba_fn(first_norm, seg):
            projected_rows = matmul(first_norm, in_proj)
            normed = mamba_core(projected_rows, seg, conv_taps, conv_bias, step_bias, decay_log, skip_weight, norm_gain)
            return low_back(matmul(normed, out_proj))

        def attend_fn(first_norm, seg):
            projected_rows = jnp.concatenate([matmul(first_norm, query_proj), matmul(first_norm, key_value_projection)], axis=1)
            return low_back(matmul(attend_core(projected_rows, seg), attn_out_proj))
        first = phase_forward(inp, seg_rows, flat_routes, mamba_fn, norm_gains[0], router[0], shared_in[0], shared_out[0], experts_in[0], experts_out[0])
        sent = low(first)
        second = phase_forward(low_back(sent + probe), seg_rows, flat_routes, attend_fn, norm_gains[1], router[1], shared_in[1], shared_out[1], experts_in[1], experts_out[1])
        return (second, sent)
    primals = (as_float(block_input), jnp.zeros((MB, TOKENS, MODEL_WIDTH), jnp.float32), as_float(in_proj), as_float(conv_taps), as_float(conv_bias), step_bias, decay_log, skip_weight, as_float(norm_gain), as_float(out_proj), as_float(query_proj), as_float(key_value_projection), as_float(attn_out_proj), as_float(norm_gains), as_float(router), as_float(shared_in), as_float(shared_out), as_float(experts_in), as_float(experts_out))
    final, pullback, sent = jax.vjp(forward, *primals, has_aux=True)
    grads = pullback(as_float(cotangent))
    phase_outputs = jnp.stack([sent, final]).astype(jnp.bfloat16)
    input_grads = jnp.stack([grads[0], grads[1]])
    return (phase_outputs, input_grads, grads[2], grads[3], grads[4], grads[5], grads[6], grads[7], grads[8], grads[9], grads[10], grads[11], grads[12], grads[13], grads[14], grads[15], grads[16], grads[17], grads[18])
```

```python
import functools

import jax
import jax.numpy as jnp
from jax import lax
from jax.experimental import pallas as pl
from jax.experimental.pallas import tpu as pltpu
from jax.sharding import Mesh
from jax.sharding import PartitionSpec as P

H = 48
P_SIZE = 64
N = 128
KW = 4
QUERY_HEADS = 12
KEY_VALUE_HEADS = 4
HEAD_SIZE = 128
DI = 3072
CONVW = 3328
WIDTH = 1536
SEQ = 64
EXPERTS = 64
SLOTS = 8
PARTS = 8
HEADS_HERE = H // PARTS
INNER = DI // PARTS
IN_COLS = 1152
QKV_COLS = 640

SIZES = {"phase": 2, "zh": 2, "zl": 2, "r": 16}
TEAM = ("phase", "zh", "zl")
HALF = ("phase", "zh")
DP = ("zh", "zl", "r")
ALL = ("phase", "zh", "zl", "r")

eps = 1e-05
single = jnp.float32
brain = jnp.bfloat16


def place_of(axes, index):
    out = {}
    for name in reversed(axes):
        out[name] = lax.rem(index, SIZES[name])
        index = lax.div(index, SIZES[name])
    return out


def size_of(axes):
    total = 1
    for name in axes:
        total *= SIZES[name]
    return total


def exchange_kernel(axes, modes, *refs):
    count = len(modes)
    sources, targets = refs[:count], refs[count : 2 * count]
    send_sem, recv_sem, own_sem = refs[2 * count :]
    n = size_of(axes)
    me = jnp.int32(0)
    for name in axes:
        me = me * SIZES[name] + lax.axis_index(name)
    barrier = pltpu.get_barrier_semaphore()
    for k in range(1, n):
        pl.semaphore_signal(
            barrier,
            inc=1,
            device_id=place_of(axes, lax.rem(me + k, n)),
            device_id_type=pl.DeviceIdType.MESH,
        )
    pl.semaphore_wait(barrier, n - 1)
    copies = []
    for k in range(1, n):
        peer = lax.rem(me + k, n)
        for item, mode in enumerate(modes):
            if mode == "pair" and k != n // 2:
                continue
            slot, source = me, sources[item]
            if mode == "swap":
                source = source.at[peer]
            if mode == "pair":
                source = source.at[lax.div(peer, n // 2)]
                slot = lax.div(me, n // 2)
            copy = pltpu.make_async_remote_copy(
                src_ref=source,
                dst_ref=targets[item].at[slot],
                send_sem=send_sem.at[item, k],
                recv_sem=recv_sem.at[item, k],
                device_id=place_of(axes, peer),
                device_id_type=pl.DeviceIdType.MESH,
            )
            copy.start()
            copies.append(copy)
    own = []
    for item, mode in enumerate(modes):
        slot = lax.div(me, n // 2) if mode == "pair" else me
        source = sources[item] if mode == "gather" else sources[item].at[slot]
        copy = pltpu.make_async_copy(source, targets[item].at[slot], own_sem.at[item])
        copy.start()
        own.append(copy)
    for copy in own:
        copy.wait()
    for copy in copies:
        copy.wait()


def exchange(items, axes, number, name):
    n = size_of(axes)
    modes = tuple(mode for _, mode in items)
    arrays = [array for array, _ in items]
    shapes = [
        jax.ShapeDtypeStruct(((n,) if mode == "gather" else ()) + array.shape, array.dtype)
        for array, mode in items
    ]
    sent = sum(s.size * s.dtype.itemsize for s in shapes)
    return pl.pallas_call(
        functools.partial(exchange_kernel, axes, modes),
        out_shape=shapes,
        in_specs=[pl.BlockSpec(memory_space=pltpu.VMEM)] * len(items),
        out_specs=[pl.BlockSpec(memory_space=pltpu.VMEM)] * len(items),
        scratch_shapes=[
            pltpu.SemaphoreType.DMA((len(items), n)),
            pltpu.SemaphoreType.DMA((len(items), n)),
            pltpu.SemaphoreType.DMA((len(items),)),
        ],
        compiler_params=pltpu.CompilerParams(
            collective_id=number, has_side_effects=True, vmem_limit_bytes=32 << 20
        ),
        cost_estimate=pl.CostEstimate(
            flops=0, bytes_accessed=2 * sent, transcendentals=0
        ),
        name=name,
    )(*arrays)


def dot(left, right):
    return jnp.dot(left, right, preferred_element_type=single)


def dot_t(left, right):
    return lax.dot_general(left, right, (((1,), (1,)), ((), ())), preferred_element_type=single)


def t_dot(left, right):
    return lax.dot_general(left, right, (((0,), (0,)), ((), ())), preferred_element_type=single)


def exact(spec, left, right):
    return jnp.einsum(
        spec, left, right, precision=lax.Precision.HIGHEST, preferred_element_type=single
    )


def rms_scale(value, gain):
    return value * lax.rsqrt(jnp.mean(value * value, axis=-1, keepdims=True) + eps) * gain


def swiglu(value):
    half = value.shape[-1] // 2
    return jax.nn.silu(value[..., :half]) * value[..., half:]


def shuffle(value):
    rows = value.shape[0]
    return value.reshape(rows, 8, 16, 12).transpose(0, 2, 1, 3).reshape(rows, WIDTH)


def unshuffle(value):
    rows = value.shape[0]
    return value.reshape(rows, 16, 8, 12).transpose(0, 2, 1, 3).reshape(rows, WIDTH)


def pad_rows(value, rows):
    return jnp.pad(value, [(0, 0)] * (value.ndim - 2) + [(0, rows - value.shape[-2]), (0, 0)])


def pad_to(value, rows, columns):
    return jnp.pad(value, ((0, rows - value.shape[0]), (0, columns - value.shape[1])))


def allowed_pairs(seg):
    position = jnp.arange(SEQ, dtype=jnp.int32)
    return (position[:, None] >= position[None, :]) & (seg[..., :, None] == seg[..., None, :])


def mamba_core(zx, seg, taps, bias, step_bias, decay_log, skip):
    rows = zx.shape[0]
    gate_part = zx[..., :INNER]
    conv_in = zx[..., INNER : 2 * INNER + 2 * N]
    step_raw = zx[..., 2 * INNER + 2 * N : 2 * INNER + 2 * N + HEADS_HERE]
    padded = jnp.pad(conv_in, ((0, 0), (KW - 1, 0), (0, 0)))
    seg_pad = jnp.pad(seg, ((0, 0), (KW - 1, 0)), constant_values=-1)
    conv = jnp.zeros_like(conv_in) + bias
    for tap in range(KW):
        same = (seg_pad[:, tap : tap + SEQ] == seg).astype(single)
        conv = conv + taps[tap] * padded[:, tap : tap + SEQ] * same[:, :, None]
    active = jax.nn.silu(conv)
    values = active[..., :INNER].reshape(rows, SEQ, HEADS_HERE, P_SIZE)
    in_state = active[..., INNER : INNER + N]
    out_state = active[..., INNER + N :]
    step = jax.nn.softplus(step_raw + step_bias)
    total = jnp.cumsum(step * (-jnp.exp(decay_log)), axis=1)
    allowed = allowed_pairs(seg)
    step_t = step.transpose(0, 2, 1)
    total_t = total.transpose(0, 2, 1)
    spread = total_t[..., :, None] - total_t[..., None, :]
    decay = jnp.where(allowed[:, None], jnp.exp(jnp.minimum(spread, 0.0)), 0.0)
    meeting = exact("nis,njs->nij", out_state, in_state)
    mixing = decay * meeting[:, None] * step_t[:, :, None, :]
    result = exact("nhij,njhp->nihp", mixing, values)
    result = result + skip[:, None] * values
    return result.reshape(rows, SEQ, INNER) * jax.nn.silu(gate_part)


def attend_scores(queries, keys, seg):
    scores = exact("nird,njd->nrij", queries, keys) * HEAD_SIZE ** (-0.5)
    scores = jnp.where(allowed_pairs(seg)[:, None], scores, -1e30)
    return jax.nn.softmax(scores, axis=-1)


def attend_mix(probs, values):
    return exact("nrij,njd->nird", probs, values)


def per_device(
    block_input,
    cotangent,
    segments,
    routes,
    in_proj,
    conv_taps,
    conv_bias,
    step_bias,
    decay_log,
    skip_weight,
    norm_gain,
    out_proj,
    query_proj,
    key_value_projection,
    attn_out_proj,
    norm_gains,
    router,
    shared_in,
    shared_out,
    experts_in,
    experts_out,
):
    phase = lax.axis_index("phase")
    first_phase = phase == 0
    zl = lax.axis_index("zl")
    team = phase * 4 + lax.axis_index("zh") * 2 + zl

    def mine(value):
        return lax.dynamic_index_in_dim(value, phase, 0, keepdims=False)

    start = mine(block_input)
    cot = mine(cotangent)
    seg = mine(segments)
    route_rows = mine(routes)

    both_ways = [(0, 1), (1, 0)]
    w_in_own, w_out_own = experts_in[0, 0], experts_out[0, 0]
    w_in_far = lax.ppermute(w_in_own, "phase", both_ways)
    w_out_far = lax.ppermute(w_out_own, "phase", both_ways)

    z_piece = in_proj[:, :DI].reshape(12, PARTS, INNER).transpose(1, 0, 2)
    x_piece = in_proj[:, DI : 2 * DI].reshape(12, PARTS, INNER).transpose(1, 0, 2)
    state_piece = jnp.broadcast_to(in_proj[None, :, 2 * DI : 2 * DI + 2 * N], (PARTS, 12, 2 * N))
    step_piece = in_proj[:, 2 * DI + 2 * N :].reshape(12, PARTS, HEADS_HERE).transpose(1, 0, 2)
    step_piece = jnp.pad(step_piece, ((0, 0), (0, 0), (0, 128 - HEADS_HERE)))
    q_piece = query_proj.reshape(12, 4, 384).transpose(1, 0, 2)
    kv_piece = key_value_projection.reshape(12, 2, 4, 128).transpose(2, 0, 1, 3).reshape(4, 12, 256)
    qkv_piece = jnp.repeat(jnp.concatenate([q_piece, kv_piece], axis=2), 2, axis=0)
    main_piece = pad_rows(
        jnp.concatenate([z_piece, x_piece, state_piece, step_piece, qkv_piece], axis=2), 16
    )
    sin_piece = shared_in[0].reshape(24, 2, 4, 16, 2, 8).transpose(4, 2, 0, 1, 3, 5)
    sin_piece = pad_rows(sin_piece.reshape(PARTS, 24, 256), 32)
    sout_piece = pad_rows(shared_out[0].reshape(2, 8, WIDTH), 16)
    small = jnp.concatenate(
        [
            pad_to(router[0], 24, 128),
            pad_to(conv_taps, 4, 128),
            pad_to(conv_bias[None], 1, 128),
            pad_to(norm_gain[None], 1, 128),
            pad_to(norm_gains[0], 2, 128),
        ],
        axis=0,
    )
    seg_piece = pad_to(seg, 8, 128)
    main_got, sin_got, sout_got, small_got, seg_got, start_all, cot_all = exchange(
        [
            (main_piece, "swap"),
            (sin_piece, "swap"),
            (sout_piece, "pair"),
            (small, "gather"),
            (seg_piece, "gather"),
            (shuffle(start), "gather"),
            (cot, "gather"),
        ],
        TEAM,
        0,
        "team_start",
    )
    seg_all = seg_got[:, 0, :SEQ]
    main_got = main_got[:, :12].reshape(96, IN_COLS + QKV_COLS)
    w_in = lax.all_gather(main_got[:, :IN_COLS], "r", axis=0, tiled=True)
    small_all = lax.all_gather(small_got, "r", axis=0)
    w_out = lax.all_gather(out_proj, "r", axis=0, tiled=True)
    sin_all = lax.all_gather(sin_got[:, :24], "r", axis=0)
    sout_all = lax.all_gather(sout_got[:, :8], "r", axis=0)
    w_qkv = lax.all_gather(main_got[:, IN_COLS:], "r", axis=0, tiled=True)
    w_attn = lax.all_gather(attn_out_proj, ("zl", "r"), axis=0, tiled=True)

    sin_full = sin_all.reshape(16, 2, 4, 24, 256).transpose(1, 2, 0, 3, 4).reshape(2, WIDTH, 256)
    sout_full = sout_all.transpose(1, 0, 2, 3).reshape(2, 128, WIDTH)
    small_all = small_all.reshape(16, 2, 4, 32, 128)
    router_full = small_all[:, :, :, :24, :EXPERTS].transpose(1, 2, 0, 3, 4)
    router_full = router_full.reshape(2, WIDTH, EXPERTS)
    conv_full = small_all[:, :, :, 24:29, :26].transpose(3, 1, 2, 0, 4).reshape(5, CONVW)
    conv_full = conv_full.astype(single)
    gain_here = small_all.reshape(16, 8, 32, 128)[:, :, 29, :24]
    gain_here = lax.dynamic_index_in_dim(gain_here, team, 1, keepdims=False)
    gain_here = gain_here.reshape(INNER).astype(single)
    gains = small_all[:, :, :, 30:32, :24].transpose(1, 3, 2, 0, 4).reshape(2, 2, WIDTH)
    gains = gains.astype(single)
    conv_here = jnp.concatenate(
        [lax.dynamic_slice_in_dim(conv_full[:, :DI], team * INNER, INNER, 1), conv_full[:, DI:]],
        axis=1,
    )
    taps_here, bias_here = conv_here[:KW], conv_here[KW]

    def heads_of(value):
        return lax.dynamic_slice_in_dim(value, team * HEADS_HERE, HEADS_HERE, 0)

    step_here, decay_here, skip_here = (
        heads_of(step_bias),
        heads_of(decay_log),
        heads_of(skip_weight),
    )

    expert_ids = jnp.arange(EXPERTS, dtype=jnp.int32)
    named = jnp.any(route_rows[:, :, None] == expert_ids, axis=1)
    position = jnp.arange(SEQ, dtype=jnp.int32)
    earlier = (position[:, None] > position[None, :]).astype(brain)
    slot = dot(earlier, named.astype(brain))
    slot = jnp.where(named, slot, -1.0).astype(brain)
    cell = jnp.arange(EXPERTS * SLOTS, dtype=jnp.int32)
    spread = (cell[None, :] // SLOTS == expert_ids[:, None]).astype(brain)
    taken = dot(slot, spread) == (cell % SLOTS).astype(single)
    taken_b = taken.astype(brain)

    def to_experts(rows):
        return lax.all_to_all(
            rows.reshape(EXPERTS, SLOTS, WIDTH), DP, split_axis=0, concat_axis=0, tiled=True
        ).reshape(EXPERTS * SLOTS, WIDTH)

    def of_block(s):
        own = phase == s
        return jnp.where(own, w_in_own, w_in_far), jnp.where(own, w_out_own, w_out_far)

    def moe_forward(s, hidden, number):
        normed = rms_scale(hidden, gains[s, 1]).astype(brain)
        logits = dot(normed, router_full[s])
        top = jnp.max(jnp.where(named, logits, -jnp.inf), axis=1, keepdims=True)
        weight = jnp.where(named, jnp.exp(logits - top), 0.0)
        gates = weight / jnp.sum(weight, axis=1, keepdims=True)
        gates_wide = jnp.where(taken, exact("ie,ec->ic", gates, spread.astype(single)), 0.0)
        gate_cell = jnp.sum(gates_wide, axis=0)
        rows_in = to_experts(t_dot(taken_b, normed).astype(brain))
        (normed_all,) = exchange([(normed, "gather")], TEAM, number, f"team_n2_{s}")
        normed_all = normed_all.reshape(PARTS * SEQ, WIDTH)
        shared_both = dot(normed_all, sin_full[s])
        shared_hid = swiglu(shared_both).astype(brain)
        shared_part = dot(shared_hid, sout_full[s]).astype(brain).reshape(PARTS, SEQ, WIDTH)
        (shared_got,) = exchange([(shared_part, "swap")], TEAM, number + 1, f"team_shared_{s}")
        w_first, w_second = of_block(s)
        both = dot(rows_in, w_first)
        hid = swiglu(both).astype(brain)
        answer = dot(hid, w_second).astype(brain)
        back = to_experts(answer)
        high = gates_wide.astype(brain)
        lower = (gates_wide - high.astype(single)).astype(brain)
        moe = dot(high, back) + dot(lower, back)
        output = hidden + moe + jnp.sum(shared_got.astype(single), axis=0)
        kept = (
            hidden,
            normed,
            gates,
            gate_cell,
            back,
            rows_in,
            both,
            hid,
            normed_all,
            shared_both,
            shared_hid,
        )
        return output.astype(brain), kept

    def moe_backward(s, d_out, d_out_all, kept, number):
        (
            hidden,
            normed,
            gates,
            gate_cell,
            back,
            rows_in,
            both,
            hid,
            normed_all,
            shared_both,
            shared_hid,
        ) = kept
        d_rows_out = dot(taken_b.T, d_out) * gate_cell[:, None]
        d_answer = to_experts(d_rows_out.astype(brain))
        d_cells = jnp.where(taken, dot_t(d_out, back), 0.0)
        d_gates = exact("ic,ec->ie", d_cells, spread.astype(single))
        d_logits = gates * (d_gates - jnp.sum(gates * d_gates, axis=1, keepdims=True))
        d_normed = exact("ie,we->iw", d_logits, router_full[s].astype(single))
        d_router = exact("iw,ie->we", normed.astype(single), d_logits)
        d_shid = dot_t(d_out_all, sout_full[s])
        d_sout = t_dot(shared_hid, d_out_all)
        d_sboth = jax.vjp(swiglu, shared_both)[1](d_shid)[0].astype(brain)
        d_sin = t_dot(normed_all, d_sboth)
        d_shared = dot_t(d_sboth, sin_full[s]).astype(brain).reshape(PARTS, SEQ, WIDTH)
        (d_shared_got,) = exchange([(d_shared, "swap")], TEAM, number, f"team_dshared_{s}")
        w_first, w_second = of_block(s)
        d_hid = dot_t(d_answer, w_second)
        d_w_second = t_dot(hid, d_answer)
        d_both = jax.vjp(swiglu, both)[1](d_hid)[0].astype(brain)
        d_w_first = t_dot(rows_in, d_both)
        d_rows = dot_t(d_both, w_first).astype(brain)
        returned = to_experts(d_rows)
        d_normed = d_normed + dot(taken_b, returned) + jnp.sum(d_shared_got.astype(single), axis=0)
        d_hidden, d_gain = jax.vjp(rms_scale, hidden, gains[s, 1])[1](d_normed)
        d_hidden = d_hidden + d_out.astype(single)
        return d_hidden, d_gain, d_router, d_sin, d_sout, d_w_first, d_w_second

    u0 = start.astype(single)
    shuffled_gain = shuffle(gains[0, 0][None])[0]
    n1_all = rms_scale(start_all.astype(single), shuffled_gain).astype(brain)
    n1_all = n1_all.reshape(PARTS * SEQ, WIDTH)
    zx = dot(n1_all, w_in).reshape(PARTS, SEQ, IN_COLS)

    def core(zx, taps, bias, step_bias, decay_log, skip):
        return mamba_core(zx, seg_all, taps, bias, step_bias, decay_log, skip)

    core_args = (zx, taps_here, bias_here, step_here, decay_here, skip_here)
    gated, core_pull = jax.vjp(core, *core_args)
    squares = jnp.sum(gated * gated, axis=-1)
    part = dot((gated * gain_here).astype(brain).reshape(PARTS * SEQ, INNER), w_out)
    part = part.astype(brain).reshape(PARTS, SEQ, WIDTH)
    squares = jnp.pad(squares[:, None], ((0, 0), (0, 7), (0, 128 - SEQ)))
    part_got, squares_got = exchange([(part, "swap"), (squares, "swap")], TEAM, 1, "team_mixed_0")
    mean_square = jnp.sum(squares_got[:, 0, :SEQ], axis=0) / DI
    inverse = lax.rsqrt(mean_square + eps)
    mixed0 = jnp.sum(part_got.astype(single), axis=0) * inverse[:, None]
    out0, kept0 = moe_forward(0, u0 + mixed0, 2)

    u1 = out0.astype(single)
    n1 = rms_scale(u1, gains[1, 0]).astype(brain)
    (n1_half,) = exchange([(shuffle(n1), "gather")], HALF, 4, "half_n1")
    n1_half = n1_half.reshape(4 * SEQ, WIDTH)
    seg_half = lax.dynamic_index_in_dim(seg_all.reshape(4, 2, SEQ), zl, 1, keepdims=False)
    qkv = dot(n1_half, w_qkv).astype(brain).astype(single).reshape(4, SEQ, QKV_COLS)
    queries = qkv[..., :384].reshape(4, SEQ, 3, HEAD_SIZE)
    keys, values = qkv[..., 384:512], qkv[..., 512:]
    probs, score_pull = jax.vjp(lambda q, k: attend_scores(q, k, seg_half), queries, keys)
    heads, mix_pull = jax.vjp(attend_mix, probs.astype(brain).astype(single), values)
    heads = heads.astype(brain).reshape(4 * SEQ, 384)
    part1 = dot(heads, w_attn).astype(brain).reshape(4, SEQ, WIDTH)
    (part1_got,) = exchange([(part1, "swap")], HALF, 5, "half_mixed")
    mixed1 = jnp.sum(part1_got.astype(single), axis=0)
    out1, kept1 = moe_forward(1, u1 + mixed1, 6)

    cot_all = cot_all.reshape(PARTS * SEQ, WIDTH)
    d_hid1, d_gain11, d_router1, d_sin1, d_sout1, d_first1, d_second1 = moe_backward(
        1, cot, cot_all, kept1, 8
    )
    far_first1 = lax.ppermute(d_first1.astype(brain), "phase", [(0, 1)])
    far_second1 = lax.ppermute(d_second1.astype(brain), "phase", [(0, 1)])
    (d_mixed1,) = exchange([(d_hid1.astype(brain), "gather")], HALF, 9, "half_dmixed")
    d_mixed1 = d_mixed1.reshape(4 * SEQ, WIDTH)
    d_heads = dot_t(d_mixed1, w_attn).reshape(4, SEQ, 3, HEAD_SIZE)
    d_attn = t_dot(heads, d_mixed1)
    d_probs, d_values = mix_pull(d_heads)
    d_queries, d_keys = score_pull(d_probs)
    d_qkv = jnp.concatenate([d_queries.reshape(4, SEQ, 384), d_keys, d_values], axis=2)
    d_qkv = d_qkv.astype(brain).reshape(4 * SEQ, QKV_COLS)
    d_w_qkv = t_dot(n1_half, d_qkv)
    d_n1_part = dot_t(d_qkv, w_qkv).astype(brain).reshape(4, SEQ, WIDTH)
    (d_n1_got,) = exchange([(d_n1_part, "swap")], HALF, 10, "half_dn1")
    d_n1 = unshuffle(jnp.sum(d_n1_got.astype(single), axis=0))
    d_u1, d_gain10 = jax.vjp(rms_scale, u1, gains[1, 0])[1](d_n1)
    d_u1 = (d_u1 + d_hid1).astype(brain)

    (d_out0_all,) = exchange([(d_u1, "gather")], TEAM, 11, "team_dout")
    d_out0_all = d_out0_all.reshape(PARTS * SEQ, WIDTH)
    d_hid0, d_gain01, d_router0, d_sin0, d_sout0, d_first0, d_second0 = moe_backward(
        0, d_u1, d_out0_all, kept0, 12
    )
    far_first0 = lax.ppermute(d_first0.astype(brain), "phase", [(1, 0)])
    far_second0 = lax.ppermute(d_second0.astype(brain), "phase", [(1, 0)])
    d_mixed0 = d_hid0.astype(brain)
    along = jnp.sum(d_mixed0.astype(single) * mixed0, axis=1)
    scalars = jnp.stack([inverse, inverse * inverse * along / DI])
    d_mixed0, scalars_all = exchange(
        [(d_mixed0, "gather"), (pad_to(scalars, 8, 128), "gather")], TEAM, 13, "team_dmixed"
    )
    d_mixed0 = d_mixed0.reshape(PARTS * SEQ, WIDTH)
    inverse_all = scalars_all[:, 0, :SEQ, None]
    along_all = scalars_all[:, 1, :SEQ, None]
    d_yn = dot_t(d_mixed0, w_out).reshape(PARTS, SEQ, INNER)
    unit = gated * inverse_all
    yn = (unit * gain_here).astype(brain).reshape(PARTS * SEQ, INNER)
    d_w_out = t_dot(yn, d_mixed0)
    d_norm_gain = jnp.sum(d_yn * unit, axis=(0, 1))
    d_gated = inverse_all * gain_here * d_yn - gated * along_all
    d_zx, d_taps, d_bias, d_step, d_decay, d_skip = core_pull(d_gated)
    d_zx = d_zx.astype(brain).reshape(PARTS * SEQ, IN_COLS)
    d_w_in = t_dot(n1_all, d_zx)
    d_n1_part0 = dot_t(d_zx, w_in).astype(brain).reshape(PARTS, SEQ, WIDTH)
    (d_n1_got0,) = exchange([(d_n1_part0, "swap")], TEAM, 14, "team_dn1")
    d_n1_0 = unshuffle(jnp.sum(d_n1_got0.astype(single), axis=0))
    d_u0, d_gain00 = jax.vjp(rms_scale, u0, gains[0, 0])[1](d_n1_0)
    d_u0 = d_u0 + d_hid0

    def by_block(block0, block1):
        keep = jnp.where(first_phase, block0, block1)
        give = jnp.where(first_phase, block1, block0)
        got = lax.ppermute(give, "phase", both_ways)
        return jnp.where(first_phase, jnp.stack([keep, got]), jnp.stack([got, keep]))[None]

    phase_outputs = by_block(out0, out1)
    input_grads = by_block(d_u0, d_u1.astype(single))
    experts_in_grad = jnp.where(
        first_phase, d_first0 + far_first0.astype(single), d_first1 + far_first1.astype(single)
    )
    experts_out_grad = jnp.where(
        first_phase, d_second0 + far_second0.astype(single), d_second1 + far_second1.astype(single)
    )

    def scatter(value):
        return lax.psum_scatter(value, "r", scatter_dimension=0, tiled=True)

    def shared_in_parts(value):
        return value.astype(brain).reshape(4, 16, 24, 256).transpose(1, 0, 2, 3)

    qkv_part = scatter(d_w_qkv.astype(brain)).reshape(PARTS, 12, QKV_COLS)
    attn_out_grad = lax.psum_scatter(
        d_attn.astype(brain), ("zl", "r"), scatter_dimension=0, tiled=True
    )
    sin_part1 = scatter(shared_in_parts(d_sin1))[0]
    sout_part1 = scatter(d_sout1.astype(brain))
    sin_part0 = scatter(shared_in_parts(d_sin0))[0]
    sout_part0 = scatter(d_sout0.astype(brain))
    out_proj_grad = scatter(d_w_out.astype(brain))

    conv_grads = jnp.concatenate([d_taps, d_bias[None]], axis=0)
    conv_all = jnp.concatenate(
        [
            lax.dynamic_update_slice_in_dim(
                jnp.zeros((KW + 1, DI), single), conv_grads[:, :INNER], team * INNER, 1
            ),
            conv_grads[:, INNER:],
        ],
        axis=1,
    )
    conv_all = conv_all.reshape(5, 8, 16, 26).transpose(2, 1, 0, 3).reshape(16, 8, 130)
    head_all = lax.dynamic_update_slice_in_dim(
        jnp.zeros((3, H), single), jnp.stack([d_step, d_decay, d_skip]), team * HEADS_HERE, 1
    )
    head_all = jnp.broadcast_to(head_all.reshape(1, 1, 3 * H), (16, 8, 3 * H))
    gain_all = lax.dynamic_update_slice_in_dim(
        jnp.zeros((16, 8, 24), single), d_norm_gain.reshape(16, 1, 24), team, 1
    )
    d_gains = jnp.stack([jnp.stack([d_gain00, d_gain01]), jnp.stack([d_gain10, d_gain11])])
    d_gains = d_gains.reshape(2, 2, 4, 16, 24).transpose(3, 0, 2, 1, 4).reshape(16, 8, 48)
    d_router = jnp.stack([d_router0, d_router1]).reshape(2, 4, 16, 24 * EXPERTS)
    d_router = d_router.transpose(2, 0, 1, 3).reshape(16, 8, 24 * EXPERTS)
    small_grads = jnp.concatenate([d_router, conv_all, gain_all, d_gains, head_all], axis=2)
    small_grads = jnp.pad(small_grads, ((0, 0), (0, 0), (0, 2 * IN_COLS - small_grads.shape[2])))
    small_grads = small_grads.astype(brain).reshape(16, 8, 2, IN_COLS)
    d_main = jnp.concatenate(
        [d_w_in.astype(brain).reshape(16, 8, 12, IN_COLS), small_grads], axis=2
    )
    main_part = scatter(d_main)[0]

    main_end, qkv_end, sin_end, sout_end = exchange(
        [
            (pad_rows(main_part, 16), "swap"),
            (pad_rows(qkv_part, 16), "swap"),
            (pad_rows(jnp.concatenate([sin_part0, sin_part1], axis=0), 32), "swap"),
            (pad_rows(jnp.stack([sout_part0, sout_part1]), 16), "pair"),
        ],
        TEAM,
        15,
        "team_end",
    )
    main_end = main_end.astype(single)
    rows_end = main_end[:, :12]

    def side_by_side(value):
        return value.transpose(1, 0, 2).reshape(value.shape[1], -1)

    in_proj_grad = jnp.concatenate(
        [
            side_by_side(rows_end[:, :, :INNER]),
            side_by_side(rows_end[:, :, INNER : 2 * INNER]),
            jnp.sum(rows_end[:, :, 2 * INNER : 2 * INNER + 2 * N], axis=0),
            side_by_side(
                rows_end[:, :, 2 * INNER + 2 * N : 2 * INNER + 2 * N + HEADS_HERE]
            ),
        ],
        axis=1,
    )
    small_end = jnp.sum(main_end[:, 12:14], axis=0).reshape(2 * IN_COLS)
    router_grad = small_end[: 24 * EXPERTS].reshape(1, 24, EXPERTS)
    at = 24 * EXPERTS
    conv_end = small_end[at : at + 130].reshape(5, 26)
    at += 130
    norm_gain_grad = small_end[at : at + 24]
    at += 24
    norm_gains_grad = small_end[at : at + 48].reshape(1, 2, 24)
    at += 48
    heads_end = small_end[at : at + 3 * H].reshape(3, H)
    qkv_end = qkv_end[:, :12].astype(single).reshape(4, 2, 12, QKV_COLS)
    qkv_end = jnp.sum(qkv_end, axis=1)
    query_grad = side_by_side(qkv_end[:, :, :384])
    kv_grad = qkv_end[:, :, 384:].reshape(4, 12, 2, 128).transpose(1, 2, 0, 3).reshape(12, 1024)
    sin_end = sin_end[:, :24].astype(single).reshape(2, 4, 24, 2, 16, 8)
    shared_in_grad = sin_end.transpose(2, 3, 1, 4, 0, 5).reshape(1, 24, 2048)
    shared_out_grad = sout_end[:, :8].astype(single).reshape(1, 16, WIDTH)

    return (
        phase_outputs,
        input_grads,
        in_proj_grad,
        conv_end[:KW],
        conv_end[KW],
        heads_end[0],
        heads_end[1],
        heads_end[2],
        norm_gain_grad,
        out_proj_grad.astype(single),
        query_grad,
        kv_grad,
        attn_out_grad.astype(single),
        norm_gains_grad,
        router_grad,
        shared_in_grad,
        shared_out_grad,
        experts_in_grad[None, None],
        experts_out_grad[None, None],
    )


def solution(mesh):
    fine = Mesh(mesh.devices.reshape(2, 2, 2, 16), ALL)
    in_specs = (
        P(None, DP, None),
        P(None, DP, None),
        P(None, DP, None),
        P(None, DP, None),
        P(ALL, None),
        P(None, ALL),
        P(ALL),
        P(),
        P(),
        P(),
        P(ALL),
        P(ALL, None),
        P(ALL, None),
        P(ALL, None),
        P(ALL, None),
        P("phase", None, DP),
        P("phase", DP, None),
        P("phase", DP, None),
        P("phase", DP, None),
        P("phase", DP, None, None),
        P("phase", DP, None, None),
    )
    out_specs = (
        P("phase", None, DP, None),
        P("phase", None, DP, None),
        P(ALL, None),
        P(None, ALL),
        P(ALL),
        P(),
        P(),
        P(),
        P(ALL),
        P(ALL, None),
        P(ALL, None),
        P(ALL, None),
        P(ALL, None),
        P("phase", None, DP),
        P("phase", DP, None),
        P("phase", DP, None),
        P("phase", DP, None),
        P("phase", DP, None, None),
        P("phase", DP, None, None),
    )
    return jax.shard_map(
        per_device, mesh=fine, in_specs=in_specs, out_specs=out_specs, check_vma=False
    )
```

```python
import functools

import jax
import jax.numpy as jnp
from jax import lax
from jax.experimental import pallas as pl
from jax.experimental.pallas import tpu as pltpu
from jax.sharding import Mesh
from jax.sharding import PartitionSpec as P

H = 48
P_SIZE = 64
N = 128
KW = 4
QUERY_HEADS = 12
KEY_VALUE_HEADS = 4
HEAD_SIZE = 128
DI = 3072
CONVW = 3328
WIDTH = 1536
SEQ = 64
EXPERTS = 64
SLOTS = 8
PARTS = 8
HEADS_HERE = H // PARTS
INNER = DI // PARTS
IN_COLS = 1152
QKV_COLS = 640

SIZES = {"phase": 2, "zh": 2, "zl": 2, "yh": 2, "x": 4, "core": 2}
TEAM = ("phase", "zh", "zl")
HALF = ("phase", "zh")
RANK = ("yh", "x", "core")
DP = ("zh", "zl", "yh", "x", "core")
ALL = ("phase", "zh", "zl", "yh", "x", "core")
MESH_ID = pl.DeviceIdType.MESH

eps = 1e-05
single = jnp.float32
brain = jnp.bfloat16


def place_of(axes, index):
    out = {}
    for name in reversed(axes):
        out[name] = lax.rem(index, SIZES[name])
        index = lax.div(index, SIZES[name])
    return out


def size_of(axes):
    total = 1
    for name in axes:
        total *= SIZES[name]
    return total


def my_place(axes):
    me = jnp.int32(0)
    for name in axes:
        me = me * SIZES[name] + lax.axis_index(name)
    return me


def greet(barrier, device):
    pl.semaphore_signal(barrier, inc=1, device_id=device, device_id_type=MESH_ID)


def send(source, target, send_sem, recv_sem, device):
    copy = pltpu.make_async_remote_copy(
        src_ref=source,
        dst_ref=target,
        send_sem=send_sem,
        recv_sem=recv_sem,
        device_id=device,
        device_id_type=MESH_ID,
    )
    copy.start()
    return copy


def team_copies(axes, modes, sources, targets, send_sem, recv_sem, own_sem):
    n = size_of(axes)
    me = my_place(axes)
    copies = []
    for k in range(1, n):
        peer = lax.rem(me + k, n)
        device = place_of(axes, peer)
        for item, mode in enumerate(modes):
            if mode in SIZES:
                continue
            source = sources[item].at[peer] if mode == "swap" else sources[item]
            copies.append(
                send(
                    source,
                    targets[item].at[me],
                    send_sem.at[item, k],
                    recv_sem.at[item, k],
                    device,
                )
            )
    for item, mode in enumerate(modes):
        slot = me
        source = sources[item] if mode == "gather" else sources[item].at[me]
        if mode in SIZES:
            slot = lax.axis_index(mode)
            source = sources[item].at[slot]
            copies.append(
                send(
                    sources[item].at[1 - slot],
                    targets[item].at[slot],
                    send_sem.at[item, 0],
                    recv_sem.at[item, 0],
                    {mode: 1 - slot},
                )
            )
        copy = pltpu.make_async_copy(source, targets[item].at[slot], own_sem.at[item])
        copy.start()
        copies.append(copy)
    return copies


def greet_team(barrier, axes):
    n = size_of(axes)
    me = my_place(axes)
    for k in range(1, n):
        greet(barrier, place_of(axes, lax.rem(me + k, n)))
    return n - 1


def exchange_kernel(axes, modes, *refs):
    count = len(modes)
    barrier = pltpu.get_barrier_semaphore()
    pl.semaphore_wait(barrier, greet_team(barrier, axes))
    copies = team_copies(axes, modes, refs[:count], refs[count : 2 * count], *refs[2 * count :])
    for copy in copies:
        copy.wait()


def received(axes, items):
    n = size_of(axes)
    return [
        jax.ShapeDtypeStruct(((n,) if mode == "gather" else ()) + array.shape, array.dtype)
        for array, mode in items
    ]


def call(kernel, arrays, shapes, scratch, number, name):
    moved = sum(s.size * s.dtype.itemsize for s in shapes)
    return pl.pallas_call(
        kernel,
        out_shape=shapes,
        in_specs=[pl.BlockSpec(memory_space=pltpu.VMEM)] * len(arrays),
        out_specs=[pl.BlockSpec(memory_space=pltpu.VMEM)] * len(shapes),
        scratch_shapes=scratch,
        compiler_params=pltpu.CompilerParams(
            collective_id=number, has_side_effects=True, vmem_limit_bytes=48 << 20
        ),
        cost_estimate=pl.CostEstimate(flops=0, bytes_accessed=2 * moved, transcendentals=0),
        name=name,
    )(*arrays)


def team_semaphores(axes, items):
    return [
        pltpu.SemaphoreType.DMA((len(items), size_of(axes))),
        pltpu.SemaphoreType.DMA((len(items), size_of(axes))),
        pltpu.SemaphoreType.DMA((len(items),)),
    ]


def exchange(items, axes, number, name):
    return call(
        functools.partial(exchange_kernel, axes, tuple(mode for _, mode in items)),
        [array for array, _ in items],
        received(axes, items),
        team_semaphores(axes, items),
        number,
        name,
    )


def rank_devices():
    yh, x, core = lax.axis_index("yh"), lax.axis_index("x"), lax.axis_index("core")
    across = [lax.rem(x + k, 4) for k in range(4)]
    out = []
    for dy in range(2):
        for dx in range(4):
            for dc in range(2):
                y_at = 1 - yh if dy else yh
                c_at = 1 - core if dc else core
                device = {"yh": y_at, "x": across[dx], "core": c_at}
                out.append((device, y_at * 8 + across[dx] * 2 + c_at))
    return out


def for_each_expert_place(action):
    z = lax.axis_index("zh") * 2 + lax.axis_index("zl")
    rank = rank_devices()

    def of_layer(layer, own):
        high, low = lax.div(layer, 2), lax.rem(layer, 2)
        for k, (device, at) in enumerate(rank):
            action(dict(device, zh=high, zl=low), layer * 16 + at, own and k == 0)

    of_layer(z, True)

    def step(k, carry):
        of_layer(lax.rem(z + k, 4), False)
        return carry

    lax.fori_loop(1, 4, step, 0)


def expert_exchange_kernel(count, modes, *refs):
    every = count + len(modes)
    sources, targets = refs[:every], refs[every : 2 * every]
    send_sem, recv_sem, own_sem, rows_sent, rows_got = refs[2 * every :]
    mine = my_place(DP)
    barrier = pltpu.get_barrier_semaphore()

    def welcome(device, at, own):
        if not own:
            greet(barrier, device)

    for_each_expert_place(welcome)
    pl.semaphore_wait(barrier, 63 + greet_team(barrier, TEAM))
    team = team_copies(
        TEAM, modes, sources[count:], targets[count:], send_sem, recv_sem, own_sem
    )

    def give(device, at, own):
        for item in range(count):
            source, target = sources[item].at[at], targets[item].at[mine]
            if own:
                pltpu.make_async_copy(source, target, rows_got.at[item]).start()
            else:
                send(source, target, rows_sent.at[item], rows_got.at[item], device)

    for_each_expert_place(give)
    for item in range(count):
        sent = sources[item].at[pl.ds(0, 63)]
        pltpu.make_async_copy(sent, sent, rows_sent.at[item]).wait()
        pltpu.make_async_copy(targets[item], targets[item], rows_got.at[item]).wait()
    for copy in team:
        copy.wait()


def expert_exchange(rows, items, number, name):
    rows = [value.reshape(EXPERTS, SLOTS, WIDTH) for value in rows]
    count = len(rows)
    out = call(
        functools.partial(expert_exchange_kernel, count, tuple(mode for _, mode in items)),
        rows + [array for array, _ in items],
        [jax.ShapeDtypeStruct(value.shape, brain) for value in rows] + received(TEAM, items),
        team_semaphores(TEAM, items)
        + [pltpu.SemaphoreType.DMA((count,)), pltpu.SemaphoreType.DMA((count,))],
        number,
        name,
    )
    rows_got = [value.reshape(EXPERTS * SLOTS, WIDTH) for value in out[:count]]
    return rows_got + list(out[count:])


def rank_gather_kernel(count, *refs):
    sources, targets = refs[:count], refs[count : 2 * count]
    send_sem, recv_sem, own_sem = refs[2 * count :]
    yh, x, core = lax.axis_index("yh"), lax.axis_index("x"), lax.axis_index("core")
    right, left, far = lax.rem(x + 1, 4), lax.rem(x + 3, 4), lax.rem(x + 2, 4)
    other = 1 - yh
    to_y, to_right, to_left, to_core = {"yh": other}, {"x": right}, {"x": left}, {"core": 1 - core}
    barrier = pltpu.get_barrier_semaphore()
    for device in (to_y, to_right, to_left, to_core):
        greet(barrier, device)
    pl.semaphore_wait(barrier, 4)

    def slot(y_at, x_at):
        return y_at * 8 + x_at * 2 + core

    sent = []

    def pass_on(item, at, kind, device, source=None):
        target = targets[item].at[at]
        copy = send(
            target if source is None else source,
            target,
            send_sem.at[item, kind],
            recv_sem.at[item, kind],
            device,
        )
        sent.append(copy)
        return copy

    def arrived(item, kind):
        pltpu.make_async_copy(sources[item], sources[item], recv_sem.at[item, kind]).wait()

    items = range(count)
    me = slot(yh, x)
    own = []
    for item in items:
        pass_on(item, me, 0, to_y, sources[item])
        pass_on(item, me, 1, to_right, sources[item])
        pass_on(item, me, 2, to_left, sources[item])
        pass_on(item, me, 7, to_core, sources[item])
        copy = pltpu.make_async_copy(sources[item], targets[item].at[me], own_sem.at[item])
        copy.start()
        own.append(copy)
    steps = (
        (1, slot(yh, left), ((5, to_right), (8, to_core))),
        (0, slot(other, x), ((3, to_right), (4, to_left), (9, to_core))),
        (2, slot(yh, right), ((10, to_core),)),
        (4, slot(other, right), ((6, to_left), (11, to_core))),
        (3, slot(other, left), ((12, to_core),)),
        (5, slot(yh, far), ((13, to_core),)),
        (6, slot(other, far), ((14, to_core),)),
    )
    for kind, at, onward in steps:
        for item in items:
            arrived(item, kind)
            for next_kind, device in onward:
                pass_on(item, at, next_kind, device)
    for item in items:
        for kind in range(7, 15):
            arrived(item, kind)
    for copy in own:
        copy.wait()
    for copy in sent:
        copy.wait_send()


def rank_gather(arrays, number, name):
    count = len(arrays)
    return call(
        functools.partial(rank_gather_kernel, count),
        arrays,
        [jax.ShapeDtypeStruct((16,) + array.shape, array.dtype) for array in arrays],
        [
            pltpu.SemaphoreType.DMA((count, 15)),
            pltpu.SemaphoreType.DMA((count, 15)),
            pltpu.SemaphoreType.DMA((count,)),
        ],
        number,
        name,
    )


def rank_sum_kernel(count, *refs):
    sources, targets = refs[:count], refs[count : 2 * count]
    from_core, totals, arrivals = (refs[(2 + k) * count : (3 + k) * count] for k in range(3))
    send_sem, recv_sem = refs[5 * count :]
    yh, x, core = lax.axis_index("yh"), lax.axis_index("x"), lax.axis_index("core")
    right, left, far = lax.rem(x + 1, 4), lax.rem(x + 3, 4), lax.rem(x + 2, 4)
    other = 1 - yh
    to_y, to_right, to_left, to_core = {"yh": other}, {"x": right}, {"x": left}, {"core": 1 - core}
    barrier = pltpu.get_barrier_semaphore()
    for device in (to_y, to_right, to_left, to_core):
        greet(barrier, device)
    pl.semaphore_wait(barrier, 4)
    items = range(count)
    sent = []

    def pass_on(item, at, kind, device):
        copy = send(
            totals[item].at[at],
            arrivals[item].at[kind],
            send_sem.at[item, kind],
            recv_sem.at[item, kind],
            device,
        )
        sent.append(copy)

    def arrived(item, kind):
        landed = arrivals[item].at[kind]
        pltpu.make_async_copy(landed, landed, recv_sem.at[item, kind]).wait()
        return arrivals[item][kind].astype(single)

    def slot(y_at, x_at):
        return y_at * 4 + x_at

    for item in items:
        sent.append(
            send(
                sources[item].at[:, 1 - core],
                from_core[item],
                send_sem.at[item, 7],
                recv_sem.at[item, 7],
                to_core,
            )
        )
    for item in items:
        landed = from_core[item]
        pltpu.make_async_copy(landed, landed, recv_sem.at[item, 7]).wait()

        def add(at):
            value = sources[item][at, core].astype(single) + from_core[item][at].astype(single)
            totals[item][at] = value.astype(brain)

        add(slot(yh, far))
        pass_on(item, slot(yh, far), 0, to_right)
        add(slot(other, far))
        pass_on(item, slot(other, far), 1, to_left)
        add(slot(other, right))
        pass_on(item, slot(other, right), 3, to_right)
        add(slot(yh, left))
        pass_on(item, slot(yh, left), 5, to_left)
        for at in (slot(yh, right), slot(other, left), slot(yh, x), slot(other, x)):
            add(at)
    for item in items:
        at = slot(yh, right)
        totals[item][at] = (totals[item][at].astype(single) + arrived(item, 0)).astype(brain)
        pass_on(item, at, 2, to_right)
        at = slot(other, left)
        totals[item][at] = (totals[item][at].astype(single) + arrived(item, 1)).astype(brain)
        pass_on(item, at, 4, to_left)
    for item in items:
        at = slot(other, x)
        value = totals[item][at].astype(single) + arrived(item, 3)
        totals[item][at] = (value + arrived(item, 4)).astype(brain)
        pass_on(item, at, 6, to_y)
    for item in items:
        value = totals[item][slot(yh, x)].astype(single) + arrived(item, 5)
        value = value + arrived(item, 2)
        targets[item][...] = (value + arrived(item, 6)).astype(targets[item].dtype)
    for copy in sent:
        copy.wait_send()


def rank_sum(arrays, number, name):
    count = len(arrays)
    arrays = [array.reshape((8, 2) + array.shape[1:]) for array in arrays]
    pieces = [array.shape[2:] for array in arrays]
    scratch = [pltpu.VMEM((8,) + piece, brain) for piece in pieces]
    scratch += [pltpu.VMEM((8,) + piece, brain) for piece in pieces]
    scratch += [pltpu.VMEM((7,) + piece, brain) for piece in pieces]
    scratch += [pltpu.SemaphoreType.DMA((count, 8)), pltpu.SemaphoreType.DMA((count, 8))]
    return call(
        functools.partial(rank_sum_kernel, count),
        arrays,
        [jax.ShapeDtypeStruct(piece, brain) for piece in pieces],
        scratch,
        number,
        name,
    )


def dot(left, right):
    return jnp.dot(left, right, preferred_element_type=single)


def dot_t(left, right):
    return lax.dot_general(left, right, (((1,), (1,)), ((), ())), preferred_element_type=single)


def t_dot(left, right):
    return lax.dot_general(left, right, (((0,), (0,)), ((), ())), preferred_element_type=single)


def exact(spec, left, right):
    return jnp.einsum(
        spec, left, right, precision=lax.Precision.HIGHEST, preferred_element_type=single
    )


def rms_scale(value, gain):
    return value * lax.rsqrt(jnp.mean(value * value, axis=-1, keepdims=True) + eps) * gain


def swiglu(value):
    half = value.shape[-1] // 2
    return jax.nn.silu(value[..., :half]) * value[..., half:]


def shuffle_matrix():
    to = jnp.arange(WIDTH, dtype=jnp.int32)
    origin = to // 12 % 8 * 192 + to // 96 * 12 + to % 12
    return (jnp.arange(WIDTH, dtype=jnp.int32)[:, None] == origin[None, :]).astype(brain)


def shuffle(value, matrix):
    return dot(value, matrix).astype(brain)


def unshuffle(value, matrix):
    high = value.astype(brain)
    lower = (value - high.astype(single)).astype(brain)
    both = dot_t(jnp.concatenate([high, lower], axis=0), matrix)
    return both[: value.shape[0]] + both[value.shape[0] :]


def after(values, first):
    return lax.optimization_barrier((values, first))[0]


def pad_rows(value, rows):
    return jnp.pad(value, [(0, 0)] * (value.ndim - 2) + [(0, rows - value.shape[-2]), (0, 0)])


def pad_to(value, rows, columns):
    return jnp.pad(value, ((0, rows - value.shape[0]), (0, columns - value.shape[1])))


def allowed_pairs(seg):
    position = jnp.arange(SEQ, dtype=jnp.int32)
    return (position[:, None] >= position[None, :]) & (seg[..., :, None] == seg[..., None, :])


def mamba_core(zx, seg, taps, bias, step_bias, decay_log, skip):
    rows = zx.shape[0]
    gate_part = zx[..., :INNER]
    conv_in = zx[..., INNER : 2 * INNER + 2 * N]
    step_raw = zx[..., 2 * INNER + 2 * N : 2 * INNER + 2 * N + HEADS_HERE]
    padded = jnp.pad(conv_in, ((0, 0), (KW - 1, 0), (0, 0)))
    seg_pad = jnp.pad(seg, ((0, 0), (KW - 1, 0)), constant_values=-1)
    conv = jnp.zeros_like(conv_in) + bias
    for tap in range(KW):
        same = (seg_pad[:, tap : tap + SEQ] == seg).astype(single)
        conv = conv + taps[tap] * padded[:, tap : tap + SEQ] * same[:, :, None]
    active = jax.nn.silu(conv)
    values = active[..., :INNER].reshape(rows, SEQ, HEADS_HERE, P_SIZE)
    in_state = active[..., INNER : INNER + N]
    out_state = active[..., INNER + N :]
    step = jax.nn.softplus(step_raw + step_bias)
    total = jnp.cumsum(step * (-jnp.exp(decay_log)), axis=1)
    allowed = allowed_pairs(seg)
    step_t = step.transpose(0, 2, 1)
    total_t = total.transpose(0, 2, 1)
    spread = total_t[..., :, None] - total_t[..., None, :]
    decay = jnp.where(allowed[:, None], jnp.exp(jnp.minimum(spread, 0.0)), 0.0)
    meeting = exact("nis,njs->nij", out_state, in_state)
    mixing = decay * meeting[:, None] * step_t[:, :, None, :]
    result = exact("nhij,njhp->nihp", mixing, values)
    result = result + skip[:, None] * values
    return result.reshape(rows, SEQ, INNER) * jax.nn.silu(gate_part)


def attend_scores(queries, keys, seg):
    scores = exact("nird,njd->nrij", queries, keys) * HEAD_SIZE ** (-0.5)
    scores = jnp.where(allowed_pairs(seg)[:, None], scores, -1e30)
    return jax.nn.softmax(scores, axis=-1)


def attend_mix(probs, values):
    return exact("nrij,njd->nird", probs, values)


def per_device(
    block_input,
    cotangent,
    segments,
    routes,
    in_proj,
    conv_taps,
    conv_bias,
    step_bias,
    decay_log,
    skip_weight,
    norm_gain,
    out_proj,
    query_proj,
    key_value_projection,
    attn_out_proj,
    norm_gains,
    router,
    shared_in,
    shared_out,
    experts_in,
    experts_out,
):
    phase = lax.axis_index("phase")
    first_phase = phase == 0
    zl = lax.axis_index("zl")
    team = phase * 4 + lax.axis_index("zh") * 2 + zl

    def mine(value):
        return lax.dynamic_index_in_dim(value, phase, 0, keepdims=False)

    start = mine(block_input)
    cot = mine(cotangent)
    seg = mine(segments)
    route_rows = mine(routes)

    both_ways = [(0, 1), (1, 0)]
    w_first, w_second = experts_in[0, 0], experts_out[0, 0]

    z_piece = in_proj[:, :DI].reshape(12, PARTS, INNER).transpose(1, 0, 2)
    x_piece = in_proj[:, DI : 2 * DI].reshape(12, PARTS, INNER).transpose(1, 0, 2)
    state_piece = jnp.broadcast_to(in_proj[None, :, 2 * DI : 2 * DI + 2 * N], (PARTS, 12, 2 * N))
    step_piece = in_proj[:, 2 * DI + 2 * N :].reshape(12, PARTS, HEADS_HERE).transpose(1, 0, 2)
    step_piece = jnp.pad(step_piece, ((0, 0), (0, 0), (0, 128 - HEADS_HERE)))
    q_piece = query_proj.reshape(12, 4, 384).transpose(1, 0, 2)
    kv_piece = key_value_projection.reshape(12, 2, 4, 128).transpose(2, 0, 1, 3).reshape(4, 12, 256)
    qkv_piece = jnp.repeat(jnp.concatenate([q_piece, kv_piece], axis=2), 2, axis=0)
    main_piece = pad_rows(
        jnp.concatenate([z_piece, x_piece, state_piece, step_piece, qkv_piece], axis=2), 16
    )
    sin_piece = shared_in[0].reshape(24, 2, 4, 16, 2, 8).transpose(4, 2, 0, 1, 3, 5)
    sin_piece = pad_rows(sin_piece.reshape(PARTS, 24, 256), 32)
    sout_piece = pad_rows(shared_out[0].reshape(2, 8, WIDTH), 16)
    attn_piece = jnp.broadcast_to(pad_rows(attn_out_proj, 16)[None], (2, 16, WIDTH))
    mixing = shuffle_matrix()
    rest = jnp.concatenate(
        [conv_taps.reshape(-1), conv_bias, norm_gain, norm_gains[0].reshape(-1)]
    )
    rest = jnp.pad(rest, (0, 512 - rest.shape[0])).reshape(4, 128)
    small = jnp.concatenate([router[0].reshape(12, 128), rest], axis=0)
    seg_piece = pad_to(seg, 8, 128)
    main_got, sin_got, sout_got, small_got, seg_got, start_all, attn_got = exchange(
        [
            (main_piece, "swap"),
            (sin_piece, "swap"),
            (sout_piece, "phase"),
            (small, "gather"),
            (seg_piece, "gather"),
            (shuffle(start, mixing), "gather"),
            (attn_piece, "zl"),
        ],
        TEAM,
        0,
        "team_start",
    )
    seg_all = seg_got[:, 0, :SEQ]
    main_got = main_got[:, :12].reshape(96, IN_COLS + QKV_COLS)
    sin_got = sin_got[:, :24].reshape(192, 256)
    w_in, small_all, w_out, sin_all, sout_all = rank_gather(
        [
            main_got[:, :IN_COLS],
            small_got.reshape(128, 128),
            pad_rows(out_proj, 32),
            sin_got[:96],
            pad_rows(sout_got[0, :8], 16),
        ],
        1,
        "rank_weights",
    )
    w_in = w_in.reshape(WIDTH, IN_COLS)
    w_out = w_out[:, :24].reshape(INNER, WIDTH)
    later_wide = jnp.concatenate([main_got[:, IN_COLS:], sin_got[96:]], axis=1)
    later_tall = jnp.concatenate([attn_got[:, :12].reshape(24, WIDTH), sout_got[1, :8]], axis=0)
    later_wide, later_tall, w_first, w_second = after(
        (later_wide, later_tall, w_first, w_second), w_in
    )
    w_first_far = lax.ppermute(w_first, "phase", both_ways)
    w_second_far = lax.ppermute(w_second, "phase", both_ways)
    later_wide = lax.all_gather(later_wide, RANK, axis=0)
    later_tall = lax.all_gather(later_tall, RANK, axis=0)
    w_qkv = later_wide[:, :, :QKV_COLS].reshape(WIDTH, QKV_COLS)
    w_attn = later_tall[:, :24].reshape(16, 2, 12, WIDTH).transpose(1, 0, 2, 3)
    w_attn = w_attn.reshape(384, WIDTH)

    def hidden_in(value):
        return value.reshape(16, 4, 24, 256).transpose(1, 0, 2, 3).reshape(WIDTH, 256)

    sin_full = (hidden_in(sin_all), hidden_in(later_wide[:, :, QKV_COLS:]))
    sout_full = (sout_all[:, :8].reshape(128, WIDTH), later_tall[:, 24:].reshape(128, WIDTH))
    small_all = small_all.reshape(16, 2, 4, 16, 128)
    router_full = small_all[:, :, :, :12].reshape(16, 2, 4, 24, EXPERTS).transpose(1, 2, 0, 3, 4)
    router_full = router_full.reshape(2, WIDTH, EXPERTS)
    rest_all = small_all[:, :, :, 12:].reshape(16, 2, 4, 512)
    conv_full = rest_all[..., :130].reshape(16, 2, 4, 5, 26).transpose(3, 1, 2, 0, 4)
    conv_full = conv_full.reshape(5, CONVW).astype(single)
    gain_here = rest_all[..., 130:154].reshape(16, 8, 24)
    gain_here = lax.dynamic_index_in_dim(gain_here, team, 1, keepdims=False)
    gain_here = gain_here.reshape(INNER).astype(single)
    gains = rest_all[..., 154:202].reshape(16, 2, 4, 2, 24).transpose(1, 3, 2, 0, 4)
    gains = gains.reshape(2, 2, WIDTH).astype(single)
    conv_here = jnp.concatenate(
        [lax.dynamic_slice_in_dim(conv_full[:, :DI], team * INNER, INNER, 1), conv_full[:, DI:]],
        axis=1,
    )
    taps_here, bias_here = conv_here[:KW], conv_here[KW]

    def heads_of(value):
        return lax.dynamic_slice_in_dim(value, team * HEADS_HERE, HEADS_HERE, 0)

    step_here, decay_here, skip_here = (
        heads_of(step_bias),
        heads_of(decay_log),
        heads_of(skip_weight),
    )

    expert_ids = jnp.arange(EXPERTS, dtype=jnp.int32)
    named = jnp.any(route_rows[:, :, None] == expert_ids, axis=1)
    position = jnp.arange(SEQ, dtype=jnp.int32)
    earlier = (position[:, None] > position[None, :]).astype(brain)
    slot = dot(earlier, named.astype(brain))
    slot = jnp.where(named, slot, -1.0).astype(brain)
    cell = jnp.arange(EXPERTS * SLOTS, dtype=jnp.int32)
    spread = (cell[None, :] // SLOTS == expert_ids[:, None]).astype(brain)
    taken = dot(slot, spread) == (cell % SLOTS).astype(single)
    taken_b = taken.astype(brain)

    def of_block(s):
        own = phase == s
        return (
            jnp.where(own, w_first, w_first_far),
            jnp.where(own, w_second, w_second_far),
        )

    def moe_open(s, hidden):
        normed = rms_scale(hidden, gains[s, 1]).astype(brain)
        logits = dot(normed, router_full[s])
        top = jnp.max(jnp.where(named, logits, -jnp.inf), axis=1, keepdims=True)
        weight = jnp.where(named, jnp.exp(logits - top), 0.0)
        gates = weight / jnp.sum(weight, axis=1, keepdims=True)
        gates_wide = jnp.where(taken, exact("ie,ec->ic", gates, spread.astype(single)), 0.0)
        return normed, gates, gates_wide, t_dot(taken_b, normed).astype(brain)

    def moe_experts(weights, rows_in):
        both = dot(rows_in, weights[0])
        hid = swiglu(both).astype(brain)
        return both, hid, dot(hid, weights[1]).astype(brain)

    def moe_shared(s, normed_all):
        both = dot(normed_all, sin_full[s])
        hid = swiglu(both).astype(brain)
        part = dot(hid, sout_full[s]).astype(brain)
        return both, hid, part.reshape(PARTS, SEQ, WIDTH)

    def moe_join(hidden, gates_wide, back, shared_got):
        high = gates_wide.astype(brain)
        lower = (gates_wide - high.astype(single)).astype(brain)
        moe = dot(high, back) + dot(lower, back)
        return (hidden + moe + jnp.sum(shared_got.astype(single), axis=0)).astype(brain)

    def back_open(d_out, gates_wide):
        gate_cell = jnp.sum(gates_wide, axis=0)
        return (t_dot(taken_b, d_out) * gate_cell[:, None]).astype(brain)

    def back_experts(weights, d_answer, both):
        d_hid = dot_t(d_answer, weights[1])
        d_both = jax.vjp(swiglu, both)[1](d_hid)[0].astype(brain)
        return d_both, dot_t(d_both, weights[0]).astype(brain)

    def back_shared(s, d_out_all, normed_all, both, hid):
        d_hid = dot_t(d_out_all, sout_full[s])
        d_sout = t_dot(hid, d_out_all)
        d_both = jax.vjp(swiglu, both)[1](d_hid)[0].astype(brain)
        d_sin = t_dot(normed_all, d_both)
        d_part = dot_t(d_both, sin_full[s]).astype(brain).reshape(PARTS, SEQ, WIDTH)
        return d_sin, d_sout, d_part

    def back_join(s, d_out, hidden, normed, gates, back, returned, d_shared_got):
        d_cells = jnp.where(taken, dot_t(d_out, back), 0.0)
        d_gates = exact("ic,ec->ie", d_cells, spread.astype(single))
        d_logits = gates * (d_gates - jnp.sum(gates * d_gates, axis=1, keepdims=True))
        d_normed = exact("ie,we->iw", d_logits, router_full[s].astype(single))
        d_router = exact("iw,ie->we", normed.astype(single), d_logits)
        d_normed = d_normed + dot(taken_b, returned) + jnp.sum(d_shared_got.astype(single), axis=0)
        d_hidden, d_gain = jax.vjp(rms_scale, hidden, gains[s, 1])[1](d_normed)
        return d_hidden + d_out.astype(single), d_gain, d_router

    def shared_in_parts(value):
        return value.astype(brain).reshape(4, 16, 24, 256).transpose(1, 0, 2, 3).reshape(16, 96, 256)

    u0 = start.astype(single)
    shuffled_gain = shuffle(gains[0, 0][None].astype(brain), mixing)[0].astype(single)
    n1_all = rms_scale(start_all.astype(single), shuffled_gain).astype(brain)
    n1_all = n1_all.reshape(PARTS * SEQ, WIDTH)
    zx = dot(n1_all, w_in).reshape(PARTS, SEQ, IN_COLS)

    def core(zx, taps, bias, step_bias, decay_log, skip):
        return mamba_core(zx, seg_all, taps, bias, step_bias, decay_log, skip)

    core_args = (zx, taps_here, bias_here, step_here, decay_here, skip_here)
    gated, core_pull = jax.vjp(core, *core_args)
    squares = jnp.sum(gated * gated, axis=-1)
    part = dot((gated * gain_here).astype(brain).reshape(PARTS * SEQ, INNER), w_out)
    part = part.astype(brain).reshape(PARTS, SEQ, WIDTH)
    squares = jnp.pad(squares[:, None], ((0, 0), (0, 7), (0, 128 - SEQ)))
    part_got, squares_got = exchange([(part, "swap"), (squares, "swap")], TEAM, 2, "team_mixed_0")
    mean_square = jnp.sum(squares_got[:, 0, :SEQ], axis=0) / DI
    inverse = lax.rsqrt(mean_square + eps)
    mixed0 = jnp.sum(part_got.astype(single), axis=0) * inverse[:, None]
    hidden0 = u0 + mixed0
    normed0, gates0, gates_wide0, rows_out0 = moe_open(0, hidden0)
    rows_in0, normed_all0 = expert_exchange([rows_out0], [(normed0, "gather")], 3, "spread_0")
    normed_all0 = normed_all0.reshape(PARTS * SEQ, WIDTH)
    weights0 = of_block(0)
    sboth0, shid0, shared_part0 = moe_shared(0, normed_all0)
    both0, hid0, answer0 = moe_experts(weights0, rows_in0)
    back0, shared_got0 = expert_exchange([answer0], [(shared_part0, "swap")], 4, "collect_0")
    out0 = moe_join(hidden0, gates_wide0, back0, shared_got0)

    u1 = out0.astype(single)
    n1 = rms_scale(u1, gains[1, 0]).astype(brain)
    (n1_half,) = exchange([(shuffle(n1, mixing), "gather")], HALF, 5, "half_n1")
    n1_half = n1_half.reshape(4 * SEQ, WIDTH)
    seg_half = lax.dynamic_index_in_dim(seg_all.reshape(4, 2, SEQ), zl, 1, keepdims=False)
    qkv = dot(n1_half, w_qkv).astype(brain).astype(single).reshape(4, SEQ, QKV_COLS)
    queries = qkv[..., :384].reshape(4, SEQ, 3, HEAD_SIZE)
    keys, values = qkv[..., 384:512], qkv[..., 512:]
    probs, score_pull = jax.vjp(lambda q, k: attend_scores(q, k, seg_half), queries, keys)
    heads, mix_pull = jax.vjp(attend_mix, probs.astype(brain).astype(single), values)
    heads = heads.astype(brain).reshape(4 * SEQ, 384)
    part1 = dot(heads, w_attn).astype(brain).reshape(4, SEQ, WIDTH)
    (part1_got,) = exchange([(part1, "swap")], HALF, 6, "half_mixed")
    mixed1 = jnp.sum(part1_got.astype(single), axis=0)
    hidden1 = u1 + mixed1

    normed1, gates1, gates_wide1, rows_out1 = moe_open(1, hidden1)
    rows_in1, d_answer1, normed_all1, cot_all = expert_exchange(
        [rows_out1, back_open(cot, gates_wide1)],
        [(normed1, "gather"), (cot, "gather")],
        7,
        "spread_1",
    )
    normed_all1 = normed_all1.reshape(PARTS * SEQ, WIDTH)
    cot_all = cot_all.reshape(PARTS * SEQ, WIDTH)
    weights1 = of_block(1)
    sboth1, shid1, shared_part1 = moe_shared(1, normed_all1)
    d_sin1, d_sout1, d_shared1 = back_shared(1, cot_all, normed_all1, sboth1, shid1)
    both1, hid1, answer1 = moe_experts(weights1, rows_in1)
    d_both1, d_rows1 = back_experts(weights1, d_answer1, both1)
    back1, returned1, shared_got1, d_shared_got1 = expert_exchange(
        [answer1, d_rows1], [(shared_part1, "swap"), (d_shared1, "swap")], 8, "collect_1"
    )
    out1 = moe_join(hidden1, gates_wide1, back1, shared_got1)

    d_hid1, d_gain11, d_router1 = back_join(
        1, cot, hidden1, normed1, gates1, back1, returned1, d_shared_got1
    )
    (d_mixed1,) = exchange([(d_hid1.astype(brain), "gather")], HALF, 11, "half_dmixed")
    d_mixed1 = d_mixed1.reshape(4 * SEQ, WIDTH)
    d_heads = dot_t(d_mixed1, w_attn).reshape(4, SEQ, 3, HEAD_SIZE)
    d_attn = t_dot(heads, d_mixed1)
    d_probs, d_values = mix_pull(d_heads)
    d_queries, d_keys = score_pull(d_probs)
    d_qkv = jnp.concatenate([d_queries.reshape(4, SEQ, 384), d_keys, d_values], axis=2)
    d_qkv = d_qkv.astype(brain).reshape(4 * SEQ, QKV_COLS)
    d_w_qkv = t_dot(n1_half, d_qkv)
    d_n1_part = dot_t(d_qkv, w_qkv).astype(brain).reshape(4, SEQ, WIDTH)
    grads_wide = jnp.concatenate(
        [d_w_qkv.astype(brain).reshape(16, 96, QKV_COLS), shared_in_parts(d_sin1)], axis=2
    )
    attn_part = d_attn.astype(brain).reshape(2, 16, 12, WIDTH).transpose(1, 0, 2, 3)
    grads_tall = jnp.concatenate(
        [attn_part.reshape(16, 24, WIDTH), d_sout1.astype(brain).reshape(16, 8, WIDTH)], axis=1
    )
    d_n1_part, grads_wide, grads_tall = lax.optimization_barrier(
        (d_n1_part, grads_wide, grads_tall)
    )
    grads_wide = lax.psum_scatter(grads_wide, RANK, scatter_dimension=0, tiled=True)[0]
    grads_tall = lax.psum_scatter(grads_tall, RANK, scatter_dimension=0, tiled=True)[0]
    (d_n1_got,) = exchange([(d_n1_part, "swap")], HALF, 12, "half_dn1")
    d_n1 = unshuffle(jnp.sum(d_n1_got.astype(single), axis=0), mixing)
    d_u1, d_gain10 = jax.vjp(rms_scale, u1, gains[1, 0])[1](d_n1)
    d_u1 = (d_u1 + d_hid1).astype(brain)

    d_answer0, d_out0_all = expert_exchange(
        [back_open(d_u1, gates_wide0)], [(d_u1, "gather")], 13, "spread_back_0"
    )
    d_out0_all = d_out0_all.reshape(PARTS * SEQ, WIDTH)
    d_sin0, d_sout0, d_shared0 = back_shared(0, d_out0_all, normed_all0, sboth0, shid0)
    d_both0, d_rows0 = back_experts(weights0, d_answer0, both0)
    expert0 = (rows_in0, d_both0, hid0, d_answer0)
    expert1 = (rows_in1, d_both1, hid1, d_answer1)
    give_rows, give_both, give_hid, give_answer = (
        jnp.where(first_phase, b, a) for a, b in zip(expert0, expert1)
    )
    give_first = t_dot(give_rows, give_both).astype(brain)
    give_second = t_dot(give_hid, give_answer).astype(brain)
    d_rows0, give_first, give_second = lax.optimization_barrier((d_rows0, give_first, give_second))
    far_first = lax.ppermute(give_first, "phase", both_ways)
    far_second = lax.ppermute(give_second, "phase", both_ways)
    returned0, d_shared_got0 = expert_exchange(
        [d_rows0], [(d_shared0, "swap")], 14, "collect_back_0"
    )
    d_hid0, d_gain01, d_router0 = back_join(
        0, d_u1, hidden0, normed0, gates0, back0, returned0, d_shared_got0
    )
    d_mixed0 = d_hid0.astype(brain)
    along = jnp.sum(d_mixed0.astype(single) * mixed0, axis=1)
    scalars = jnp.stack([inverse, inverse * inverse * along / DI])
    d_mixed0, scalars_all = exchange(
        [(d_mixed0, "gather"), (pad_to(scalars, 8, 128), "gather")], TEAM, 15, "team_dmixed"
    )
    d_mixed0 = d_mixed0.reshape(PARTS * SEQ, WIDTH)
    inverse_all = scalars_all[:, 0, :SEQ, None]
    along_all = scalars_all[:, 1, :SEQ, None]
    d_yn = dot_t(d_mixed0, w_out).reshape(PARTS, SEQ, INNER)
    unit = gated * inverse_all
    yn = (unit * gain_here).astype(brain).reshape(PARTS * SEQ, INNER)
    d_w_out = t_dot(yn, d_mixed0)
    d_norm_gain = jnp.sum(d_yn * unit, axis=(0, 1))
    d_gated = inverse_all * gain_here * d_yn - gated * along_all
    d_zx, d_taps, d_bias, d_step, d_decay, d_skip = core_pull(d_gated)
    d_zx = d_zx.astype(brain).reshape(PARTS * SEQ, IN_COLS)
    d_w_in = t_dot(n1_all, d_zx)
    d_n1_part0 = dot_t(d_zx, w_in).astype(brain).reshape(PARTS, SEQ, WIDTH)
    d_n1_part0, grads_wide, grads_tall = lax.optimization_barrier(
        (d_n1_part0, grads_wide, grads_tall)
    )
    (d_n1_got0,) = exchange([(d_n1_part0, "swap")], TEAM, 16, "team_dn1")
    d_n1_0 = unshuffle(jnp.sum(d_n1_got0.astype(single), axis=0), mixing)
    d_u0, d_gain00 = jax.vjp(rms_scale, u0, gains[0, 0])[1](d_n1_0)
    d_u0 = d_u0 + d_hid0

    def by_block(block0, block1):
        keep = jnp.where(first_phase, block0, block1)
        give = jnp.where(first_phase, block1, block0)
        got = lax.ppermute(give, "phase", both_ways)
        return jnp.where(first_phase, jnp.stack([keep, got]), jnp.stack([got, keep]))[None]

    phase_outputs = by_block(out0, out1)
    input_grads = by_block(d_u0, d_u1.astype(single))
    rows_kept, d_both_kept, hid_kept, d_answer_kept = (
        jnp.where(first_phase, a, b) for a, b in zip(expert0, expert1)
    )
    experts_in_grad = t_dot(rows_kept, d_both_kept) + far_first.astype(single)
    experts_out_grad = t_dot(hid_kept, d_answer_kept) + far_second.astype(single)

    qkv_part = grads_wide[:, :QKV_COLS].reshape(PARTS, 12, QKV_COLS)
    sin_part1 = grads_wide[:, QKV_COLS:].reshape(4, 24, 256)
    attn_part, sout_part1 = grads_tall[:24].reshape(2, 12, WIDTH), grads_tall[24:]

    conv_grads = jnp.concatenate([d_taps, d_bias[None]], axis=0)
    conv_all = jnp.concatenate(
        [
            lax.dynamic_update_slice_in_dim(
                jnp.zeros((KW + 1, DI), single), conv_grads[:, :INNER], team * INNER, 1
            ),
            conv_grads[:, INNER:],
        ],
        axis=1,
    )
    conv_all = conv_all.reshape(5, 8, 16, 26).transpose(2, 1, 0, 3).reshape(16, 8, 130)
    head_all = lax.dynamic_update_slice_in_dim(
        jnp.zeros((3, H), single), jnp.stack([d_step, d_decay, d_skip]), team * HEADS_HERE, 1
    )
    head_all = jnp.broadcast_to(head_all.reshape(1, 1, 3 * H), (16, 8, 3 * H))
    gain_all = lax.dynamic_update_slice_in_dim(
        jnp.zeros((16, 8, 24), single), d_norm_gain.reshape(16, 1, 24), team, 1
    )
    d_gains = jnp.stack([jnp.stack([d_gain00, d_gain01]), jnp.stack([d_gain10, d_gain11])])
    d_gains = d_gains.reshape(2, 2, 4, 16, 24).transpose(3, 0, 2, 1, 4).reshape(16, 8, 48)
    d_router = jnp.stack([d_router0, d_router1]).reshape(2, 4, 16, 24 * EXPERTS)
    d_router = d_router.transpose(2, 0, 1, 3).reshape(16, 8, 24 * EXPERTS)
    small_grads = jnp.concatenate([d_router, conv_all, gain_all, d_gains, head_all], axis=2)
    small_grads = jnp.pad(small_grads, ((0, 0), (0, 0), (0, 2 * IN_COLS - small_grads.shape[2])))
    small_grads = small_grads.astype(brain).reshape(16, 8, 2, IN_COLS)
    d_main = jnp.concatenate(
        [d_w_in.astype(brain).reshape(16, 8, 12, IN_COLS), small_grads], axis=2
    )
    d_outs = jnp.concatenate(
        [d_w_out.astype(brain).reshape(16, 24, WIDTH), d_sout0.astype(brain).reshape(16, 8, WIDTH)],
        axis=1,
    )
    main_part, outs_part, sin_part0 = rank_sum(
        [d_main.reshape(16, 112, IN_COLS), d_outs, shared_in_parts(d_sin0)], 17, "rank_grads"
    )
    main_part = main_part.reshape(PARTS, 14, IN_COLS)
    out_proj_grad, sout_part0 = outs_part[:24], outs_part[24:]
    sin_part0 = sin_part0.reshape(4, 24, 256)

    main_end, qkv_end, sin_end, sout_end, attn_end = exchange(
        [
            (pad_rows(main_part, 16), "swap"),
            (pad_rows(qkv_part, 16), "swap"),
            (pad_rows(jnp.concatenate([sin_part0, sin_part1], axis=0), 32), "swap"),
            (pad_rows(jnp.stack([sout_part0, sout_part1]), 16), "phase"),
            (pad_rows(attn_part, 16), "zl"),
        ],
        TEAM,
        18,
        "team_end",
    )
    main_end = main_end.astype(single)
    rows_end = main_end[:, :12]

    def side_by_side(value):
        return value.transpose(1, 0, 2).reshape(value.shape[1], -1)

    in_proj_grad = jnp.concatenate(
        [
            side_by_side(rows_end[:, :, :INNER]),
            side_by_side(rows_end[:, :, INNER : 2 * INNER]),
            jnp.sum(rows_end[:, :, 2 * INNER : 2 * INNER + 2 * N], axis=0),
            side_by_side(
                rows_end[:, :, 2 * INNER + 2 * N : 2 * INNER + 2 * N + HEADS_HERE]
            ),
        ],
        axis=1,
    )
    small_end = jnp.sum(main_end[:, 12:14], axis=0).reshape(2 * IN_COLS)
    router_grad = small_end[: 24 * EXPERTS].reshape(1, 24, EXPERTS)
    at = 24 * EXPERTS
    conv_end = small_end[at : at + 130].reshape(5, 26)
    at += 130
    norm_gain_grad = small_end[at : at + 24]
    at += 24
    norm_gains_grad = small_end[at : at + 48].reshape(1, 2, 24)
    at += 48
    heads_end = small_end[at : at + 3 * H].reshape(3, H)
    qkv_end = qkv_end[:, :12].astype(single).reshape(4, 2, 12, QKV_COLS)
    qkv_end = jnp.sum(qkv_end, axis=1)
    query_grad = side_by_side(qkv_end[:, :, :384])
    kv_grad = qkv_end[:, :, 384:].reshape(4, 12, 2, 128).transpose(1, 2, 0, 3).reshape(12, 1024)
    sin_end = sin_end[:, :24].astype(single).reshape(2, 4, 24, 2, 16, 8)
    shared_in_grad = sin_end.transpose(2, 3, 1, 4, 0, 5).reshape(1, 24, 2048)
    shared_out_grad = sout_end[:, :8].astype(single).reshape(1, 16, WIDTH)
    attn_out_grad = jnp.sum(attn_end[:, :12].astype(single), axis=0)

    return (
        phase_outputs,
        input_grads,
        in_proj_grad,
        conv_end[:KW],
        conv_end[KW],
        heads_end[0],
        heads_end[1],
        heads_end[2],
        norm_gain_grad,
        out_proj_grad.astype(single),
        query_grad,
        kv_grad,
        attn_out_grad,
        norm_gains_grad,
        router_grad,
        shared_in_grad,
        shared_out_grad,
        experts_in_grad[None, None],
        experts_out_grad[None, None],
    )


def solution(mesh):
    fine = Mesh(mesh.devices.reshape(tuple(SIZES.values())), ALL)
    in_specs = (
        P(None, DP, None),
        P(None, DP, None),
        P(None, DP, None),
        P(None, DP, None),
        P(ALL, None),
        P(None, ALL),
        P(ALL),
        P(),
        P(),
        P(),
        P(ALL),
        P(ALL, None),
        P(ALL, None),
        P(ALL, None),
        P(ALL, None),
        P("phase", None, DP),
        P("phase", DP, None),
        P("phase", DP, None),
        P("phase", DP, None),
        P("phase", DP, None, None),
        P("phase", DP, None, None),
    )
    out_specs = (
        P("phase", None, DP, None),
        P("phase", None, DP, None),
        P(ALL, None),
        P(None, ALL),
        P(ALL),
        P(),
        P(),
        P(),
        P(ALL),
        P(ALL, None),
        P(ALL, None),
        P(ALL, None),
        P(ALL, None),
        P("phase", None, DP),
        P("phase", DP, None),
        P("phase", DP, None),
        P("phase", DP, None),
        P("phase", DP, None, None),
        P("phase", DP, None, None),
    )
    return jax.shard_map(
        per_device, mesh=fine, in_specs=in_specs, out_specs=out_specs, check_vma=False
    )
```

```python
import functools

import jax
import jax.numpy as jnp
from jax import lax
from jax.experimental import pallas as pl
from jax.experimental.pallas import tpu as pltpu
from jax.sharding import Mesh
from jax.sharding import PartitionSpec as P

H = 48
P_SIZE = 64
N = 128
KW = 4
QUERY_HEADS = 12
KEY_VALUE_HEADS = 4
HEAD_SIZE = 128
DI = 3072
CONVW = 3328
WIDTH = 1536
SEQ = 64
EXPERTS = 64
SLOTS = 8
PARTS = 8
HEADS_HERE = H // PARTS
INNER = DI // PARTS
IN_COLS = 1152
QKV_COLS = 640

SIZES = {"phase": 2, "zh": 2, "zl": 2, "yh": 2, "x": 4, "core": 2}
TEAM = ("phase", "zh", "zl")
HALF = ("phase", "zh")
RANK = ("yh", "x", "core")
DP = ("zh", "zl", "yh", "x", "core")
ALL = ("phase", "zh", "zl", "yh", "x", "core")
MESH_ID = pl.DeviceIdType.MESH

eps = 1e-05
single = jnp.float32
brain = jnp.bfloat16


def place_of(axes, index):
    out = {}
    for name in reversed(axes):
        out[name] = lax.rem(index, SIZES[name])
        index = lax.div(index, SIZES[name])
    return out


def size_of(axes):
    total = 1
    for name in axes:
        total *= SIZES[name]
    return total


def my_place(axes):
    me = jnp.int32(0)
    for name in axes:
        me = me * SIZES[name] + lax.axis_index(name)
    return me


def greet(barrier, device):
    pl.semaphore_signal(barrier, inc=1, device_id=device, device_id_type=MESH_ID)


def send(source, target, send_sem, recv_sem, device):
    copy = pltpu.make_async_remote_copy(
        src_ref=source,
        dst_ref=target,
        send_sem=send_sem,
        recv_sem=recv_sem,
        device_id=device,
        device_id_type=MESH_ID,
    )
    copy.start()
    return copy


def team_copies(axes, modes, sources, targets, send_sem, recv_sem, own_sem):
    n = size_of(axes)
    me = my_place(axes)
    copies = []
    for k in range(1, n):
        peer = lax.rem(me + k, n)
        device = place_of(axes, peer)
        for item, mode in enumerate(modes):
            if mode in SIZES:
                continue
            source = sources[item].at[peer] if mode == "swap" else sources[item]
            copies.append(
                send(
                    source,
                    targets[item].at[me],
                    send_sem.at[item, k],
                    recv_sem.at[item, k],
                    device,
                )
            )
    for item, mode in enumerate(modes):
        slot = me
        source = sources[item] if mode == "gather" else sources[item].at[me]
        if mode in SIZES:
            slot = lax.axis_index(mode)
            source = sources[item].at[slot]
            copies.append(
                send(
                    sources[item].at[1 - slot],
                    targets[item].at[slot],
                    send_sem.at[item, 0],
                    recv_sem.at[item, 0],
                    {mode: 1 - slot},
                )
            )
        copy = pltpu.make_async_copy(source, targets[item].at[slot], own_sem.at[item])
        copy.start()
        copies.append(copy)
    return copies


def greet_team(barrier, axes):
    n = size_of(axes)
    me = my_place(axes)
    for k in range(1, n):
        greet(barrier, place_of(axes, lax.rem(me + k, n)))
    return n - 1


def exchange_kernel(axes, modes, *refs):
    count = len(modes)
    barrier = pltpu.get_barrier_semaphore()
    pl.semaphore_wait(barrier, greet_team(barrier, axes))
    copies = team_copies(axes, modes, refs[:count], refs[count : 2 * count], *refs[2 * count :])
    for copy in copies:
        copy.wait()


def received(axes, items):
    n = size_of(axes)
    return [
        jax.ShapeDtypeStruct(((n,) if mode == "gather" else ()) + array.shape, array.dtype)
        for array, mode in items
    ]


def call(kernel, arrays, shapes, scratch, number, name, microseconds):
    moved = sum(s.size * s.dtype.itemsize for s in shapes)
    return pl.pallas_call(
        kernel,
        out_shape=shapes,
        in_specs=[pl.BlockSpec(memory_space=pltpu.VMEM)] * len(arrays),
        out_specs=[pl.BlockSpec(memory_space=pltpu.VMEM)] * len(shapes),
        scratch_shapes=scratch,
        compiler_params=pltpu.CompilerParams(
            collective_id=number, has_side_effects=True, vmem_limit_bytes=48 << 20
        ),
        cost_estimate=pl.CostEstimate(
            flops=microseconds * 10**9, bytes_accessed=2 * moved, transcendentals=0
        ),
        name=name,
    )(*arrays)


def team_semaphores(axes, items):
    return [
        pltpu.SemaphoreType.DMA((len(items), size_of(axes))),
        pltpu.SemaphoreType.DMA((len(items), size_of(axes))),
        pltpu.SemaphoreType.DMA((len(items),)),
    ]


def exchange(items, axes, number, name):
    return call(
        functools.partial(exchange_kernel, axes, tuple(mode for _, mode in items)),
        [array for array, _ in items],
        received(axes, items),
        team_semaphores(axes, items),
        number,
        name,
        20,
    )


def rank_devices():
    yh, x, core = lax.axis_index("yh"), lax.axis_index("x"), lax.axis_index("core")
    across = [lax.rem(x + k, 4) for k in range(4)]
    out = []
    for dy in range(2):
        for dx in range(4):
            for dc in range(2):
                y_at = 1 - yh if dy else yh
                c_at = 1 - core if dc else core
                device = {"yh": y_at, "x": across[dx], "core": c_at}
                out.append((device, y_at * 8 + across[dx] * 2 + c_at))
    return out


def for_each_expert_place(action):
    z = lax.axis_index("zh") * 2 + lax.axis_index("zl")
    rank = rank_devices()

    def of_layer(layer, own):
        high, low = lax.div(layer, 2), lax.rem(layer, 2)
        for k, (device, at) in enumerate(rank):
            action(dict(device, zh=high, zl=low), layer * 16 + at, own and k == 0)

    of_layer(z, True)

    def step(k, carry):
        of_layer(lax.rem(z + k, 4), False)
        return carry

    lax.fori_loop(1, 4, step, 0)


def expert_exchange_kernel(count, modes, *refs):
    every = count + len(modes)
    sources, targets = refs[:every], refs[every : 2 * every]
    send_sem, recv_sem, own_sem, rows_sent, rows_got = refs[2 * every :]
    mine = my_place(DP)
    barrier = pltpu.get_barrier_semaphore()

    def welcome(device, at, own):
        if not own:
            greet(barrier, device)

    for_each_expert_place(welcome)
    pl.semaphore_wait(barrier, 63 + greet_team(barrier, TEAM))
    team = team_copies(
        TEAM, modes, sources[count:], targets[count:], send_sem, recv_sem, own_sem
    )

    def give(device, at, own):
        for item in range(count):
            source, target = sources[item].at[at], targets[item].at[mine]
            if own:
                pltpu.make_async_copy(source, target, rows_got.at[item]).start()
            else:
                send(source, target, rows_sent.at[item], rows_got.at[item], device)

    for_each_expert_place(give)
    for item in range(count):
        sent = sources[item].at[pl.ds(0, 63)]
        pltpu.make_async_copy(sent, sent, rows_sent.at[item]).wait()
        pltpu.make_async_copy(targets[item], targets[item], rows_got.at[item]).wait()
    for copy in team:
        copy.wait()


def expert_exchange(rows, items, number, name):
    rows = [value.reshape(EXPERTS, SLOTS, WIDTH) for value in rows]
    count = len(rows)
    out = call(
        functools.partial(expert_exchange_kernel, count, tuple(mode for _, mode in items)),
        rows + [array for array, _ in items],
        [jax.ShapeDtypeStruct(value.shape, brain) for value in rows] + received(TEAM, items),
        team_semaphores(TEAM, items)
        + [pltpu.SemaphoreType.DMA((count,)), pltpu.SemaphoreType.DMA((count,))],
        number,
        name,
        50 * count,
    )
    rows_got = [value.reshape(EXPERTS * SLOTS, WIDTH) for value in out[:count]]
    return rows_got + list(out[count:])


def rank_gather_kernel(count, *refs):
    sources, targets = refs[:count], refs[count : 2 * count]
    send_sem, recv_sem, own_sem = refs[2 * count :]
    yh, x, core = lax.axis_index("yh"), lax.axis_index("x"), lax.axis_index("core")
    right, left, far = lax.rem(x + 1, 4), lax.rem(x + 3, 4), lax.rem(x + 2, 4)
    other = 1 - yh
    to_y, to_right, to_left, to_core = {"yh": other}, {"x": right}, {"x": left}, {"core": 1 - core}
    barrier = pltpu.get_barrier_semaphore()
    for device in (to_y, to_right, to_left, to_core):
        greet(barrier, device)
    pl.semaphore_wait(barrier, 4)

    def slot(y_at, x_at):
        return y_at * 8 + x_at * 2 + core

    sent = []

    def pass_on(item, at, kind, device, source=None):
        target = targets[item].at[at]
        copy = send(
            target if source is None else source,
            target,
            send_sem.at[item, kind],
            recv_sem.at[item, kind],
            device,
        )
        sent.append(copy)
        return copy

    def arrived(item, kind):
        pltpu.make_async_copy(sources[item], sources[item], recv_sem.at[item, kind]).wait()

    items = range(count)
    me = slot(yh, x)
    own = []
    for item in items:
        pass_on(item, me, 0, to_y, sources[item])
        pass_on(item, me, 1, to_right, sources[item])
        pass_on(item, me, 2, to_left, sources[item])
        pass_on(item, me, 7, to_core, sources[item])
        copy = pltpu.make_async_copy(sources[item], targets[item].at[me], own_sem.at[item])
        copy.start()
        own.append(copy)
    steps = (
        (1, slot(yh, left), ((5, to_right), (8, to_core))),
        (0, slot(other, x), ((3, to_right), (4, to_left), (9, to_core))),
        (2, slot(yh, right), ((10, to_core),)),
        (4, slot(other, right), ((6, to_left), (11, to_core))),
        (3, slot(other, left), ((12, to_core),)),
        (5, slot(yh, far), ((13, to_core),)),
        (6, slot(other, far), ((14, to_core),)),
    )
    for kind, at, onward in steps:
        for item in items:
            arrived(item, kind)
            for next_kind, device in onward:
                pass_on(item, at, next_kind, device)
    for item in items:
        for kind in range(7, 15):
            arrived(item, kind)
    for copy in own:
        copy.wait()
    for copy in sent:
        copy.wait_send()


def rank_gather(arrays, number, name):
    count = len(arrays)
    return call(
        functools.partial(rank_gather_kernel, count),
        arrays,
        [jax.ShapeDtypeStruct((16,) + array.shape, array.dtype) for array in arrays],
        [
            pltpu.SemaphoreType.DMA((count, 15)),
            pltpu.SemaphoreType.DMA((count, 15)),
            pltpu.SemaphoreType.DMA((count,)),
        ],
        number,
        name,
        40,
    )


def rank_sum_kernel(count, extra, *refs):
    every = count + extra
    sources, given = refs[:count], refs[count:every]
    targets, taken = refs[every : every + count], refs[every + count : 2 * every]
    refs = refs[2 * every :]
    from_core, totals, arrivals = (refs[k * count : (k + 1) * count] for k in range(3))
    send_sem, recv_sem, give_sem, take_sem = refs[3 * count :]
    yh, x, core = lax.axis_index("yh"), lax.axis_index("x"), lax.axis_index("core")
    right, left, far = lax.rem(x + 1, 4), lax.rem(x + 3, 4), lax.rem(x + 2, 4)
    other = 1 - yh
    to_y, to_right, to_left, to_core = {"yh": other}, {"x": right}, {"x": left}, {"core": 1 - core}
    barrier = pltpu.get_barrier_semaphore()
    to_phase = {"phase": 1 - lax.axis_index("phase")}
    for device in (to_y, to_right, to_left, to_core, to_phase):
        greet(barrier, device)
    pl.semaphore_wait(barrier, 5)
    items = range(count)
    sent = []

    def pass_on(item, at, kind, device):
        copy = send(
            totals[item].at[at],
            arrivals[item].at[kind],
            send_sem.at[item, kind],
            recv_sem.at[item, kind],
            device,
        )
        sent.append(copy)

    def arrived(item, kind):
        landed = arrivals[item].at[kind]
        pltpu.make_async_copy(landed, landed, recv_sem.at[item, kind]).wait()
        return arrivals[item][kind].astype(single)

    def slot(y_at, x_at):
        return y_at * 4 + x_at

    for item in items:
        sent.append(
            send(
                sources[item].at[:, 1 - core],
                from_core[item],
                send_sem.at[item, 7],
                recv_sem.at[item, 7],
                to_core,
            )
        )
    swaps = [
        send(given[k], taken[k], give_sem.at[k], take_sem.at[k], to_phase) for k in range(extra)
    ]
    for item in items:
        landed = from_core[item]
        pltpu.make_async_copy(landed, landed, recv_sem.at[item, 7]).wait()

        def add(at):
            value = sources[item][at, core].astype(single) + from_core[item][at].astype(single)
            totals[item][at] = value.astype(brain)

        add(slot(yh, far))
        pass_on(item, slot(yh, far), 0, to_right)
        add(slot(other, far))
        pass_on(item, slot(other, far), 1, to_left)
        add(slot(other, right))
        pass_on(item, slot(other, right), 3, to_right)
        add(slot(yh, left))
        pass_on(item, slot(yh, left), 5, to_left)
        for at in (slot(yh, right), slot(other, left), slot(yh, x), slot(other, x)):
            add(at)
    for item in items:
        at = slot(yh, right)
        totals[item][at] = (totals[item][at].astype(single) + arrived(item, 0)).astype(brain)
        pass_on(item, at, 2, to_right)
        at = slot(other, left)
        totals[item][at] = (totals[item][at].astype(single) + arrived(item, 1)).astype(brain)
        pass_on(item, at, 4, to_left)
    for item in items:
        at = slot(other, x)
        value = totals[item][at].astype(single) + arrived(item, 3)
        totals[item][at] = (value + arrived(item, 4)).astype(brain)
        pass_on(item, at, 6, to_y)
    for item in items:
        value = totals[item][slot(yh, x)].astype(single) + arrived(item, 5)
        value = value + arrived(item, 2)
        targets[item][...] = (value + arrived(item, 6)).astype(targets[item].dtype)
    for copy in sent:
        copy.wait_send()
    for copy in swaps:
        copy.wait()


def rank_sum(arrays, swapped, number, name):
    count, extra = len(arrays), len(swapped)
    arrays = [array.reshape((8, 2) + array.shape[1:]) for array in arrays]
    pieces = [array.shape[2:] for array in arrays]
    scratch = [pltpu.VMEM((8,) + piece, brain) for piece in pieces]
    scratch += [pltpu.VMEM((8,) + piece, brain) for piece in pieces]
    scratch += [pltpu.VMEM((7,) + piece, brain) for piece in pieces]
    scratch += [pltpu.SemaphoreType.DMA((count, 8)), pltpu.SemaphoreType.DMA((count, 8))]
    scratch += [pltpu.SemaphoreType.DMA((extra,)), pltpu.SemaphoreType.DMA((extra,))]
    return call(
        functools.partial(rank_sum_kernel, count, extra),
        arrays + swapped,
        [jax.ShapeDtypeStruct(piece, brain) for piece in pieces]
        + [jax.ShapeDtypeStruct(array.shape, array.dtype) for array in swapped],
        scratch,
        number,
        name,
        45,
    )


def dot(left, right):
    return jnp.dot(left, right, preferred_element_type=single)


def dot_t(left, right):
    return lax.dot_general(left, right, (((1,), (1,)), ((), ())), preferred_element_type=single)


def t_dot(left, right):
    return lax.dot_general(left, right, (((0,), (0,)), ((), ())), preferred_element_type=single)


def exact(spec, left, right):
    return jnp.einsum(
        spec, left, right, precision=lax.Precision.HIGHEST, preferred_element_type=single
    )


def rms_scale(value, gain):
    return value * lax.rsqrt(jnp.mean(value * value, axis=-1, keepdims=True) + eps) * gain


def swiglu(value):
    half = value.shape[-1] // 2
    return jax.nn.silu(value[..., :half]) * value[..., half:]


def shuffle_matrix():
    to = jnp.arange(WIDTH, dtype=jnp.int32)
    origin = to // 12 % 8 * 192 + to // 96 * 12 + to % 12
    return (jnp.arange(WIDTH, dtype=jnp.int32)[:, None] == origin[None, :]).astype(brain)


def shuffle(value, matrix):
    return dot(value, matrix).astype(brain)


def unshuffle(value, matrix):
    high = value.astype(brain)
    lower = (value - high.astype(single)).astype(brain)
    both = dot_t(jnp.concatenate([high, lower], axis=0), matrix)
    return both[: value.shape[0]] + both[value.shape[0] :]


def after(values, first):
    return lax.optimization_barrier((values, first))[0]


def pad_rows(value, rows):
    return jnp.pad(value, [(0, 0)] * (value.ndim - 2) + [(0, rows - value.shape[-2]), (0, 0)])


def pad_to(value, rows, columns):
    return jnp.pad(value, ((0, rows - value.shape[0]), (0, columns - value.shape[1])))


def allowed_pairs(seg):
    position = jnp.arange(SEQ, dtype=jnp.int32)
    return (position[:, None] >= position[None, :]) & (seg[..., :, None] == seg[..., None, :])


def product(left, right, dims, precision=None):
    return lax.dot_general(
        left, right, (dims, ((), ())), precision=precision, preferred_element_type=single
    )


def sharp(left, right, dims):
    return product(left, right, dims, lax.Precision.HIGHEST)


def blunt(left, right, dims):
    return product(left.astype(brain), right.astype(brain), dims)


def mamba_parts(zx_ref, masks_ref, same_ref, taps_ref, heads_ref):
    zx = zx_ref[0]
    conv_in = zx[:, INNER : 2 * INNER + 2 * N]
    taps = taps_ref[...]
    same = same_ref[0]
    moved = [conv_in]
    for k in range(1, KW):
        moved.append(pltpu.roll(conv_in, k, 0) * same[:, k : k + 1])
    conv = taps[KW : KW + 1]
    for k in range(KW):
        conv = conv + taps[KW - 1 - k : KW - k] * moved[k]
    gate = jax.nn.sigmoid(conv)
    active = conv * gate
    heads = heads_ref[...]
    raw = zx[:, 2 * INNER + 2 * N :] + heads[0:1]
    step = jnp.maximum(raw, 0.0) + jnp.log1p(jnp.exp(-jnp.abs(raw)))
    rate = step * heads[1:2]
    rows = lax.broadcasted_iota(jnp.int32, (SEQ, SEQ), 0)
    columns = lax.broadcasted_iota(jnp.int32, (SEQ, SEQ), 1)
    lower = (rows >= columns).astype(single)
    total = sharp(lower, rate, ((1,), (0,)))
    total_t = sharp(rate, lower, ((0,), (1,)))
    unit = (rows == columns).astype(single)
    step_t = sharp(step, unit, ((0,), (1,)))
    values = active[:, :INNER]
    in_state, out_state = active[:, INNER : INNER + N], active[:, INNER + N :]
    meeting = sharp(out_state, in_state, ((1,), (1,)))
    allowed = masks_ref[0]
    decays = []
    results = []
    for h in range(HEADS_HERE):
        fall = jnp.exp(jnp.minimum(total[:, h : h + 1] - total_t[h : h + 1], 0.0)) * allowed
        mixing = fall * meeting * step_t[h : h + 1]
        decays.append((fall, mixing))
        results.append(blunt(mixing, values[:, h * P_SIZE : (h + 1) * P_SIZE], ((1,), (0,))))
    result = jnp.concatenate(results, axis=1) + taps[5:6, :INNER] * values
    z = zx[:, :INNER]
    open_z = jax.nn.sigmoid(z)
    return (
        (zx, taps, same, moved, conv, gate, heads, raw, step, step_t, unit, lower),
        (values, in_state, out_state, meeting, decays, result, z, open_z),
    )


def mamba_forward_kernel(zx_ref, masks_ref, same_ref, taps_ref, heads_ref, part_ref, squares_ref):
    (_, taps, *_), (*_, result, z, open_z) = mamba_parts(
        zx_ref, masks_ref, same_ref, taps_ref, heads_ref
    )
    gated = result * (z * open_z)
    part_ref[0] = (gated * taps[6:7, :INNER]).astype(brain)
    sums = sharp(jnp.ones((8, INNER), single), gated * gated, ((1,), (1,)))
    squares_ref[0] = jnp.concatenate([sums, jnp.zeros((8, 128 - SEQ), single)], axis=1)


def mamba_backward_kernel(
    zx_ref, masks_ref, same_ref, taps_ref, heads_ref, d_yn_ref, scalars_ref, d_zx_ref, yn_ref, sums_ref
):
    first, second = mamba_parts(zx_ref, masks_ref, same_ref, taps_ref, heads_ref)
    (zx, taps, same, moved, conv, gate, heads, raw, step, step_t, unit, lower) = first
    (values, in_state, out_state, meeting, decays, result, z, open_z) = second
    scalars = sharp(unit, scalars_ref[0][:, :SEQ], ((1,), (1,)))
    inverse, along = scalars[:, 0:1], scalars[:, 1:2]
    gain, skip = taps[6:7, :INNER], taps[5:6, :INNER]
    d_yn = d_yn_ref[0]
    shut = z * open_z
    gated = result * shut
    scaled = gated * inverse
    yn_ref[0] = (scaled * gain).astype(brain)
    d_gain = jnp.sum(d_yn * scaled, axis=0, keepdims=True)
    d_gated = inverse * gain * d_yn - gated * along
    d_z = d_gated * result * (open_z * (1.0 + z * (1.0 - open_z)))
    d_result = d_gated * shut
    d_skip = jnp.sum(d_result * values, axis=0, keepdims=True)
    lanes = lax.broadcasted_iota(jnp.int32, (1, 128), 1)
    rows = lax.broadcasted_iota(jnp.int32, (128, 1), 0)
    d_meeting = jnp.zeros((SEQ, SEQ), single)
    by_row = jnp.zeros((SEQ, 128), single)
    by_column = jnp.zeros((128, SEQ), single)
    d_step_t = jnp.zeros((128, SEQ), single)
    d_values = []
    for h in range(HEADS_HERE):
        fall, mixing = decays[h]
        own = slice(h * P_SIZE, (h + 1) * P_SIZE)
        d_mixing = blunt(d_result[:, own], values[:, own], ((1,), (1,)))
        d_values.append(blunt(mixing, d_result[:, own], ((0,), (0,))))
        spread = d_mixing * fall
        d_meeting = d_meeting + spread * step_t[h : h + 1]
        spread = spread * meeting
        moving = spread * step_t[h : h + 1]
        by_row = by_row + jnp.sum(moving, axis=1, keepdims=True) * (lanes == h).astype(single)
        at = (rows == h).astype(single)
        by_column = by_column + at * jnp.sum(moving, axis=0, keepdims=True)
        d_step_t = d_step_t + at * jnp.sum(spread, axis=0, keepdims=True)
    d_total = by_row - sharp(unit, by_column, ((1,), (1,)))
    d_rate = sharp(lower, d_total, ((0,), (0,)))
    d_step = sharp(unit, d_step_t, ((1,), (1,))) + d_rate * heads[1:2]
    d_raw = d_step * jax.nn.sigmoid(raw)
    d_decay = jnp.sum(d_rate * step, axis=0, keepdims=True) * heads[1:2]
    d_active = jnp.concatenate(
        [
            jnp.concatenate(d_values, axis=1) + skip * d_result,
            sharp(d_meeting, out_state, ((0,), (0,))),
            sharp(d_meeting, in_state, ((1,), (0,))),
        ],
        axis=1,
    )
    d_conv = d_active * (gate * (1.0 + conv * (1.0 - gate)))
    d_taps = [jnp.sum(d_conv * moved[KW - 1 - k], axis=0, keepdims=True) for k in range(KW)]
    d_in = taps[KW - 1 : KW] * d_conv
    for k in range(1, KW):
        d_in = d_in + pltpu.roll(
            taps[KW - 1 - k : KW - k] * (d_conv * same[:, k : k + 1]), SEQ - k, 0
        )
    d_zx_ref[0] = jnp.concatenate([d_z, d_in, d_raw], axis=1).astype(brain)
    wide = INNER + 2 * N

    def widen(value):
        return jnp.concatenate(
            [value, jnp.zeros((1, wide - value.shape[1]), single)], axis=1
        )

    sums = jnp.concatenate(
        d_taps
        + [jnp.sum(d_conv, axis=0, keepdims=True), widen(d_skip), widen(d_gain)]
        + [widen(jnp.sum(d_raw, axis=0, keepdims=True)), widen(d_decay)]
        + [jnp.zeros((7, wide), single)],
        axis=0,
    )

    @pl.when(pl.program_id(0) == 0)
    def _():
        sums_ref[...] = jnp.zeros_like(sums_ref)

    sums_ref[...] += sums


def by_sequence(kernel, arrays, fixed, shapes, total_shapes, name):
    def whole(shape):
        return pl.BlockSpec(shape, lambda n: (0,) * len(shape))

    def one(shape):
        return pl.BlockSpec((1,) + shape[1:], lambda n: (n,) + (0,) * (len(shape) - 1))

    return pl.pallas_call(
        kernel,
        grid=(PARTS,),
        out_shape=shapes + total_shapes,
        in_specs=[
            whole(array.shape) if place in fixed else one(array.shape)
            for place, array in enumerate(arrays)
        ],
        out_specs=[one(s.shape) for s in shapes] + [whole(s.shape) for s in total_shapes],
        compiler_params=pltpu.CompilerParams(vmem_limit_bytes=32 << 20),
        name=name,
    )(*arrays)


def attend_scores(queries, keys, seg):
    scores = exact("nird,njd->nrij", queries, keys) * HEAD_SIZE ** (-0.5)
    scores = jnp.where(allowed_pairs(seg)[:, None], scores, -1e30)
    return jax.nn.softmax(scores, axis=-1)


def attend_mix(probs, values):
    return exact("nrij,njd->nird", probs, values)


def per_device(
    block_input,
    cotangent,
    segments,
    routes,
    in_proj,
    conv_taps,
    conv_bias,
    step_bias,
    decay_log,
    skip_weight,
    norm_gain,
    out_proj,
    query_proj,
    key_value_projection,
    attn_out_proj,
    norm_gains,
    router,
    shared_in,
    shared_out,
    experts_in,
    experts_out,
):
    phase = lax.axis_index("phase")
    first_phase = phase == 0
    zl = lax.axis_index("zl")
    team = phase * 4 + lax.axis_index("zh") * 2 + zl

    def mine(value):
        return lax.dynamic_index_in_dim(value, phase, 0, keepdims=False)

    start = mine(block_input)
    cot = mine(cotangent)
    seg = mine(segments)
    route_rows = mine(routes)

    both_ways = [(0, 1), (1, 0)]
    w_first, w_second = experts_in[0, 0], experts_out[0, 0]

    z_piece = in_proj[:, :DI].reshape(12, PARTS, INNER).transpose(1, 0, 2)
    x_piece = in_proj[:, DI : 2 * DI].reshape(12, PARTS, INNER).transpose(1, 0, 2)
    state_piece = jnp.broadcast_to(in_proj[None, :, 2 * DI : 2 * DI + 2 * N], (PARTS, 12, 2 * N))
    step_piece = in_proj[:, 2 * DI + 2 * N :].reshape(12, PARTS, HEADS_HERE).transpose(1, 0, 2)
    step_piece = jnp.pad(step_piece, ((0, 0), (0, 0), (0, 128 - HEADS_HERE)))
    q_piece = query_proj.reshape(12, 4, 384).transpose(1, 0, 2)
    kv_piece = key_value_projection.reshape(12, 2, 4, 128).transpose(2, 0, 1, 3).reshape(4, 12, 256)
    qkv_piece = jnp.repeat(jnp.concatenate([q_piece, kv_piece], axis=2), 2, axis=0)
    main_piece = pad_rows(
        jnp.concatenate([z_piece, x_piece, state_piece, step_piece, qkv_piece], axis=2), 16
    )
    sin_piece = shared_in[0].reshape(24, 2, 4, 16, 2, 8).transpose(4, 2, 0, 1, 3, 5)
    sin_piece = pad_rows(sin_piece.reshape(PARTS, 24, 256), 32)
    sout_piece = pad_rows(shared_out[0].reshape(2, 8, WIDTH), 16)
    attn_piece = jnp.broadcast_to(pad_rows(attn_out_proj, 16)[None], (2, 16, WIDTH))
    mixing = shuffle_matrix()
    rest = jnp.concatenate(
        [conv_taps.reshape(-1), conv_bias, norm_gain, norm_gains[0].reshape(-1)]
    )
    rest = jnp.pad(rest, (0, 512 - rest.shape[0])).reshape(4, 128)
    small = jnp.concatenate([router[0].reshape(12, 128), rest], axis=0)
    seg_piece = pad_to(seg, 8, 128)
    main_got, sin_got, sout_got, small_got, seg_got, start_all, attn_got = exchange(
        [
            (main_piece, "swap"),
            (sin_piece, "swap"),
            (sout_piece, "phase"),
            (small, "gather"),
            (seg_piece, "gather"),
            (shuffle(start, mixing), "gather"),
            (attn_piece, "zl"),
        ],
        TEAM,
        0,
        "team_start",
    )
    seg_all = seg_got[:, 0, :SEQ]
    main_got = main_got[:, :12].reshape(96, IN_COLS + QKV_COLS)
    sin_got = sin_got[:, :24].reshape(192, 256)
    w_in, small_all, w_out, sin_all, sout_all = rank_gather(
        [
            main_got[:, :IN_COLS],
            small_got.reshape(128, 128),
            pad_rows(out_proj, 32),
            sin_got[:96],
            pad_rows(sout_got[0, :8], 16),
        ],
        1,
        "rank_weights",
    )
    w_in = w_in.reshape(WIDTH, IN_COLS)
    w_out = w_out[:, :24].reshape(INNER, WIDTH)
    later_wide = jnp.concatenate([main_got[:, IN_COLS:], sin_got[96:]], axis=1)
    later_tall = jnp.concatenate([attn_got[:, :12].reshape(24, WIDTH), sout_got[1, :8]], axis=0)
    later_wide, later_tall = after((later_wide, later_tall), w_in)
    w_first_far = lax.ppermute(w_first, "phase", both_ways)
    w_second_far = lax.ppermute(w_second, "phase", both_ways)
    later_wide = lax.all_gather(later_wide, RANK, axis=0)
    later_tall = lax.all_gather(later_tall, RANK, axis=0)
    w_qkv = later_wide[:, :, :QKV_COLS].reshape(WIDTH, QKV_COLS)
    w_attn = later_tall[:, :24].reshape(16, 2, 12, WIDTH).transpose(1, 0, 2, 3)
    w_attn = w_attn.reshape(384, WIDTH)

    def hidden_in(value):
        return value.reshape(16, 4, 24, 256).transpose(1, 0, 2, 3).reshape(WIDTH, 256)

    sin_full = (hidden_in(sin_all), hidden_in(later_wide[:, :, QKV_COLS:]))
    sout_full = (sout_all[:, :8].reshape(128, WIDTH), later_tall[:, 24:].reshape(128, WIDTH))
    small_all = small_all.reshape(16, 2, 4, 16, 128)
    router_full = small_all[:, :, :, :12].reshape(16, 2, 4, 24, EXPERTS).transpose(1, 2, 0, 3, 4)
    router_full = router_full.reshape(2, WIDTH, EXPERTS)
    rest_all = small_all[:, :, :, 12:].reshape(16, 2, 4, 512)
    conv_full = rest_all[..., :130].reshape(16, 2, 4, 5, 26).transpose(3, 1, 2, 0, 4)
    conv_full = conv_full.reshape(5, CONVW).astype(single)
    gain_here = rest_all[..., 130:154].reshape(16, 8, 24)
    gain_here = lax.dynamic_index_in_dim(gain_here, team, 1, keepdims=False)
    gain_here = gain_here.reshape(INNER).astype(single)
    gains = rest_all[..., 154:202].reshape(16, 2, 4, 2, 24).transpose(1, 3, 2, 0, 4)
    gains = gains.reshape(2, 2, WIDTH).astype(single)
    conv_here = jnp.concatenate(
        [lax.dynamic_slice_in_dim(conv_full[:, :DI], team * INNER, INNER, 1), conv_full[:, DI:]],
        axis=1,
    )

    def heads_of(value):
        return lax.dynamic_slice_in_dim(value, team * HEADS_HERE, HEADS_HERE, 0)

    skip_wide = jnp.repeat(heads_of(skip_weight), P_SIZE)
    columns = jnp.stack([jnp.pad(skip_wide, (0, 2 * N)), jnp.pad(gain_here, (0, 2 * N))])
    taps_here = jnp.concatenate([conv_here, columns, jnp.zeros((1, INNER + 2 * N), single)], axis=0)
    heads_here = jnp.stack([heads_of(step_bias), -jnp.exp(heads_of(decay_log))])
    heads_here = pad_to(heads_here, 8, 128)
    allowed_all = allowed_pairs(seg_all).astype(single)
    same_all = [
        jnp.pad(seg_all[:, k:] == seg_all[:, : SEQ - k], ((0, 0), (k, 0))) for k in range(KW)
    ]
    same_all = jnp.pad(jnp.stack(same_all, axis=2).astype(single), ((0, 0), (0, 0), (0, 128 - KW)))

    expert_ids = jnp.arange(EXPERTS, dtype=jnp.int32)
    named = jnp.any(route_rows[:, :, None] == expert_ids, axis=1)
    position = jnp.arange(SEQ, dtype=jnp.int32)
    earlier = (position[:, None] > position[None, :]).astype(brain)
    slot = dot(earlier, named.astype(brain))
    slot = jnp.where(named, slot, -1.0).astype(brain)
    cell = jnp.arange(EXPERTS * SLOTS, dtype=jnp.int32)
    spread = (cell[None, :] // SLOTS == expert_ids[:, None]).astype(brain)
    taken = dot(slot, spread) == (cell % SLOTS).astype(single)
    taken_b = taken.astype(brain)

    def of_block(s):
        own = phase == s
        return (
            jnp.where(own, w_first, w_first_far),
            jnp.where(own, w_second, w_second_far),
        )

    def moe_open(s, hidden):
        normed = rms_scale(hidden, gains[s, 1]).astype(brain)
        logits = dot(normed, router_full[s])
        top = jnp.max(jnp.where(named, logits, -jnp.inf), axis=1, keepdims=True)
        weight = jnp.where(named, jnp.exp(logits - top), 0.0)
        gates = weight / jnp.sum(weight, axis=1, keepdims=True)
        gates_wide = jnp.where(taken, exact("ie,ec->ic", gates, spread.astype(single)), 0.0)
        return normed, gates, gates_wide, t_dot(taken_b, normed).astype(brain)

    def moe_experts(weights, rows_in):
        both = dot(rows_in, weights[0])
        hid = swiglu(both).astype(brain)
        return both, hid, dot(hid, weights[1]).astype(brain)

    def moe_shared(s, normed_all):
        both = dot(normed_all, sin_full[s])
        hid = swiglu(both).astype(brain)
        part = dot(hid, sout_full[s]).astype(brain)
        return both, hid, part.reshape(PARTS, SEQ, WIDTH)

    def moe_join(hidden, gates_wide, back, shared_got):
        high = gates_wide.astype(brain)
        lower = (gates_wide - high.astype(single)).astype(brain)
        moe = dot(high, back) + dot(lower, back)
        return (hidden + moe + jnp.sum(shared_got.astype(single), axis=0)).astype(brain)

    def back_open(d_out, gates_wide):
        gate_cell = jnp.sum(gates_wide, axis=0)
        return (t_dot(taken_b, d_out) * gate_cell[:, None]).astype(brain)

    def back_experts(weights, d_answer, both):
        d_hid = dot_t(d_answer, weights[1])
        d_both = jax.vjp(swiglu, both)[1](d_hid)[0].astype(brain)
        return d_both, dot_t(d_both, weights[0]).astype(brain)

    def back_shared(s, d_out_all, normed_all, both, hid):
        d_hid = dot_t(d_out_all, sout_full[s])
        d_sout = t_dot(hid, d_out_all)
        d_both = jax.vjp(swiglu, both)[1](d_hid)[0].astype(brain)
        d_sin = t_dot(normed_all, d_both)
        d_part = dot_t(d_both, sin_full[s]).astype(brain).reshape(PARTS, SEQ, WIDTH)
        return d_sin, d_sout, d_part

    def back_join(s, d_out, hidden, normed, gates, back, returned, d_shared_got):
        d_cells = jnp.where(taken, dot_t(d_out, back), 0.0)
        d_gates = exact("ic,ec->ie", d_cells, spread.astype(single))
        d_logits = gates * (d_gates - jnp.sum(gates * d_gates, axis=1, keepdims=True))
        d_normed = exact("ie,we->iw", d_logits, router_full[s].astype(single))
        d_router = exact("iw,ie->we", normed.astype(single), d_logits)
        d_normed = d_normed + dot(taken_b, returned) + jnp.sum(d_shared_got.astype(single), axis=0)
        d_hidden, d_gain = jax.vjp(rms_scale, hidden, gains[s, 1])[1](d_normed)
        return d_hidden + d_out.astype(single), d_gain, d_router

    def shared_in_parts(value):
        return value.astype(brain).reshape(4, 16, 24, 256).transpose(1, 0, 2, 3).reshape(16, 96, 256)

    u0 = start.astype(single)
    shuffled_gain = shuffle(gains[0, 0][None].astype(brain), mixing)[0].astype(single)
    n1_all = rms_scale(start_all.astype(single), shuffled_gain).astype(brain)
    n1_all = n1_all.reshape(PARTS * SEQ, WIDTH)
    zx = dot(n1_all, w_in).reshape(PARTS, SEQ, IN_COLS)

    core_inputs = [zx, allowed_all, same_all, taps_here, heads_here]
    part, squares = by_sequence(
        mamba_forward_kernel,
        core_inputs,
        (3, 4),
        [
            jax.ShapeDtypeStruct((PARTS, SEQ, INNER), brain),
            jax.ShapeDtypeStruct((PARTS, 8, 128), single),
        ],
        [],
        "mamba_forward",
    )
    part = dot(part.reshape(PARTS * SEQ, INNER), w_out)
    part = part.astype(brain).reshape(PARTS, SEQ, WIDTH)
    part_got, squares_got = exchange([(part, "swap"), (squares, "swap")], TEAM, 2, "team_mixed_0")
    mean_square = jnp.sum(squares_got[:, 0, :SEQ], axis=0) / DI
    inverse = lax.rsqrt(mean_square + eps)
    mixed0 = jnp.sum(part_got.astype(single), axis=0) * inverse[:, None]
    hidden0 = u0 + mixed0
    normed0, gates0, gates_wide0, rows_out0 = moe_open(0, hidden0)
    rows_in0, normed_all0 = expert_exchange([rows_out0], [(normed0, "gather")], 3, "spread_0")
    normed_all0 = normed_all0.reshape(PARTS * SEQ, WIDTH)
    weights0 = of_block(0)
    sboth0, shid0, shared_part0 = moe_shared(0, normed_all0)
    both0, hid0, answer0 = moe_experts(weights0, rows_in0)
    back0, shared_got0 = expert_exchange([answer0], [(shared_part0, "swap")], 4, "collect_0")
    out0 = moe_join(hidden0, gates_wide0, back0, shared_got0)

    u1 = out0.astype(single)
    n1 = rms_scale(u1, gains[1, 0]).astype(brain)
    (n1_half,) = exchange([(shuffle(n1, mixing), "gather")], HALF, 5, "half_n1")
    n1_half = n1_half.reshape(4 * SEQ, WIDTH)
    seg_half = lax.dynamic_index_in_dim(seg_all.reshape(4, 2, SEQ), zl, 1, keepdims=False)
    qkv = dot(n1_half, w_qkv).astype(brain).astype(single).reshape(4, SEQ, QKV_COLS)
    queries = qkv[..., :384].reshape(4, SEQ, 3, HEAD_SIZE)
    keys, values = qkv[..., 384:512], qkv[..., 512:]
    probs, score_pull = jax.vjp(lambda q, k: attend_scores(q, k, seg_half), queries, keys)
    heads, mix_pull = jax.vjp(attend_mix, probs.astype(brain).astype(single), values)
    heads = heads.astype(brain).reshape(4 * SEQ, 384)
    part1 = dot(heads, w_attn).astype(brain).reshape(4, SEQ, WIDTH)
    (part1_got,) = exchange([(part1, "swap")], HALF, 6, "half_mixed")
    mixed1 = jnp.sum(part1_got.astype(single), axis=0)
    hidden1 = u1 + mixed1

    normed1, gates1, gates_wide1, rows_out1 = moe_open(1, hidden1)
    rows_in1, d_answer1, normed_all1, cot_all = expert_exchange(
        [rows_out1, back_open(cot, gates_wide1)],
        [(normed1, "gather"), (cot, "gather")],
        7,
        "spread_1",
    )
    normed_all1 = normed_all1.reshape(PARTS * SEQ, WIDTH)
    cot_all = cot_all.reshape(PARTS * SEQ, WIDTH)
    weights1 = of_block(1)
    sboth1, shid1, shared_part1 = moe_shared(1, normed_all1)
    d_sin1, d_sout1, d_shared1 = back_shared(1, cot_all, normed_all1, sboth1, shid1)
    both1, hid1, answer1 = moe_experts(weights1, rows_in1)
    d_both1, d_rows1 = back_experts(weights1, d_answer1, both1)
    back1, returned1, shared_got1, d_shared_got1 = expert_exchange(
        [answer1, d_rows1], [(shared_part1, "swap"), (d_shared1, "swap")], 8, "collect_1"
    )
    out1 = moe_join(hidden1, gates_wide1, back1, shared_got1)

    d_hid1, d_gain11, d_router1 = back_join(
        1, cot, hidden1, normed1, gates1, back1, returned1, d_shared_got1
    )
    (d_mixed1,) = exchange([(d_hid1.astype(brain), "gather")], HALF, 11, "half_dmixed")
    d_mixed1 = d_mixed1.reshape(4 * SEQ, WIDTH)
    d_heads = dot_t(d_mixed1, w_attn).reshape(4, SEQ, 3, HEAD_SIZE)
    d_attn = t_dot(heads, d_mixed1)
    d_probs, d_values = mix_pull(d_heads)
    d_queries, d_keys = score_pull(d_probs)
    d_qkv = jnp.concatenate([d_queries.reshape(4, SEQ, 384), d_keys, d_values], axis=2)
    d_qkv = d_qkv.astype(brain).reshape(4 * SEQ, QKV_COLS)
    d_w_qkv = t_dot(n1_half, d_qkv)
    d_n1_part = dot_t(d_qkv, w_qkv).astype(brain).reshape(4, SEQ, WIDTH)
    grads_wide = jnp.concatenate(
        [d_w_qkv.astype(brain).reshape(16, 96, QKV_COLS), shared_in_parts(d_sin1)], axis=2
    )
    attn_part = d_attn.astype(brain).reshape(2, 16, 12, WIDTH).transpose(1, 0, 2, 3)
    grads_tall = jnp.concatenate(
        [attn_part.reshape(16, 24, WIDTH), d_sout1.astype(brain).reshape(16, 8, WIDTH)], axis=1
    )
    d_n1_part, grads_wide, grads_tall = lax.optimization_barrier(
        (d_n1_part, grads_wide, grads_tall)
    )
    grads_wide = lax.psum_scatter(grads_wide, RANK, scatter_dimension=0, tiled=True)[0]
    grads_tall = lax.psum_scatter(grads_tall, RANK, scatter_dimension=0, tiled=True)[0]
    (d_n1_got,) = exchange([(d_n1_part, "swap")], HALF, 12, "half_dn1")
    d_n1 = unshuffle(jnp.sum(d_n1_got.astype(single), axis=0), mixing)
    d_u1, d_gain10 = jax.vjp(rms_scale, u1, gains[1, 0])[1](d_n1)
    d_u1 = (d_u1 + d_hid1).astype(brain)

    d_answer0, d_out0_all = expert_exchange(
        [back_open(d_u1, gates_wide0)], [(d_u1, "gather")], 13, "spread_back_0"
    )
    d_out0_all = d_out0_all.reshape(PARTS * SEQ, WIDTH)
    d_sin0, d_sout0, d_shared0 = back_shared(0, d_out0_all, normed_all0, sboth0, shid0)
    d_both0, d_rows0 = back_experts(weights0, d_answer0, both0)
    expert0 = (rows_in0, d_both0, hid0, d_answer0)
    expert1 = (rows_in1, d_both1, hid1, d_answer1)
    give_rows, give_both, give_hid, give_answer = (
        jnp.where(first_phase, b, a) for a, b in zip(expert0, expert1)
    )
    give_first = t_dot(give_rows, give_both).astype(brain)
    give_second = t_dot(give_hid, give_answer).astype(brain)
    d_rows0, give_first, give_second = lax.optimization_barrier((d_rows0, give_first, give_second))
    far_first = lax.ppermute(give_first, "phase", both_ways)
    far_second = lax.ppermute(give_second, "phase", both_ways)
    returned0, d_shared_got0 = expert_exchange(
        [d_rows0], [(d_shared0, "swap")], 14, "collect_back_0"
    )
    d_hid0, d_gain01, d_router0 = back_join(
        0, d_u1, hidden0, normed0, gates0, back0, returned0, d_shared_got0
    )
    d_mixed0 = d_hid0.astype(brain)
    along = jnp.sum(d_mixed0.astype(single) * mixed0, axis=1)
    scalars = jnp.stack([inverse, inverse * inverse * along / DI])
    d_mixed0, scalars_all = exchange(
        [(d_mixed0, "gather"), (pad_to(scalars, 8, 128), "gather")], TEAM, 15, "team_dmixed"
    )
    d_mixed0 = d_mixed0.reshape(PARTS * SEQ, WIDTH)
    d_yn = dot_t(d_mixed0, w_out).reshape(PARTS, SEQ, INNER)
    d_zx, yn, core_sums = by_sequence(
        mamba_backward_kernel,
        core_inputs + [d_yn, scalars_all],
        (3, 4),
        [
            jax.ShapeDtypeStruct((PARTS, SEQ, IN_COLS), brain),
            jax.ShapeDtypeStruct((PARTS, SEQ, INNER), brain),
        ],
        [jax.ShapeDtypeStruct((16, INNER + 2 * N), single)],
        "mamba_backward",
    )
    d_w_out = t_dot(yn.reshape(PARTS * SEQ, INNER), d_mixed0)
    d_zx = d_zx.reshape(PARTS * SEQ, IN_COLS)
    d_norm_gain = core_sums[6, :INNER]
    d_skip = jnp.sum(core_sums[5, :INNER].reshape(HEADS_HERE, P_SIZE), axis=1)
    d_step, d_decay = core_sums[7, :HEADS_HERE], core_sums[8, :HEADS_HERE]
    d_w_in = t_dot(n1_all, d_zx)
    d_n1_part0 = dot_t(d_zx, w_in).astype(brain).reshape(PARTS, SEQ, WIDTH)
    d_n1_part0, grads_wide, grads_tall = lax.optimization_barrier(
        (d_n1_part0, grads_wide, grads_tall)
    )
    (d_n1_got0,) = exchange([(d_n1_part0, "swap")], TEAM, 16, "team_dn1")
    d_n1_0 = unshuffle(jnp.sum(d_n1_got0.astype(single), axis=0), mixing)
    d_u0, d_gain00 = jax.vjp(rms_scale, u0, gains[0, 0])[1](d_n1_0)
    d_u0 = d_u0 + d_hid0

    def keep_and_give(block0, block1):
        return jnp.where(first_phase, block0, block1), jnp.where(first_phase, block1, block0)

    def by_block(kept, got):
        return jnp.where(first_phase, jnp.stack([kept, got]), jnp.stack([got, kept]))[None]

    keep_out, give_out = keep_and_give(out0, out1)
    keep_grad, give_grad = keep_and_give(d_u0, d_u1.astype(single))

    qkv_part = grads_wide[:, :QKV_COLS].reshape(PARTS, 12, QKV_COLS)
    sin_part1 = grads_wide[:, QKV_COLS:].reshape(4, 24, 256)
    attn_part, sout_part1 = grads_tall[:24].reshape(2, 12, WIDTH), grads_tall[24:]

    conv_grads = core_sums[: KW + 1]
    conv_all = jnp.concatenate(
        [
            lax.dynamic_update_slice_in_dim(
                jnp.zeros((KW + 1, DI), single), conv_grads[:, :INNER], team * INNER, 1
            ),
            conv_grads[:, INNER:],
        ],
        axis=1,
    )
    conv_all = conv_all.reshape(5, 8, 16, 26).transpose(2, 1, 0, 3).reshape(16, 8, 130)
    head_all = lax.dynamic_update_slice_in_dim(
        jnp.zeros((3, H), single), jnp.stack([d_step, d_decay, d_skip]), team * HEADS_HERE, 1
    )
    head_all = jnp.broadcast_to(head_all.reshape(1, 1, 3 * H), (16, 8, 3 * H))
    gain_all = lax.dynamic_update_slice_in_dim(
        jnp.zeros((16, 8, 24), single), d_norm_gain.reshape(16, 1, 24), team, 1
    )
    d_gains = jnp.stack([jnp.stack([d_gain00, d_gain01]), jnp.stack([d_gain10, d_gain11])])
    d_gains = d_gains.reshape(2, 2, 4, 16, 24).transpose(3, 0, 2, 1, 4).reshape(16, 8, 48)
    d_router = jnp.stack([d_router0, d_router1]).reshape(2, 4, 16, 24 * EXPERTS)
    d_router = d_router.transpose(2, 0, 1, 3).reshape(16, 8, 24 * EXPERTS)
    small_grads = jnp.concatenate([d_router, conv_all, gain_all, d_gains, head_all], axis=2)
    small_grads = jnp.pad(small_grads, ((0, 0), (0, 0), (0, 2048 - small_grads.shape[2])))
    small_grads = small_grads.astype(brain).reshape(16, 128, 128)
    d_outs = jnp.concatenate(
        [d_w_out.astype(brain).reshape(16, 24, WIDTH), d_sout0.astype(brain).reshape(16, 8, WIDTH)],
        axis=1,
    )
    main_part, outs_part, sin_part0, small_part, got_out, got_grad = rank_sum(
        [
            d_w_in.astype(brain).reshape(16, 96, IN_COLS),
            d_outs,
            shared_in_parts(d_sin0),
            small_grads,
        ],
        [give_out, give_grad],
        17,
        "rank_grads",
    )
    phase_outputs = by_block(keep_out, got_out)
    input_grads = by_block(keep_grad, got_grad)
    main_part = main_part.reshape(PARTS, 12, IN_COLS)
    out_proj_grad, sout_part0 = outs_part[:24], outs_part[24:]
    sin_part0 = sin_part0.reshape(4, 24, 256)

    rows_kept, d_both_kept, hid_kept, d_answer_kept = (
        jnp.where(first_phase, a, b) for a, b in zip(expert0, expert1)
    )
    far_first, far_second = after((far_first, far_second), main_part)
    experts_in_grad = t_dot(rows_kept, d_both_kept) + far_first.astype(single)
    experts_out_grad = t_dot(hid_kept, d_answer_kept) + far_second.astype(single)

    main_end, qkv_end, sin_end, sout_end, attn_end, small_end = exchange(
        [
            (pad_rows(main_part, 16), "swap"),
            (pad_rows(qkv_part, 16), "swap"),
            (pad_rows(jnp.concatenate([sin_part0, sin_part1], axis=0), 32), "swap"),
            (pad_rows(jnp.stack([sout_part0, sout_part1]), 16), "phase"),
            (pad_rows(attn_part, 16), "zl"),
            (small_part.reshape(PARTS, 16, 128), "swap"),
        ],
        TEAM,
        18,
        "team_end",
    )
    rows_end = main_end[:, :12].astype(single)

    def side_by_side(value):
        return value.transpose(1, 0, 2).reshape(value.shape[1], -1)

    in_proj_grad = jnp.concatenate(
        [
            side_by_side(rows_end[:, :, :INNER]),
            side_by_side(rows_end[:, :, INNER : 2 * INNER]),
            jnp.sum(rows_end[:, :, 2 * INNER : 2 * INNER + 2 * N], axis=0),
            side_by_side(
                rows_end[:, :, 2 * INNER + 2 * N : 2 * INNER + 2 * N + HEADS_HERE]
            ),
        ],
        axis=1,
    )
    small_end = jnp.sum(small_end.astype(single), axis=0).reshape(2048)
    router_grad = small_end[: 24 * EXPERTS].reshape(1, 24, EXPERTS)
    at = 24 * EXPERTS
    conv_end = small_end[at : at + 130].reshape(5, 26)
    at += 130
    norm_gain_grad = small_end[at : at + 24]
    at += 24
    norm_gains_grad = small_end[at : at + 48].reshape(1, 2, 24)
    at += 48
    heads_end = small_end[at : at + 3 * H].reshape(3, H)
    qkv_end = qkv_end[:, :12].astype(single).reshape(4, 2, 12, QKV_COLS)
    qkv_end = jnp.sum(qkv_end, axis=1)
    query_grad = side_by_side(qkv_end[:, :, :384])
    kv_grad = qkv_end[:, :, 384:].reshape(4, 12, 2, 128).transpose(1, 2, 0, 3).reshape(12, 1024)
    sin_end = sin_end[:, :24].astype(single).reshape(2, 4, 24, 2, 16, 8)
    shared_in_grad = sin_end.transpose(2, 3, 1, 4, 0, 5).reshape(1, 24, 2048)
    shared_out_grad = sout_end[:, :8].astype(single).reshape(1, 16, WIDTH)
    attn_out_grad = jnp.sum(attn_end[:, :12].astype(single), axis=0)

    return (
        phase_outputs,
        input_grads,
        in_proj_grad,
        conv_end[:KW],
        conv_end[KW],
        heads_end[0],
        heads_end[1],
        heads_end[2],
        norm_gain_grad,
        out_proj_grad.astype(single),
        query_grad,
        kv_grad,
        attn_out_grad,
        norm_gains_grad,
        router_grad,
        shared_in_grad,
        shared_out_grad,
        experts_in_grad[None, None],
        experts_out_grad[None, None],
    )


def solution(mesh):
    fine = Mesh(mesh.devices.reshape(tuple(SIZES.values())), ALL)
    in_specs = (
        P(None, DP, None),
        P(None, DP, None),
        P(None, DP, None),
        P(None, DP, None),
        P(ALL, None),
        P(None, ALL),
        P(ALL),
        P(),
        P(),
        P(),
        P(ALL),
        P(ALL, None),
        P(ALL, None),
        P(ALL, None),
        P(ALL, None),
        P("phase", None, DP),
        P("phase", DP, None),
        P("phase", DP, None),
        P("phase", DP, None),
        P("phase", DP, None, None),
        P("phase", DP, None, None),
    )
    out_specs = (
        P("phase", None, DP, None),
        P("phase", None, DP, None),
        P(ALL, None),
        P(None, ALL),
        P(ALL),
        P(),
        P(),
        P(),
        P(ALL),
        P(ALL, None),
        P(ALL, None),
        P(ALL, None),
        P(ALL, None),
        P("phase", None, DP),
        P("phase", DP, None),
        P("phase", DP, None),
        P("phase", DP, None),
        P("phase", DP, None, None),
        P("phase", DP, None, None),
    )
    return jax.shard_map(
        per_device, mesh=fine, in_specs=in_specs, out_specs=out_specs, check_vma=False
    )
```

```python
import functools

import jax
import jax.numpy as jnp
from jax import lax
from jax.experimental import pallas as pl
from jax.experimental.pallas import tpu as pltpu
from jax.sharding import Mesh
from jax.sharding import PartitionSpec as P

H = 48
P_SIZE = 64
N = 128
KW = 4
QUERY_HEADS = 12
KEY_VALUE_HEADS = 4
HEAD_SIZE = 128
DI = 3072
CONVW = 3328
WIDTH = 1536
SEQ = 64
EXPERTS = 64
SLOTS = 8
PARTS = 8
HEADS_HERE = H // PARTS
INNER = DI // PARTS
IN_COLS = 1152
QKV_COLS = 640

SIZES = {"phase": 2, "zh": 2, "zl": 2, "yh": 2, "x": 4, "core": 2}
TEAM = ("phase", "zh", "zl")
HALF = ("phase", "zh")
QUAD = ("zh", "zl")
RANK = ("yh", "x", "core")
DP = ("zh", "zl", "yh", "x", "core")
ALL = ("phase", "zh", "zl", "yh", "x", "core")
MESH_ID = pl.DeviceIdType.MESH

eps = 1e-05
single = jnp.float32
brain = jnp.bfloat16


def place_of(axes, index):
    out = {}
    for name in reversed(axes):
        out[name] = lax.rem(index, SIZES[name])
        index = lax.div(index, SIZES[name])
    return out


def size_of(axes):
    total = 1
    for name in axes:
        total *= SIZES[name]
    return total


def my_place(axes):
    me = jnp.int32(0)
    for name in axes:
        me = me * SIZES[name] + lax.axis_index(name)
    return me


def greet(barrier, device):
    pl.semaphore_signal(barrier, inc=1, device_id=device, device_id_type=MESH_ID)


def send(source, target, send_sem, recv_sem, device):
    copy = pltpu.make_async_remote_copy(
        src_ref=source,
        dst_ref=target,
        send_sem=send_sem,
        recv_sem=recv_sem,
        device_id=device,
        device_id_type=MESH_ID,
    )
    copy.start()
    return copy


def team_copies(axes, modes, sources, targets, send_sem, recv_sem, own_sem):
    n = size_of(axes)
    me = my_place(axes)
    copies = []
    for k in range(1, n):
        peer = lax.rem(me + k, n)
        device = place_of(axes, peer)
        for item, mode in enumerate(modes):
            if mode in SIZES:
                continue
            source = sources[item].at[peer] if mode == "swap" else sources[item]
            copies.append(
                send(
                    source,
                    targets[item].at[me],
                    send_sem.at[item, k],
                    recv_sem.at[item, k],
                    device,
                )
            )
    for item, mode in enumerate(modes):
        slot = me
        source = sources[item] if mode == "gather" else sources[item].at[me]
        if mode in SIZES:
            slot = lax.axis_index(mode)
            source = sources[item].at[slot]
            copies.append(
                send(
                    sources[item].at[1 - slot],
                    targets[item].at[slot],
                    send_sem.at[item, 0],
                    recv_sem.at[item, 0],
                    {mode: 1 - slot},
                )
            )
        copy = pltpu.make_async_copy(source, targets[item].at[slot], own_sem.at[item])
        copy.start()
        copies.append(copy)
    return copies


def greet_team(barrier, axes):
    n = size_of(axes)
    me = my_place(axes)
    for k in range(1, n):
        greet(barrier, place_of(axes, lax.rem(me + k, n)))
    return n - 1


def exchange_kernel(axes, modes, *refs):
    count = len(modes)
    barrier = pltpu.get_barrier_semaphore()
    pl.semaphore_wait(barrier, greet_team(barrier, axes))
    copies = team_copies(axes, modes, refs[:count], refs[count : 2 * count], *refs[2 * count :])
    for copy in copies:
        copy.wait()


def received(axes, items):
    n = size_of(axes)
    return [
        jax.ShapeDtypeStruct(((n,) if mode == "gather" else ()) + array.shape, array.dtype)
        for array, mode in items
    ]


def call(kernel, arrays, shapes, scratch, number, name, microseconds):
    moved = sum(s.size * s.dtype.itemsize for s in shapes)
    return pl.pallas_call(
        kernel,
        out_shape=shapes,
        in_specs=[pl.BlockSpec(memory_space=pltpu.VMEM)] * len(arrays),
        out_specs=[pl.BlockSpec(memory_space=pltpu.VMEM)] * len(shapes),
        scratch_shapes=scratch,
        compiler_params=pltpu.CompilerParams(
            collective_id=number, has_side_effects=True, vmem_limit_bytes=48 << 20
        ),
        cost_estimate=pl.CostEstimate(
            flops=microseconds * 10**9, bytes_accessed=2 * moved, transcendentals=0
        ),
        name=name,
    )(*arrays)


def team_semaphores(axes, items):
    return [
        pltpu.SemaphoreType.DMA((len(items), size_of(axes))),
        pltpu.SemaphoreType.DMA((len(items), size_of(axes))),
        pltpu.SemaphoreType.DMA((len(items),)),
    ]


def exchange(items, axes, number, name):
    return call(
        functools.partial(exchange_kernel, axes, tuple(mode for _, mode in items)),
        [array for array, _ in items],
        received(axes, items),
        team_semaphores(axes, items),
        number,
        name,
        20,
    )


def rank_devices():
    yh, x, core = lax.axis_index("yh"), lax.axis_index("x"), lax.axis_index("core")
    across = [lax.rem(x + k, 4) for k in range(4)]
    out = []
    for dy in range(2):
        for dx in range(4):
            for dc in range(2):
                y_at = 1 - yh if dy else yh
                c_at = 1 - core if dc else core
                device = {"yh": y_at, "x": across[dx], "core": c_at}
                out.append((device, y_at * 8 + across[dx] * 2 + c_at))
    return out


def for_each_expert_place(action):
    z = lax.axis_index("zh") * 2 + lax.axis_index("zl")
    rank = rank_devices()

    def of_layer(layer, own):
        high, low = lax.div(layer, 2), lax.rem(layer, 2)
        for k, (device, at) in enumerate(rank):
            action(dict(device, zh=high, zl=low), layer * 16 + at, own and k == 0)

    of_layer(z, True)

    def step(k, carry):
        of_layer(lax.rem(z + k, 4), False)
        return carry

    lax.fori_loop(1, 4, step, 0)


def expert_exchange_kernel(count, modes, *refs):
    every = count + len(modes)
    sources, targets = refs[:every], refs[every : 2 * every]
    send_sem, recv_sem, own_sem, rows_sent, rows_got = refs[2 * every :]
    mine = my_place(DP)
    barrier = pltpu.get_barrier_semaphore()

    def welcome(device, at, own):
        if not own:
            greet(barrier, device)

    for_each_expert_place(welcome)
    pl.semaphore_wait(barrier, 63)
    team = team_copies(
        QUAD, modes, sources[count:], targets[count:], send_sem, recv_sem, own_sem
    )

    def give(device, at, own):
        for item in range(count):
            source, target = sources[item].at[at], targets[item].at[mine]
            if own:
                pltpu.make_async_copy(source, target, rows_got.at[item]).start()
            else:
                send(source, target, rows_sent.at[item], rows_got.at[item], device)

    for_each_expert_place(give)
    for item in range(count):
        sent = sources[item].at[pl.ds(0, 63)]
        pltpu.make_async_copy(sent, sent, rows_sent.at[item]).wait()
        pltpu.make_async_copy(targets[item], targets[item], rows_got.at[item]).wait()
    for copy in team:
        copy.wait()


def expert_exchange(rows, items, number, name):
    rows = [value.reshape(EXPERTS, SLOTS, WIDTH) for value in rows]
    count = len(rows)
    out = call(
        functools.partial(expert_exchange_kernel, count, tuple(mode for _, mode in items)),
        rows + [array for array, _ in items],
        [jax.ShapeDtypeStruct(value.shape, brain) for value in rows] + received(QUAD, items),
        team_semaphores(QUAD, items)
        + [pltpu.SemaphoreType.DMA((count,)), pltpu.SemaphoreType.DMA((count,))],
        number,
        name,
        40 * count,
    )
    rows_got = [value.reshape(EXPERTS * SLOTS, WIDTH) for value in out[:count]]
    return rows_got + list(out[count:])


def rank_gather_kernel(count, modes, *refs):
    every = count + len(modes)
    sources, targets = refs[:count], refs[every : every + count]
    team_sources, team_targets = refs[count:every], refs[every + count : 2 * every]
    send_sem, recv_sem, own_sem, *team_sems = refs[2 * every :]
    yh, x, core = lax.axis_index("yh"), lax.axis_index("x"), lax.axis_index("core")
    right, left, far = lax.rem(x + 1, 4), lax.rem(x + 3, 4), lax.rem(x + 2, 4)
    other = 1 - yh
    to_y, to_right, to_left, to_core = {"yh": other}, {"x": right}, {"x": left}, {"core": 1 - core}
    barrier = pltpu.get_barrier_semaphore()
    for device in (to_y, to_right, to_left, to_core):
        greet(barrier, device)
    pl.semaphore_wait(barrier, 4 + greet_team(barrier, TEAM))

    def slot(y_at, x_at):
        return y_at * 8 + x_at * 2 + core

    sent = []

    def pass_on(item, at, kind, device, source=None):
        target = targets[item].at[at]
        copy = send(
            target if source is None else source,
            target,
            send_sem.at[item, kind],
            recv_sem.at[item, kind],
            device,
        )
        sent.append(copy)
        return copy

    def arrived(item, kind):
        pltpu.make_async_copy(sources[item], sources[item], recv_sem.at[item, kind]).wait()

    items = range(count)
    me = slot(yh, x)
    own = []
    for item in items:
        pass_on(item, me, 0, to_y, sources[item])
        pass_on(item, me, 1, to_right, sources[item])
        pass_on(item, me, 2, to_left, sources[item])
        pass_on(item, me, 7, to_core, sources[item])
        copy = pltpu.make_async_copy(sources[item], targets[item].at[me], own_sem.at[item])
        copy.start()
        own.append(copy)
    team = team_copies(TEAM, modes, team_sources, team_targets, *team_sems)
    steps = (
        (1, slot(yh, left), ((5, to_right), (8, to_core))),
        (0, slot(other, x), ((3, to_right), (4, to_left), (9, to_core))),
        (2, slot(yh, right), ((10, to_core),)),
        (4, slot(other, right), ((6, to_left), (11, to_core))),
        (3, slot(other, left), ((12, to_core),)),
        (5, slot(yh, far), ((13, to_core),)),
        (6, slot(other, far), ((14, to_core),)),
    )
    for kind, at, onward in steps:
        for item in items:
            arrived(item, kind)
            for next_kind, device in onward:
                pass_on(item, at, next_kind, device)
    for item in items:
        for kind in range(7, 15):
            arrived(item, kind)
    for copy in own:
        copy.wait()
    for copy in sent:
        copy.wait_send()
    for copy in team:
        copy.wait()


def rank_gather(arrays, items, number, name):
    count = len(arrays)
    return call(
        functools.partial(rank_gather_kernel, count, tuple(mode for _, mode in items)),
        arrays + [array for array, _ in items],
        [jax.ShapeDtypeStruct((16,) + array.shape, array.dtype) for array in arrays]
        + received(TEAM, items),
        [
            pltpu.SemaphoreType.DMA((count, 15)),
            pltpu.SemaphoreType.DMA((count, 15)),
            pltpu.SemaphoreType.DMA((count,)),
        ]
        + team_semaphores(TEAM, items),
        number,
        name,
        40,
    )


def rank_sum_kernel(count, extra, *refs):
    every = count + extra
    sources, given = refs[:count], refs[count:every]
    targets, taken = refs[every : every + count], refs[every + count : 2 * every]
    refs = refs[2 * every :]
    from_core, totals, arrivals = (refs[k * count : (k + 1) * count] for k in range(3))
    send_sem, recv_sem, give_sem, take_sem = refs[3 * count :]
    yh, x, core = lax.axis_index("yh"), lax.axis_index("x"), lax.axis_index("core")
    right, left, far = lax.rem(x + 1, 4), lax.rem(x + 3, 4), lax.rem(x + 2, 4)
    other = 1 - yh
    to_y, to_right, to_left, to_core = {"yh": other}, {"x": right}, {"x": left}, {"core": 1 - core}
    barrier = pltpu.get_barrier_semaphore()
    to_phase = {"phase": 1 - lax.axis_index("phase")}
    for device in (to_y, to_right, to_left, to_core, to_phase):
        greet(barrier, device)
    pl.semaphore_wait(barrier, 5)
    items = range(count)
    sent = []

    def pass_on(item, at, kind, device):
        copy = send(
            totals[item].at[at],
            arrivals[item].at[kind],
            send_sem.at[item, kind],
            recv_sem.at[item, kind],
            device,
        )
        sent.append(copy)

    def arrived(item, kind):
        landed = arrivals[item].at[kind]
        pltpu.make_async_copy(landed, landed, recv_sem.at[item, kind]).wait()
        return arrivals[item][kind].astype(single)

    def slot(y_at, x_at):
        return y_at * 4 + x_at

    for item in items:
        sent.append(
            send(
                sources[item].at[:, 1 - core],
                from_core[item],
                send_sem.at[item, 7],
                recv_sem.at[item, 7],
                to_core,
            )
        )
    swaps = [
        send(given[k], taken[k], give_sem.at[k], take_sem.at[k], to_phase) for k in range(extra)
    ]
    for item in items:
        landed = from_core[item]
        pltpu.make_async_copy(landed, landed, recv_sem.at[item, 7]).wait()

        def add(at):
            value = sources[item][at, core].astype(single) + from_core[item][at].astype(single)
            totals[item][at] = value.astype(brain)

        add(slot(yh, far))
        pass_on(item, slot(yh, far), 0, to_right)
        add(slot(other, far))
        pass_on(item, slot(other, far), 1, to_left)
        add(slot(other, right))
        pass_on(item, slot(other, right), 3, to_right)
        add(slot(yh, left))
        pass_on(item, slot(yh, left), 5, to_left)
        for at in (slot(yh, right), slot(other, left), slot(yh, x), slot(other, x)):
            add(at)
    for item in items:
        at = slot(yh, right)
        totals[item][at] = (totals[item][at].astype(single) + arrived(item, 0)).astype(brain)
        pass_on(item, at, 2, to_right)
        at = slot(other, left)
        totals[item][at] = (totals[item][at].astype(single) + arrived(item, 1)).astype(brain)
        pass_on(item, at, 4, to_left)
    for item in items:
        at = slot(other, x)
        value = totals[item][at].astype(single) + arrived(item, 3)
        totals[item][at] = (value + arrived(item, 4)).astype(brain)
        pass_on(item, at, 6, to_y)
    for item in items:
        value = totals[item][slot(yh, x)].astype(single) + arrived(item, 5)
        value = value + arrived(item, 2)
        targets[item][...] = (value + arrived(item, 6)).astype(targets[item].dtype)
    for copy in sent:
        copy.wait_send()
    for copy in swaps:
        copy.wait()


def rank_sum(arrays, swapped, number, name):
    count, extra = len(arrays), len(swapped)
    arrays = [array.reshape((8, 2) + array.shape[1:]) for array in arrays]
    pieces = [array.shape[2:] for array in arrays]
    scratch = [pltpu.VMEM((8,) + piece, brain) for piece in pieces]
    scratch += [pltpu.VMEM((8,) + piece, brain) for piece in pieces]
    scratch += [pltpu.VMEM((7,) + piece, brain) for piece in pieces]
    scratch += [pltpu.SemaphoreType.DMA((count, 8)), pltpu.SemaphoreType.DMA((count, 8))]
    scratch += [pltpu.SemaphoreType.DMA((extra,)), pltpu.SemaphoreType.DMA((extra,))]
    return call(
        functools.partial(rank_sum_kernel, count, extra),
        arrays + swapped,
        [jax.ShapeDtypeStruct(piece, brain) for piece in pieces]
        + [jax.ShapeDtypeStruct(array.shape, array.dtype) for array in swapped],
        scratch,
        number,
        name,
        45,
    )


def dot(left, right):
    return jnp.dot(left, right, preferred_element_type=single)


def dot_t(left, right):
    return lax.dot_general(left, right, (((1,), (1,)), ((), ())), preferred_element_type=single)


def t_dot(left, right):
    return lax.dot_general(left, right, (((0,), (0,)), ((), ())), preferred_element_type=single)


def exact(spec, left, right):
    return jnp.einsum(
        spec, left, right, precision=lax.Precision.HIGHEST, preferred_element_type=single
    )


def rms_scale(value, gain):
    return value * lax.rsqrt(jnp.mean(value * value, axis=-1, keepdims=True) + eps) * gain


def swiglu(value):
    half = value.shape[-1] // 2
    return jax.nn.silu(value[..., :half]) * value[..., half:]


def shuffle_matrix():
    to = jnp.arange(WIDTH, dtype=jnp.int32)
    origin = to // 12 % 8 * 192 + to // 96 * 12 + to % 12
    return (jnp.arange(WIDTH, dtype=jnp.int32)[:, None] == origin[None, :]).astype(brain)


def shuffle(value, matrix):
    return dot(value, matrix).astype(brain)


def unshuffle(value, matrix):
    high = value.astype(brain)
    lower = (value - high.astype(single)).astype(brain)
    both = dot_t(jnp.concatenate([high, lower], axis=0), matrix)
    return both[: value.shape[0]] + both[value.shape[0] :]


def after(values, first):
    return lax.optimization_barrier((values, first))[0]


def pad_rows(value, rows):
    return jnp.pad(value, [(0, 0)] * (value.ndim - 2) + [(0, rows - value.shape[-2]), (0, 0)])


def pad_to(value, rows, columns):
    return jnp.pad(value, ((0, rows - value.shape[0]), (0, columns - value.shape[1])))


def allowed_pairs(seg):
    position = jnp.arange(SEQ, dtype=jnp.int32)
    return (position[:, None] >= position[None, :]) & (seg[..., :, None] == seg[..., None, :])


def product(left, right, dims, precision=None):
    return lax.dot_general(
        left, right, (dims, ((), ())), precision=precision, preferred_element_type=single
    )


def sharp(left, right, dims):
    return product(left, right, dims, lax.Precision.HIGHEST)


def blunt(left, right, dims):
    return product(left.astype(brain), right.astype(brain), dims)


def mamba_parts(zx_ref, masks_ref, same_ref, taps_ref, heads_ref):
    zx = zx_ref[0]
    conv_in = zx[:, INNER : 2 * INNER + 2 * N]
    taps = taps_ref[...]
    same = same_ref[0]
    moved = [conv_in]
    for k in range(1, KW):
        moved.append(pltpu.roll(conv_in, k, 0) * same[:, k : k + 1])
    conv = taps[KW : KW + 1]
    for k in range(KW):
        conv = conv + taps[KW - 1 - k : KW - k] * moved[k]
    gate = jax.nn.sigmoid(conv)
    active = conv * gate
    heads = heads_ref[...]
    raw = zx[:, 2 * INNER + 2 * N :] + heads[0:1]
    step = jnp.maximum(raw, 0.0) + jnp.log1p(jnp.exp(-jnp.abs(raw)))
    rate = step * heads[1:2]
    rows = lax.broadcasted_iota(jnp.int32, (SEQ, SEQ), 0)
    columns = lax.broadcasted_iota(jnp.int32, (SEQ, SEQ), 1)
    lower = (rows >= columns).astype(single)
    total = sharp(lower, rate, ((1,), (0,)))
    total_t = sharp(rate, lower, ((0,), (1,)))
    unit = (rows == columns).astype(single)
    step_t = sharp(step, unit, ((0,), (1,)))
    values = active[:, :INNER]
    in_state, out_state = active[:, INNER : INNER + N], active[:, INNER + N :]
    meeting = sharp(out_state, in_state, ((1,), (1,)))
    allowed = masks_ref[0]
    decays = []
    results = []
    for h in range(HEADS_HERE):
        fall = jnp.exp(jnp.minimum(total[:, h : h + 1] - total_t[h : h + 1], 0.0)) * allowed
        mixing = fall * meeting * step_t[h : h + 1]
        decays.append((fall, mixing))
        results.append(blunt(mixing, values[:, h * P_SIZE : (h + 1) * P_SIZE], ((1,), (0,))))
    result = jnp.concatenate(results, axis=1) + taps[5:6, :INNER] * values
    z = zx[:, :INNER]
    open_z = jax.nn.sigmoid(z)
    return (
        (zx, taps, same, moved, conv, gate, heads, raw, step, step_t, unit, lower),
        (values, in_state, out_state, meeting, decays, result, z, open_z),
    )


def mamba_forward_kernel(zx_ref, masks_ref, same_ref, taps_ref, heads_ref, part_ref, squares_ref):
    (_, taps, *_), (*_, result, z, open_z) = mamba_parts(
        zx_ref, masks_ref, same_ref, taps_ref, heads_ref
    )
    gated = result * (z * open_z)
    part_ref[0] = (gated * taps[6:7, :INNER]).astype(brain)
    sums = sharp(jnp.ones((8, INNER), single), gated * gated, ((1,), (1,)))
    squares_ref[0] = jnp.concatenate([sums, jnp.zeros((8, 128 - SEQ), single)], axis=1)


def mamba_backward_kernel(
    zx_ref, masks_ref, same_ref, taps_ref, heads_ref, d_yn_ref, scalars_ref, d_zx_ref, yn_ref, sums_ref
):
    first, second = mamba_parts(zx_ref, masks_ref, same_ref, taps_ref, heads_ref)
    (zx, taps, same, moved, conv, gate, heads, raw, step, step_t, unit, lower) = first
    (values, in_state, out_state, meeting, decays, result, z, open_z) = second
    scalars = sharp(unit, scalars_ref[0][:, :SEQ], ((1,), (1,)))
    inverse, along = scalars[:, 0:1], scalars[:, 1:2]
    gain, skip = taps[6:7, :INNER], taps[5:6, :INNER]
    d_yn = d_yn_ref[0]
    shut = z * open_z
    gated = result * shut
    scaled = gated * inverse
    yn_ref[0] = (scaled * gain).astype(brain)
    d_gain = jnp.sum(d_yn * scaled, axis=0, keepdims=True)
    d_gated = inverse * gain * d_yn - gated * along
    d_z = d_gated * result * (open_z * (1.0 + z * (1.0 - open_z)))
    d_result = d_gated * shut
    d_skip = jnp.sum(d_result * values, axis=0, keepdims=True)
    lanes = lax.broadcasted_iota(jnp.int32, (1, 128), 1)
    rows = lax.broadcasted_iota(jnp.int32, (128, 1), 0)
    d_meeting = jnp.zeros((SEQ, SEQ), single)
    by_row = jnp.zeros((SEQ, 128), single)
    by_column = jnp.zeros((128, SEQ), single)
    d_step_t = jnp.zeros((128, SEQ), single)
    d_values = []
    for h in range(HEADS_HERE):
        fall, mixing = decays[h]
        own = slice(h * P_SIZE, (h + 1) * P_SIZE)
        d_mixing = blunt(d_result[:, own], values[:, own], ((1,), (1,)))
        d_values.append(blunt(mixing, d_result[:, own], ((0,), (0,))))
        spread = d_mixing * fall
        d_meeting = d_meeting + spread * step_t[h : h + 1]
        spread = spread * meeting
        moving = spread * step_t[h : h + 1]
        by_row = by_row + jnp.sum(moving, axis=1, keepdims=True) * (lanes == h).astype(single)
        at = (rows == h).astype(single)
        by_column = by_column + at * jnp.sum(moving, axis=0, keepdims=True)
        d_step_t = d_step_t + at * jnp.sum(spread, axis=0, keepdims=True)
    d_total = by_row - sharp(unit, by_column, ((1,), (1,)))
    d_rate = sharp(lower, d_total, ((0,), (0,)))
    d_step = sharp(unit, d_step_t, ((1,), (1,))) + d_rate * heads[1:2]
    d_raw = d_step * jax.nn.sigmoid(raw)
    d_decay = jnp.sum(d_rate * step, axis=0, keepdims=True) * heads[1:2]
    d_active = jnp.concatenate(
        [
            jnp.concatenate(d_values, axis=1) + skip * d_result,
            sharp(d_meeting, out_state, ((0,), (0,))),
            sharp(d_meeting, in_state, ((1,), (0,))),
        ],
        axis=1,
    )
    d_conv = d_active * (gate * (1.0 + conv * (1.0 - gate)))
    d_taps = [jnp.sum(d_conv * moved[KW - 1 - k], axis=0, keepdims=True) for k in range(KW)]
    d_in = taps[KW - 1 : KW] * d_conv
    for k in range(1, KW):
        d_in = d_in + pltpu.roll(
            taps[KW - 1 - k : KW - k] * (d_conv * same[:, k : k + 1]), SEQ - k, 0
        )
    d_zx_ref[0] = jnp.concatenate([d_z, d_in, d_raw], axis=1).astype(brain)
    wide = INNER + 2 * N

    def widen(value):
        return jnp.concatenate(
            [value, jnp.zeros((1, wide - value.shape[1]), single)], axis=1
        )

    sums = jnp.concatenate(
        d_taps
        + [jnp.sum(d_conv, axis=0, keepdims=True), widen(d_skip), widen(d_gain)]
        + [widen(jnp.sum(d_raw, axis=0, keepdims=True)), widen(d_decay)]
        + [jnp.zeros((7, wide), single)],
        axis=0,
    )

    @pl.when(pl.program_id(0) == 0)
    def _():
        sums_ref[...] = jnp.zeros_like(sums_ref)

    sums_ref[...] += sums


def by_sequence(kernel, arrays, fixed, shapes, total_shapes, name):
    def whole(shape):
        return pl.BlockSpec(shape, lambda n: (0,) * len(shape))

    def one(shape):
        return pl.BlockSpec((1,) + shape[1:], lambda n: (n,) + (0,) * (len(shape) - 1))

    return pl.pallas_call(
        kernel,
        grid=(PARTS,),
        out_shape=shapes + total_shapes,
        in_specs=[
            whole(array.shape) if place in fixed else one(array.shape)
            for place, array in enumerate(arrays)
        ],
        out_specs=[one(s.shape) for s in shapes] + [whole(s.shape) for s in total_shapes],
        compiler_params=pltpu.CompilerParams(vmem_limit_bytes=32 << 20),
        name=name,
    )(*arrays)


def attend_scores(queries, keys, seg):
    scores = exact("nird,njd->nrij", queries, keys) * HEAD_SIZE ** (-0.5)
    scores = jnp.where(allowed_pairs(seg)[:, None], scores, -1e30)
    return jax.nn.softmax(scores, axis=-1)


def attend_mix(probs, values):
    return exact("nrij,njd->nird", probs, values)


def per_device(
    block_input,
    cotangent,
    segments,
    routes,
    in_proj,
    conv_taps,
    conv_bias,
    step_bias,
    decay_log,
    skip_weight,
    norm_gain,
    out_proj,
    query_proj,
    key_value_projection,
    attn_out_proj,
    norm_gains,
    router,
    shared_in,
    shared_out,
    experts_in,
    experts_out,
):
    phase = lax.axis_index("phase")
    first_phase = phase == 0
    zl = lax.axis_index("zl")
    team = phase * 4 + lax.axis_index("zh") * 2 + zl

    def mine(value):
        return lax.dynamic_index_in_dim(value, phase, 0, keepdims=False)

    start = mine(block_input)
    cot = mine(cotangent)
    seg = mine(segments)
    route_rows = mine(routes)

    both_ways = [(0, 1), (1, 0)]
    w_first, w_second = experts_in[0, 0], experts_out[0, 0]

    z_piece = in_proj[:, :DI].reshape(12, PARTS, INNER).transpose(1, 0, 2)
    x_piece = in_proj[:, DI : 2 * DI].reshape(12, PARTS, INNER).transpose(1, 0, 2)
    state_piece = jnp.broadcast_to(in_proj[None, :, 2 * DI : 2 * DI + 2 * N], (PARTS, 12, 2 * N))
    step_piece = in_proj[:, 2 * DI + 2 * N :].reshape(12, PARTS, HEADS_HERE).transpose(1, 0, 2)
    step_piece = jnp.pad(step_piece, ((0, 0), (0, 0), (0, 128 - HEADS_HERE)))
    q_piece = query_proj.reshape(12, 4, 384).transpose(1, 0, 2)
    kv_piece = key_value_projection.reshape(12, 2, 4, 128).transpose(2, 0, 1, 3).reshape(4, 12, 256)
    qkv_piece = jnp.repeat(jnp.concatenate([q_piece, kv_piece], axis=2), 2, axis=0)
    in_piece = pad_rows(jnp.concatenate([z_piece, x_piece, state_piece, step_piece], axis=2), 16)
    qkv_piece = pad_rows(qkv_piece, 16)
    sin_piece = shared_in[0].reshape(24, 2, 4, 256).transpose(2, 0, 1, 3).reshape(4, 24, 512)
    sin_piece = pad_rows(jnp.concatenate([sin_piece, sin_piece], axis=0), 32)
    sout_piece = jnp.broadcast_to(shared_out, (2, 16, WIDTH))
    attn_piece = jnp.broadcast_to(pad_rows(attn_out_proj, 16)[None], (2, 16, WIDTH))
    mixing = shuffle_matrix()
    rest = jnp.concatenate(
        [conv_taps.reshape(-1), conv_bias, norm_gain, norm_gains[0].reshape(-1)]
    )
    rest = jnp.pad(rest, (0, 512 - rest.shape[0])).reshape(4, 128)
    small = jnp.concatenate([router[0].reshape(12, 128), rest], axis=0)
    seg_piece = pad_to(seg, 8, 128)
    in_got, sin_got, sout_got, small_got, seg_got = exchange(
        [
            (in_piece, "swap"),
            (sin_piece, "swap"),
            (sout_piece, "phase"),
            (small, "gather"),
            (seg_piece, "gather"),
        ],
        TEAM,
        0,
        "team_start",
    )
    seg_all = seg_got[:, 0, :SEQ]
    sin_got = sin_got[:, :24].reshape(2, 96, 512)
    w_in, small_all, w_out, sin_all, sout_all, start_all, qkv_got, attn_got = rank_gather(
        [
            in_got[:, :12].reshape(96, IN_COLS),
            small_got.reshape(128, 128),
            pad_rows(out_proj, 32),
            sin_got[0],
            sout_got[0],
        ],
        [(shuffle(start, mixing), "gather"), (qkv_piece, "swap"), (attn_piece, "zl")],
        1,
        "rank_weights",
    )
    w_in = w_in.reshape(WIDTH, IN_COLS)
    w_out = w_out[:, :24].reshape(INNER, WIDTH)
    later_wide = jnp.concatenate([qkv_got[:, :12].reshape(96, QKV_COLS), sin_got[1]], axis=1)
    later_tall = jnp.concatenate([attn_got[:, :12].reshape(24, WIDTH), sout_got[1]], axis=0)
    w_first_far = lax.ppermute(w_first, "phase", both_ways)
    w_second_far = lax.ppermute(w_second, "phase", both_ways)
    later_wide = lax.all_gather(later_wide, RANK, axis=0)
    later_tall = lax.all_gather(later_tall, RANK, axis=0)
    w_qkv = later_wide[:, :, :QKV_COLS].reshape(WIDTH, QKV_COLS)
    w_attn = later_tall[:, :24].reshape(16, 2, 12, WIDTH).transpose(1, 0, 2, 3)
    w_attn = w_attn.reshape(384, WIDTH)

    def hidden_in(value):
        return value.reshape(16, 4, 24, 512).transpose(1, 0, 2, 3).reshape(WIDTH, 512)

    sin_full = (hidden_in(sin_all), hidden_in(later_wide[:, :, QKV_COLS:]))
    sout_full = (sout_all.reshape(256, WIDTH), later_tall[:, 24:].reshape(256, WIDTH))
    small_all = small_all.reshape(16, 2, 4, 16, 128)
    router_full = small_all[:, :, :, :12].reshape(16, 2, 4, 24, EXPERTS).transpose(1, 2, 0, 3, 4)
    router_full = router_full.reshape(2, WIDTH, EXPERTS)
    rest_all = small_all[:, :, :, 12:].reshape(16, 2, 4, 512)
    conv_full = rest_all[..., :130].reshape(16, 2, 4, 5, 26).transpose(3, 1, 2, 0, 4)
    conv_full = conv_full.reshape(5, CONVW).astype(single)
    gain_here = rest_all[..., 130:154].reshape(16, 8, 24)
    gain_here = lax.dynamic_index_in_dim(gain_here, team, 1, keepdims=False)
    gain_here = gain_here.reshape(INNER).astype(single)
    gains = rest_all[..., 154:202].reshape(16, 2, 4, 2, 24).transpose(1, 3, 2, 0, 4)
    gains = gains.reshape(2, 2, WIDTH).astype(single)
    conv_here = jnp.concatenate(
        [lax.dynamic_slice_in_dim(conv_full[:, :DI], team * INNER, INNER, 1), conv_full[:, DI:]],
        axis=1,
    )

    def heads_of(value):
        return lax.dynamic_slice_in_dim(value, team * HEADS_HERE, HEADS_HERE, 0)

    skip_wide = jnp.repeat(heads_of(skip_weight), P_SIZE)
    columns = jnp.stack([jnp.pad(skip_wide, (0, 2 * N)), jnp.pad(gain_here, (0, 2 * N))])
    taps_here = jnp.concatenate([conv_here, columns, jnp.zeros((1, INNER + 2 * N), single)], axis=0)
    heads_here = jnp.stack([heads_of(step_bias), -jnp.exp(heads_of(decay_log))])
    heads_here = pad_to(heads_here, 8, 128)
    allowed_all = allowed_pairs(seg_all).astype(single)
    same_all = [
        jnp.pad(seg_all[:, k:] == seg_all[:, : SEQ - k], ((0, 0), (k, 0))) for k in range(KW)
    ]
    same_all = jnp.pad(jnp.stack(same_all, axis=2).astype(single), ((0, 0), (0, 0), (0, 128 - KW)))

    expert_ids = jnp.arange(EXPERTS, dtype=jnp.int32)
    named = jnp.any(route_rows[:, :, None] == expert_ids, axis=1)
    position = jnp.arange(SEQ, dtype=jnp.int32)
    earlier = (position[:, None] > position[None, :]).astype(brain)
    slot = dot(earlier, named.astype(brain))
    slot = jnp.where(named, slot, -1.0).astype(brain)
    cell = jnp.arange(EXPERTS * SLOTS, dtype=jnp.int32)
    spread = (cell[None, :] // SLOTS == expert_ids[:, None]).astype(brain)
    taken = dot(slot, spread) == (cell % SLOTS).astype(single)
    taken_b = taken.astype(brain)

    def of_block(s):
        own = phase == s
        return (
            jnp.where(own, w_first, w_first_far),
            jnp.where(own, w_second, w_second_far),
        )

    def moe_open(s, hidden):
        normed = rms_scale(hidden, gains[s, 1]).astype(brain)
        logits = dot(normed, router_full[s])
        top = jnp.max(jnp.where(named, logits, -jnp.inf), axis=1, keepdims=True)
        weight = jnp.where(named, jnp.exp(logits - top), 0.0)
        gates = weight / jnp.sum(weight, axis=1, keepdims=True)
        gates_wide = jnp.where(taken, exact("ie,ec->ic", gates, spread.astype(single)), 0.0)
        return normed, gates, gates_wide, t_dot(taken_b, normed).astype(brain)

    def moe_experts(weights, rows_in):
        both = dot(rows_in, weights[0])
        hid = swiglu(both).astype(brain)
        return both, hid, dot(hid, weights[1]).astype(brain)

    def moe_shared(s, normed_all):
        both = dot(normed_all, sin_full[s])
        hid = swiglu(both).astype(brain)
        part = dot(hid, sout_full[s]).astype(brain)
        return both, hid, part.reshape(4, SEQ, WIDTH)

    def moe_join(hidden, gates_wide, back, shared_got):
        high = gates_wide.astype(brain)
        lower = (gates_wide - high.astype(single)).astype(brain)
        moe = dot(high, back) + dot(lower, back)
        return (hidden + moe + jnp.sum(shared_got.astype(single), axis=0)).astype(brain)

    def back_open(d_out, gates_wide):
        gate_cell = jnp.sum(gates_wide, axis=0)
        return (t_dot(taken_b, d_out) * gate_cell[:, None]).astype(brain)

    def back_experts(weights, d_answer, both):
        d_hid = dot_t(d_answer, weights[1])
        d_both = jax.vjp(swiglu, both)[1](d_hid)[0].astype(brain)
        return d_both, dot_t(d_both, weights[0]).astype(brain)

    def back_shared(s, d_out_all, normed_all, both, hid):
        d_hid = dot_t(d_out_all, sout_full[s])
        d_sout = t_dot(hid, d_out_all)
        d_both = jax.vjp(swiglu, both)[1](d_hid)[0].astype(brain)
        d_sin = t_dot(normed_all, d_both)
        d_part = dot_t(d_both, sin_full[s]).astype(brain).reshape(4, SEQ, WIDTH)
        return d_sin, d_sout, d_part

    def back_join(s, d_out, hidden, normed, gates, back, returned, d_shared_got):
        d_cells = jnp.where(taken, dot_t(d_out, back), 0.0)
        d_gates = exact("ic,ec->ie", d_cells, spread.astype(single))
        d_logits = gates * (d_gates - jnp.sum(gates * d_gates, axis=1, keepdims=True))
        d_normed = exact("ie,we->iw", d_logits, router_full[s].astype(single))
        d_router = exact("iw,ie->we", normed.astype(single), d_logits)
        d_normed = d_normed + dot(taken_b, returned) + jnp.sum(d_shared_got.astype(single), axis=0)
        d_hidden, d_gain = jax.vjp(rms_scale, hidden, gains[s, 1])[1](d_normed)
        return d_hidden + d_out.astype(single), d_gain, d_router

    def shared_in_parts(value):
        return value.astype(brain).reshape(4, 16, 24, 512).transpose(1, 0, 2, 3).reshape(16, 96, 512)

    u0 = start.astype(single)
    shuffled_gain = shuffle(gains[0, 0][None].astype(brain), mixing)[0].astype(single)
    n1_all = rms_scale(start_all.astype(single), shuffled_gain).astype(brain)
    n1_all = n1_all.reshape(PARTS * SEQ, WIDTH)
    zx = dot(n1_all, w_in).reshape(PARTS, SEQ, IN_COLS)

    core_inputs = [zx, allowed_all, same_all, taps_here, heads_here]
    part, squares = by_sequence(
        mamba_forward_kernel,
        core_inputs,
        (3, 4),
        [
            jax.ShapeDtypeStruct((PARTS, SEQ, INNER), brain),
            jax.ShapeDtypeStruct((PARTS, 8, 128), single),
        ],
        [],
        "mamba_forward",
    )
    part = dot(part.reshape(PARTS * SEQ, INNER), w_out)
    part = part.astype(brain).reshape(PARTS, SEQ, WIDTH)
    part = after(part, (w_first_far, w_second_far))
    part_got, squares_got = exchange([(part, "swap"), (squares, "swap")], TEAM, 2, "team_mixed_0")
    mean_square = jnp.sum(squares_got[:, 0, :SEQ], axis=0) / DI
    inverse = lax.rsqrt(mean_square + eps)
    mixed0 = jnp.sum(part_got.astype(single), axis=0) * inverse[:, None]
    hidden0 = u0 + mixed0
    normed0, gates0, gates_wide0, rows_out0 = moe_open(0, hidden0)
    rows_in0, normed_all0 = expert_exchange([rows_out0], [(normed0, "gather")], 3, "spread_0")
    normed_all0 = normed_all0.reshape(4 * SEQ, WIDTH)
    weights0 = of_block(0)
    sboth0, shid0, shared_part0 = moe_shared(0, normed_all0)
    both0, hid0, answer0 = moe_experts(weights0, rows_in0)
    back0, shared_got0 = expert_exchange([answer0], [(shared_part0, "swap")], 4, "collect_0")
    out0 = moe_join(hidden0, gates_wide0, back0, shared_got0)

    u1 = out0.astype(single)
    n1 = rms_scale(u1, gains[1, 0]).astype(brain)
    (n1_half,) = exchange([(shuffle(n1, mixing), "gather")], HALF, 5, "half_n1")
    n1_half = n1_half.reshape(4 * SEQ, WIDTH)
    seg_half = lax.dynamic_index_in_dim(seg_all.reshape(4, 2, SEQ), zl, 1, keepdims=False)
    qkv = dot(n1_half, w_qkv).astype(brain).astype(single).reshape(4, SEQ, QKV_COLS)
    queries = qkv[..., :384].reshape(4, SEQ, 3, HEAD_SIZE)
    keys, values = qkv[..., 384:512], qkv[..., 512:]
    probs, score_pull = jax.vjp(lambda q, k: attend_scores(q, k, seg_half), queries, keys)
    heads, mix_pull = jax.vjp(attend_mix, probs.astype(brain).astype(single), values)
    heads = heads.astype(brain).reshape(4 * SEQ, 384)
    part1 = dot(heads, w_attn).astype(brain).reshape(4, SEQ, WIDTH)
    (part1_got,) = exchange([(part1, "swap")], HALF, 6, "half_mixed")
    mixed1 = jnp.sum(part1_got.astype(single), axis=0)
    hidden1 = u1 + mixed1

    normed1, gates1, gates_wide1, rows_out1 = moe_open(1, hidden1)
    rows_in1, d_answer1, normed_all1, cot_all = expert_exchange(
        [rows_out1, back_open(cot, gates_wide1)],
        [(normed1, "gather"), (cot, "gather")],
        7,
        "spread_1",
    )
    normed_all1 = normed_all1.reshape(4 * SEQ, WIDTH)
    cot_all = cot_all.reshape(4 * SEQ, WIDTH)
    weights1 = of_block(1)
    sboth1, shid1, shared_part1 = moe_shared(1, normed_all1)
    d_sin1, d_sout1, d_shared1 = back_shared(1, cot_all, normed_all1, sboth1, shid1)
    both1, hid1, answer1 = moe_experts(weights1, rows_in1)
    d_both1, d_rows1 = back_experts(weights1, d_answer1, both1)
    back1, returned1, shared_got1, d_shared_got1 = expert_exchange(
        [answer1, d_rows1], [(shared_part1, "swap"), (d_shared1, "swap")], 8, "collect_1"
    )
    out1 = moe_join(hidden1, gates_wide1, back1, shared_got1)

    d_hid1, d_gain11, d_router1 = back_join(
        1, cot, hidden1, normed1, gates1, back1, returned1, d_shared_got1
    )
    (d_mixed1,) = exchange([(d_hid1.astype(brain), "gather")], HALF, 11, "half_dmixed")
    d_mixed1 = d_mixed1.reshape(4 * SEQ, WIDTH)
    d_heads = dot_t(d_mixed1, w_attn).reshape(4, SEQ, 3, HEAD_SIZE)
    d_attn = t_dot(heads, d_mixed1)
    d_probs, d_values = mix_pull(d_heads)
    d_queries, d_keys = score_pull(d_probs)
    d_qkv = jnp.concatenate([d_queries.reshape(4, SEQ, 384), d_keys, d_values], axis=2)
    d_qkv = d_qkv.astype(brain).reshape(4 * SEQ, QKV_COLS)
    d_w_qkv = t_dot(n1_half, d_qkv)
    d_n1_part = dot_t(d_qkv, w_qkv).astype(brain).reshape(4, SEQ, WIDTH)
    grads_wide = jnp.concatenate(
        [d_w_qkv.astype(brain).reshape(16, 96, QKV_COLS), shared_in_parts(d_sin1)], axis=2
    )
    attn_part = d_attn.astype(brain).reshape(2, 16, 12, WIDTH).transpose(1, 0, 2, 3)
    grads_tall = jnp.concatenate(
        [attn_part.reshape(16, 24, WIDTH), d_sout1.astype(brain).reshape(16, 16, WIDTH)], axis=1
    )
    grads_tall = jnp.pad(grads_tall.reshape(16, 40 * WIDTH), ((0, 0), (0, 54 * IN_COLS - 40 * WIDTH)))
    grads_later = jnp.concatenate([grads_wide, grads_tall.reshape(16, 54, IN_COLS)], axis=1)
    d_n1_part, grads_later = lax.optimization_barrier((d_n1_part, grads_later))
    grads_later = lax.psum_scatter(grads_later, RANK, scatter_dimension=0, tiled=True)[0]
    (d_n1_got,) = exchange([(d_n1_part, "swap")], HALF, 12, "half_dn1")
    d_n1 = unshuffle(jnp.sum(d_n1_got.astype(single), axis=0), mixing)
    d_u1, d_gain10 = jax.vjp(rms_scale, u1, gains[1, 0])[1](d_n1)
    d_u1 = (d_u1 + d_hid1).astype(brain)

    d_answer0, d_out0_all = expert_exchange(
        [back_open(d_u1, gates_wide0)], [(d_u1, "gather")], 13, "spread_back_0"
    )
    d_out0_all = d_out0_all.reshape(4 * SEQ, WIDTH)
    d_sin0, d_sout0, d_shared0 = back_shared(0, d_out0_all, normed_all0, sboth0, shid0)
    d_both0, d_rows0 = back_experts(weights0, d_answer0, both0)
    expert0 = (rows_in0, d_both0, hid0, d_answer0)
    expert1 = (rows_in1, d_both1, hid1, d_answer1)
    give_rows, give_both, give_hid, give_answer = (
        jnp.where(first_phase, b, a) for a, b in zip(expert0, expert1)
    )
    give_first = t_dot(give_rows, give_both).astype(brain)
    give_second = t_dot(give_hid, give_answer).astype(brain)
    d_rows0, give_first, give_second = lax.optimization_barrier((d_rows0, give_first, give_second))
    far_first = lax.ppermute(give_first, "phase", both_ways)
    far_second = lax.ppermute(give_second, "phase", both_ways)
    returned0, d_shared_got0 = expert_exchange(
        [d_rows0], [(d_shared0, "swap")], 14, "collect_back_0"
    )
    d_hid0, d_gain01, d_router0 = back_join(
        0, d_u1, hidden0, normed0, gates0, back0, returned0, d_shared_got0
    )
    d_mixed0 = d_hid0.astype(brain)
    along = jnp.sum(d_mixed0.astype(single) * mixed0, axis=1)
    scalars = jnp.stack([inverse, inverse * inverse * along / DI])
    d_mixed0, scalars_all = exchange(
        [(d_mixed0, "gather"), (pad_to(scalars, 8, 128), "gather")], TEAM, 15, "team_dmixed"
    )
    d_mixed0 = d_mixed0.reshape(PARTS * SEQ, WIDTH)
    d_yn = dot_t(d_mixed0, w_out).reshape(PARTS, SEQ, INNER)
    d_zx, yn, core_sums = by_sequence(
        mamba_backward_kernel,
        core_inputs + [d_yn, scalars_all],
        (3, 4),
        [
            jax.ShapeDtypeStruct((PARTS, SEQ, IN_COLS), brain),
            jax.ShapeDtypeStruct((PARTS, SEQ, INNER), brain),
        ],
        [jax.ShapeDtypeStruct((16, INNER + 2 * N), single)],
        "mamba_backward",
    )
    d_w_out = t_dot(yn.reshape(PARTS * SEQ, INNER), d_mixed0)
    d_zx = d_zx.reshape(PARTS * SEQ, IN_COLS)
    d_norm_gain = core_sums[6, :INNER]
    d_skip = jnp.sum(core_sums[5, :INNER].reshape(HEADS_HERE, P_SIZE), axis=1)
    d_step, d_decay = core_sums[7, :HEADS_HERE], core_sums[8, :HEADS_HERE]
    d_w_in = t_dot(n1_all, d_zx)
    d_n1_part0 = dot_t(d_zx, w_in).astype(brain).reshape(PARTS, SEQ, WIDTH)
    d_n1_part0, grads_later = lax.optimization_barrier((d_n1_part0, grads_later))
    (d_n1_got0,) = exchange([(d_n1_part0, "swap")], TEAM, 16, "team_dn1")
    d_n1_0 = unshuffle(jnp.sum(d_n1_got0.astype(single), axis=0), mixing)
    d_u0, d_gain00 = jax.vjp(rms_scale, u0, gains[0, 0])[1](d_n1_0)
    d_u0 = d_u0 + d_hid0

    def keep_and_give(block0, block1):
        return jnp.where(first_phase, block0, block1), jnp.where(first_phase, block1, block0)

    def by_block(kept, got):
        return jnp.where(first_phase, jnp.stack([kept, got]), jnp.stack([got, kept]))[None]

    keep_out, give_out = keep_and_give(out0, out1)
    keep_grad, give_grad = keep_and_give(d_u0, d_u1.astype(single))

    qkv_part = grads_later[:96, :QKV_COLS].reshape(PARTS, 12, QKV_COLS)
    sin_part1 = grads_later[:96, QKV_COLS:].reshape(4, 24, 512)
    grads_tall = grads_later[96:].reshape(54 * IN_COLS)[: 40 * WIDTH].reshape(40, WIDTH)
    attn_part, sout_part1 = grads_tall[:24].reshape(2, 12, WIDTH), grads_tall[24:]

    conv_grads = core_sums[: KW + 1]
    conv_all = jnp.concatenate(
        [
            lax.dynamic_update_slice_in_dim(
                jnp.zeros((KW + 1, DI), single), conv_grads[:, :INNER], team * INNER, 1
            ),
            conv_grads[:, INNER:],
        ],
        axis=1,
    )
    conv_all = conv_all.reshape(5, 8, 16, 26).transpose(2, 1, 0, 3).reshape(16, 8, 130)
    head_all = lax.dynamic_update_slice_in_dim(
        jnp.zeros((3, H), single), jnp.stack([d_step, d_decay, d_skip]), team * HEADS_HERE, 1
    )
    head_all = jnp.broadcast_to(head_all.reshape(1, 1, 3 * H), (16, 8, 3 * H))
    gain_all = lax.dynamic_update_slice_in_dim(
        jnp.zeros((16, 8, 24), single), d_norm_gain.reshape(16, 1, 24), team, 1
    )
    d_gains = jnp.stack([jnp.stack([d_gain00, d_gain01]), jnp.stack([d_gain10, d_gain11])])
    d_gains = d_gains.reshape(2, 2, 4, 16, 24).transpose(3, 0, 2, 1, 4).reshape(16, 8, 48)
    d_router = jnp.stack([d_router0, d_router1]).reshape(2, 4, 16, 24 * EXPERTS)
    d_router = d_router.transpose(2, 0, 1, 3).reshape(16, 8, 24 * EXPERTS)
    small_grads = jnp.concatenate([d_router, conv_all, gain_all, d_gains, head_all], axis=2)
    small_grads = jnp.pad(small_grads, ((0, 0), (0, 0), (0, 2048 - small_grads.shape[2])))
    small_grads = small_grads.astype(brain).reshape(16, 128, 128)
    d_outs = jnp.concatenate(
        [
            d_w_out.astype(brain).reshape(16, 24, WIDTH),
            d_sout0.astype(brain).reshape(16, 16, WIDTH),
            jnp.zeros((16, 8, WIDTH), brain),
        ],
        axis=1,
    )
    main_part, outs_part, sin_part0, small_part, got_out, got_grad = rank_sum(
        [
            d_w_in.astype(brain).reshape(16, 96, IN_COLS),
            d_outs,
            shared_in_parts(d_sin0),
            small_grads,
        ],
        [give_out, give_grad],
        17,
        "rank_grads",
    )
    phase_outputs = by_block(keep_out, got_out)
    input_grads = by_block(keep_grad, got_grad)
    main_part = main_part.reshape(PARTS, 12, IN_COLS)
    out_proj_grad, sout_part0 = outs_part[:24], outs_part[24:40]
    sin_part0 = sin_part0.reshape(4, 24, 512)

    rows_kept, d_both_kept, hid_kept, d_answer_kept = (
        jnp.where(first_phase, a, b) for a, b in zip(expert0, expert1)
    )
    far_first, far_second = after((far_first, far_second), main_part)
    experts_in_grad = t_dot(rows_kept, d_both_kept) + far_first.astype(single)
    experts_out_grad = t_dot(hid_kept, d_answer_kept) + far_second.astype(single)

    main_end, qkv_end, sin_end, sout_end, attn_end, small_end = exchange(
        [
            (pad_rows(main_part, 16), "swap"),
            (pad_rows(qkv_part, 16), "swap"),
            (pad_rows(jnp.concatenate([sin_part0, sin_part1], axis=0), 32), "swap"),
            (jnp.stack([sout_part0, sout_part1]), "phase"),
            (pad_rows(attn_part, 16), "zl"),
            (small_part.reshape(PARTS, 16, 128), "swap"),
        ],
        TEAM,
        18,
        "team_end",
    )
    rows_end = main_end[:, :12].astype(single)

    def side_by_side(value):
        return value.transpose(1, 0, 2).reshape(value.shape[1], -1)

    in_proj_grad = jnp.concatenate(
        [
            side_by_side(rows_end[:, :, :INNER]),
            side_by_side(rows_end[:, :, INNER : 2 * INNER]),
            jnp.sum(rows_end[:, :, 2 * INNER : 2 * INNER + 2 * N], axis=0),
            side_by_side(
                rows_end[:, :, 2 * INNER + 2 * N : 2 * INNER + 2 * N + HEADS_HERE]
            ),
        ],
        axis=1,
    )
    small_end = jnp.sum(small_end.astype(single), axis=0).reshape(2048)
    router_grad = small_end[: 24 * EXPERTS].reshape(1, 24, EXPERTS)
    at = 24 * EXPERTS
    conv_end = small_end[at : at + 130].reshape(5, 26)
    at += 130
    norm_gain_grad = small_end[at : at + 24]
    at += 24
    norm_gains_grad = small_end[at : at + 48].reshape(1, 2, 24)
    at += 48
    heads_end = small_end[at : at + 3 * H].reshape(3, H)
    qkv_end = qkv_end[:, :12].astype(single).reshape(4, 2, 12, QKV_COLS)
    qkv_end = jnp.sum(qkv_end, axis=1)
    query_grad = side_by_side(qkv_end[:, :, :384])
    kv_grad = qkv_end[:, :, 384:].reshape(4, 12, 2, 128).transpose(1, 2, 0, 3).reshape(12, 1024)
    sin_end = jnp.sum(sin_end[:, :24].astype(single).reshape(2, 4, 24, 2, 256), axis=0)
    shared_in_grad = sin_end.transpose(1, 2, 0, 3).reshape(1, 24, 2048)
    shared_out_grad = jnp.sum(sout_end.astype(single), axis=0)[None]
    attn_out_grad = jnp.sum(attn_end[:, :12].astype(single), axis=0)

    return (
        phase_outputs,
        input_grads,
        in_proj_grad,
        conv_end[:KW],
        conv_end[KW],
        heads_end[0],
        heads_end[1],
        heads_end[2],
        norm_gain_grad,
        out_proj_grad.astype(single),
        query_grad,
        kv_grad,
        attn_out_grad,
        norm_gains_grad,
        router_grad,
        shared_in_grad,
        shared_out_grad,
        experts_in_grad[None, None],
        experts_out_grad[None, None],
    )


def solution(mesh):
    fine = Mesh(mesh.devices.reshape(tuple(SIZES.values())), ALL)
    in_specs = (
        P(None, DP, None),
        P(None, DP, None),
        P(None, DP, None),
        P(None, DP, None),
        P(ALL, None),
        P(None, ALL),
        P(ALL),
        P(),
        P(),
        P(),
        P(ALL),
        P(ALL, None),
        P(ALL, None),
        P(ALL, None),
        P(ALL, None),
        P("phase", None, DP),
        P("phase", DP, None),
        P("phase", DP, None),
        P("phase", DP, None),
        P("phase", DP, None, None),
        P("phase", DP, None, None),
    )
    out_specs = (
        P("phase", None, DP, None),
        P("phase", None, DP, None),
        P(ALL, None),
        P(None, ALL),
        P(ALL),
        P(),
        P(),
        P(),
        P(ALL),
        P(ALL, None),
        P(ALL, None),
        P(ALL, None),
        P(ALL, None),
        P("phase", None, DP),
        P("phase", DP, None),
        P("phase", DP, None),
        P("phase", DP, None),
        P("phase", DP, None, None),
        P("phase", DP, None, None),
    )
    return jax.shard_map(
        per_device, mesh=fine, in_specs=in_specs, out_specs=out_specs, check_vma=False
    )
```

```python
import functools

import jax
import jax.numpy as jnp
from jax import lax
from jax.experimental import pallas as pl
from jax.experimental.pallas import tpu as pltpu
from jax.sharding import Mesh
from jax.sharding import PartitionSpec as P

H = 48
P_SIZE = 64
N = 128
KW = 4
QUERY_HEADS = 12
KEY_VALUE_HEADS = 4
HEAD_SIZE = 128
DI = 3072
CONVW = 3328
WIDTH = 1536
SEQ = 64
EXPERTS = 64
SLOTS = 8
PARTS = 8
HEADS_HERE = H // PARTS
INNER = DI // PARTS
IN_COLS = 1152
QKV_COLS = 640

SIZES = {"phase": 2, "zh": 2, "zl": 2, "yh": 2, "x": 4, "core": 2}
TEAM = ("phase", "zh", "zl")
HALF = ("phase", "zh")
QUAD = ("zh", "zl")
RANK = ("yh", "x", "core")
DP = ("zh", "zl", "yh", "x", "core")
ALL = ("phase", "zh", "zl", "yh", "x", "core")
MESH_ID = pl.DeviceIdType.MESH

eps = 1e-05
single = jnp.float32
brain = jnp.bfloat16


def place_of(axes, index):
    out = {}
    for name in reversed(axes):
        out[name] = lax.rem(index, SIZES[name])
        index = lax.div(index, SIZES[name])
    return out


def size_of(axes):
    total = 1
    for name in axes:
        total *= SIZES[name]
    return total


def my_place(axes):
    me = jnp.int32(0)
    for name in axes:
        me = me * SIZES[name] + lax.axis_index(name)
    return me


def greet(barrier, device):
    pl.semaphore_signal(barrier, inc=1, device_id=device, device_id_type=MESH_ID)


def send(source, target, send_sem, recv_sem, device):
    copy = pltpu.make_async_remote_copy(
        src_ref=source,
        dst_ref=target,
        send_sem=send_sem,
        recv_sem=recv_sem,
        device_id=device,
        device_id_type=MESH_ID,
    )
    copy.start()
    return copy


def team_copies(axes, modes, sources, targets, send_sem, recv_sem, own_sem):
    n = size_of(axes)
    me = my_place(axes)
    copies = []
    for k in range(1, n):
        peer = lax.rem(me + k, n)
        device = place_of(axes, peer)
        for item, mode in enumerate(modes):
            if mode in SIZES:
                continue
            source = sources[item].at[peer] if mode == "swap" else sources[item]
            copies.append(
                send(
                    source,
                    targets[item].at[me],
                    send_sem.at[item, k],
                    recv_sem.at[item, k],
                    device,
                )
            )
    for item, mode in enumerate(modes):
        slot = me
        source = sources[item] if mode == "gather" else sources[item].at[me]
        if mode in SIZES:
            slot = lax.axis_index(mode)
            source = sources[item].at[slot]
            copies.append(
                send(
                    sources[item].at[1 - slot],
                    targets[item].at[slot],
                    send_sem.at[item, 0],
                    recv_sem.at[item, 0],
                    {mode: 1 - slot},
                )
            )
        copy = pltpu.make_async_copy(source, targets[item].at[slot], own_sem.at[item])
        copy.start()
        copies.append(copy)
    return copies


def greet_team(barrier, axes):
    n = size_of(axes)
    me = my_place(axes)
    for k in range(1, n):
        greet(barrier, place_of(axes, lax.rem(me + k, n)))
    return n - 1


def exchange_kernel(axes, modes, *refs):
    count = len(modes)
    barrier = pltpu.get_barrier_semaphore()
    pl.semaphore_wait(barrier, greet_team(barrier, axes))
    copies = team_copies(axes, modes, refs[:count], refs[count : 2 * count], *refs[2 * count :])
    for copy in copies:
        copy.wait()


def received(axes, items):
    n = size_of(axes)
    return [
        jax.ShapeDtypeStruct(((n,) if mode == "gather" else ()) + array.shape, array.dtype)
        for array, mode in items
    ]


def call(kernel, arrays, shapes, scratch, number, name, microseconds):
    moved = sum(s.size * s.dtype.itemsize for s in shapes)
    return pl.pallas_call(
        kernel,
        out_shape=shapes,
        in_specs=[pl.BlockSpec(memory_space=pltpu.VMEM)] * len(arrays),
        out_specs=[pl.BlockSpec(memory_space=pltpu.VMEM)] * len(shapes),
        scratch_shapes=scratch,
        compiler_params=pltpu.CompilerParams(
            collective_id=number, has_side_effects=True, vmem_limit_bytes=48 << 20
        ),
        cost_estimate=pl.CostEstimate(
            flops=microseconds * 10**9, bytes_accessed=2 * moved, transcendentals=0
        ),
        name=name,
    )(*arrays)


def team_semaphores(axes, items):
    return [
        pltpu.SemaphoreType.DMA((len(items), size_of(axes))),
        pltpu.SemaphoreType.DMA((len(items), size_of(axes))),
        pltpu.SemaphoreType.DMA((len(items),)),
    ]


def exchange(items, axes, number, name):
    return call(
        functools.partial(exchange_kernel, axes, tuple(mode for _, mode in items)),
        [array for array, _ in items],
        received(axes, items),
        team_semaphores(axes, items),
        number,
        name,
        20,
    )


def rank_devices():
    yh, x, core = lax.axis_index("yh"), lax.axis_index("x"), lax.axis_index("core")
    across = [lax.rem(x + k, 4) for k in range(4)]
    out = []
    for dy in range(2):
        for dx in range(4):
            for dc in range(2):
                y_at = 1 - yh if dy else yh
                c_at = 1 - core if dc else core
                device = {"yh": y_at, "x": across[dx], "core": c_at}
                out.append((device, y_at * 8 + across[dx] * 2 + c_at))
    return out


def for_each_expert_place(action):
    z = lax.axis_index("zh") * 2 + lax.axis_index("zl")
    rank = rank_devices()

    def of_layer(layer, own):
        high, low = lax.div(layer, 2), lax.rem(layer, 2)
        for k, (device, at) in enumerate(rank):
            action(dict(device, zh=high, zl=low), layer * 16 + at, own and k == 0)

    of_layer(z, True)

    def step(k, carry):
        of_layer(lax.rem(z + k, 4), False)
        return carry

    lax.fori_loop(1, 4, step, 0)


def expert_exchange_kernel(count, modes, *refs):
    every = count + len(modes)
    sources, targets = refs[:every], refs[every : 2 * every]
    send_sem, recv_sem, own_sem, rows_sent, rows_got = refs[2 * every :]
    mine = my_place(DP)
    barrier = pltpu.get_barrier_semaphore()

    def welcome(device, at, own):
        if not own:
            greet(barrier, device)

    for_each_expert_place(welcome)
    pl.semaphore_wait(barrier, 63)
    team = team_copies(
        QUAD, modes, sources[count:], targets[count:], send_sem, recv_sem, own_sem
    )

    def give(device, at, own):
        for item in range(count):
            source, target = sources[item].at[at], targets[item].at[mine]
            if own:
                pltpu.make_async_copy(source, target, rows_got.at[item]).start()
            else:
                send(source, target, rows_sent.at[item], rows_got.at[item], device)

    for_each_expert_place(give)
    for item in range(count):
        sent = sources[item].at[pl.ds(0, 63)]
        pltpu.make_async_copy(sent, sent, rows_sent.at[item]).wait()
        pltpu.make_async_copy(targets[item], targets[item], rows_got.at[item]).wait()
    for copy in team:
        copy.wait()


def expert_exchange(rows, items, number, name):
    rows = [value.reshape(EXPERTS, SLOTS, WIDTH) for value in rows]
    count = len(rows)
    out = call(
        functools.partial(expert_exchange_kernel, count, tuple(mode for _, mode in items)),
        rows + [array for array, _ in items],
        [jax.ShapeDtypeStruct(value.shape, brain) for value in rows] + received(QUAD, items),
        team_semaphores(QUAD, items)
        + [pltpu.SemaphoreType.DMA((count,)), pltpu.SemaphoreType.DMA((count,))],
        number,
        name,
        40 * count,
    )
    rows_got = [value.reshape(EXPERTS * SLOTS, WIDTH) for value in out[:count]]
    return rows_got + list(out[count:])


def rank_gather_kernel(count, modes, *refs):
    every = count + len(modes)
    sources, targets = refs[:count], refs[every : every + count]
    team_sources, team_targets = refs[count:every], refs[every + count : 2 * every]
    send_sem, recv_sem, own_sem, *team_sems = refs[2 * every :]
    yh, x, core = lax.axis_index("yh"), lax.axis_index("x"), lax.axis_index("core")
    right, left, far = lax.rem(x + 1, 4), lax.rem(x + 3, 4), lax.rem(x + 2, 4)
    other = 1 - yh
    to_y, to_right, to_left, to_core = {"yh": other}, {"x": right}, {"x": left}, {"core": 1 - core}
    barrier = pltpu.get_barrier_semaphore()
    for device in (to_y, to_right, to_left, to_core):
        greet(barrier, device)
    pl.semaphore_wait(barrier, 4 + greet_team(barrier, TEAM))

    def slot(y_at, x_at):
        return y_at * 8 + x_at * 2 + core

    sent = []

    def pass_on(item, at, kind, device, source=None):
        target = targets[item].at[at]
        copy = send(
            target if source is None else source,
            target,
            send_sem.at[item, kind],
            recv_sem.at[item, kind],
            device,
        )
        sent.append(copy)
        return copy

    def arrived(item, kind):
        pltpu.make_async_copy(sources[item], sources[item], recv_sem.at[item, kind]).wait()

    items = range(count)
    me = slot(yh, x)
    own = []
    for item in items:
        pass_on(item, me, 0, to_y, sources[item])
        pass_on(item, me, 1, to_right, sources[item])
        pass_on(item, me, 2, to_left, sources[item])
        pass_on(item, me, 7, to_core, sources[item])
        copy = pltpu.make_async_copy(sources[item], targets[item].at[me], own_sem.at[item])
        copy.start()
        own.append(copy)
    team = team_copies(TEAM, modes, team_sources, team_targets, *team_sems)
    steps = (
        (1, slot(yh, left), ((5, to_right), (8, to_core))),
        (0, slot(other, x), ((3, to_right), (4, to_left), (9, to_core))),
        (2, slot(yh, right), ((10, to_core),)),
        (4, slot(other, right), ((6, to_left), (11, to_core))),
        (3, slot(other, left), ((12, to_core),)),
        (5, slot(yh, far), ((13, to_core),)),
        (6, slot(other, far), ((14, to_core),)),
    )
    for kind, at, onward in steps:
        for item in items:
            arrived(item, kind)
            for next_kind, device in onward:
                pass_on(item, at, next_kind, device)
    for item in items:
        for kind in range(7, 15):
            arrived(item, kind)
    for copy in own:
        copy.wait()
    for copy in sent:
        copy.wait_send()
    for copy in team:
        copy.wait()


def rank_gather(arrays, items, number, name):
    count = len(arrays)
    return call(
        functools.partial(rank_gather_kernel, count, tuple(mode for _, mode in items)),
        arrays + [array for array, _ in items],
        [jax.ShapeDtypeStruct((16,) + array.shape, array.dtype) for array in arrays]
        + received(TEAM, items),
        [
            pltpu.SemaphoreType.DMA((count, 15)),
            pltpu.SemaphoreType.DMA((count, 15)),
            pltpu.SemaphoreType.DMA((count,)),
        ]
        + team_semaphores(TEAM, items),
        number,
        name,
        40,
    )


def rank_sum_kernel(count, modes, *refs):
    every = count + len(modes)
    sources, team_sources = refs[:count], refs[count:every]
    targets, team_targets = refs[every : every + count], refs[every + count : 2 * every]
    refs = refs[2 * every :]
    from_core, totals, arrivals = (refs[k * count : (k + 1) * count] for k in range(3))
    send_sem, recv_sem, *team_sems = refs[3 * count :]
    yh, x, core = lax.axis_index("yh"), lax.axis_index("x"), lax.axis_index("core")
    right, left, far = lax.rem(x + 1, 4), lax.rem(x + 3, 4), lax.rem(x + 2, 4)
    other = 1 - yh
    to_y, to_right, to_left, to_core = {"yh": other}, {"x": right}, {"x": left}, {"core": 1 - core}
    barrier = pltpu.get_barrier_semaphore()
    for device in (to_y, to_right, to_left, to_core):
        greet(barrier, device)
    pl.semaphore_wait(barrier, 4 + greet_team(barrier, TEAM))
    items = range(count)
    sent = []

    def pass_on(item, at, kind, device):
        copy = send(
            totals[item].at[at],
            arrivals[item].at[kind],
            send_sem.at[item, kind],
            recv_sem.at[item, kind],
            device,
        )
        sent.append(copy)

    def arrived(item, kind):
        landed = arrivals[item].at[kind]
        pltpu.make_async_copy(landed, landed, recv_sem.at[item, kind]).wait()
        return arrivals[item][kind].astype(single)

    def slot(y_at, x_at):
        return y_at * 4 + x_at

    for item in items:
        sent.append(
            send(
                sources[item].at[:, 1 - core],
                from_core[item],
                send_sem.at[item, 7],
                recv_sem.at[item, 7],
                to_core,
            )
        )
    team = team_copies(TEAM, modes, team_sources, team_targets, *team_sems)
    for item in items:
        landed = from_core[item]
        pltpu.make_async_copy(landed, landed, recv_sem.at[item, 7]).wait()

        def add(at):
            value = sources[item][at, core].astype(single) + from_core[item][at].astype(single)
            totals[item][at] = value.astype(brain)

        add(slot(yh, far))
        pass_on(item, slot(yh, far), 0, to_right)
        add(slot(other, far))
        pass_on(item, slot(other, far), 1, to_left)
        add(slot(other, right))
        pass_on(item, slot(other, right), 3, to_right)
        add(slot(yh, left))
        pass_on(item, slot(yh, left), 5, to_left)
        for at in (slot(yh, right), slot(other, left), slot(yh, x), slot(other, x)):
            add(at)
    for item in items:
        at = slot(yh, right)
        totals[item][at] = (totals[item][at].astype(single) + arrived(item, 0)).astype(brain)
        pass_on(item, at, 2, to_right)
        at = slot(other, left)
        totals[item][at] = (totals[item][at].astype(single) + arrived(item, 1)).astype(brain)
        pass_on(item, at, 4, to_left)
    for item in items:
        at = slot(other, x)
        value = totals[item][at].astype(single) + arrived(item, 3)
        totals[item][at] = (value + arrived(item, 4)).astype(brain)
        pass_on(item, at, 6, to_y)
    for item in items:
        value = totals[item][slot(yh, x)].astype(single) + arrived(item, 5)
        value = value + arrived(item, 2)
        targets[item][...] = (value + arrived(item, 6)).astype(targets[item].dtype)
    for copy in sent:
        copy.wait_send()
    for copy in team:
        copy.wait()


def rank_sum(arrays, items, number, name):
    count = len(arrays)
    arrays = [array.reshape((8, 2) + array.shape[1:]) for array in arrays]
    pieces = [array.shape[2:] for array in arrays]
    scratch = [pltpu.VMEM((8,) + piece, brain) for piece in pieces]
    scratch += [pltpu.VMEM((8,) + piece, brain) for piece in pieces]
    scratch += [pltpu.VMEM((7,) + piece, brain) for piece in pieces]
    scratch += [pltpu.SemaphoreType.DMA((count, 8)), pltpu.SemaphoreType.DMA((count, 8))]
    return call(
        functools.partial(rank_sum_kernel, count, tuple(mode for _, mode in items)),
        arrays + [array for array, _ in items],
        [jax.ShapeDtypeStruct(piece, brain) for piece in pieces] + received(TEAM, items),
        scratch + team_semaphores(TEAM, items),
        number,
        name,
        45,
    )


def dot(left, right):
    return jnp.dot(left, right, preferred_element_type=single)


def dot_t(left, right):
    return lax.dot_general(left, right, (((1,), (1,)), ((), ())), preferred_element_type=single)


def t_dot(left, right):
    return lax.dot_general(left, right, (((0,), (0,)), ((), ())), preferred_element_type=single)


def exact(spec, left, right):
    return jnp.einsum(
        spec, left, right, precision=lax.Precision.HIGHEST, preferred_element_type=single
    )


def rms_scale(value, gain):
    return value * lax.rsqrt(jnp.mean(value * value, axis=-1, keepdims=True) + eps) * gain


def swiglu(value):
    half = value.shape[-1] // 2
    return jax.nn.silu(value[..., :half]) * value[..., half:]


def shuffle_matrix():
    to = jnp.arange(WIDTH, dtype=jnp.int32)
    origin = to // 12 % 8 * 192 + to // 96 * 12 + to % 12
    return (jnp.arange(WIDTH, dtype=jnp.int32)[:, None] == origin[None, :]).astype(brain)


def shuffle(value, matrix):
    return dot(value, matrix).astype(brain)


def unshuffle(value, matrix):
    high = value.astype(brain)
    lower = (value - high.astype(single)).astype(brain)
    both = dot_t(jnp.concatenate([high, lower], axis=0), matrix)
    return both[: value.shape[0]] + both[value.shape[0] :]


def after(values, first):
    return lax.optimization_barrier((values, first))[0]


def pad_rows(value, rows):
    return jnp.pad(value, [(0, 0)] * (value.ndim - 2) + [(0, rows - value.shape[-2]), (0, 0)])


def pad_to(value, rows, columns):
    return jnp.pad(value, ((0, rows - value.shape[0]), (0, columns - value.shape[1])))


def allowed_pairs(seg):
    position = jnp.arange(SEQ, dtype=jnp.int32)
    return (position[:, None] >= position[None, :]) & (seg[..., :, None] == seg[..., None, :])


def product(left, right, dims, precision=None):
    return lax.dot_general(
        left, right, (dims, ((), ())), precision=precision, preferred_element_type=single
    )


def sharp(left, right, dims):
    return product(left, right, dims, lax.Precision.HIGHEST)


def blunt(left, right, dims):
    return product(left.astype(brain), right.astype(brain), dims)


def mamba_parts(zx_ref, masks_ref, same_ref, taps_ref, heads_ref):
    zx = zx_ref[0]
    conv_in = zx[:, INNER : 2 * INNER + 2 * N]
    taps = taps_ref[...]
    same = same_ref[0]
    moved = [conv_in]
    for k in range(1, KW):
        moved.append(pltpu.roll(conv_in, k, 0) * same[:, k : k + 1])
    conv = taps[KW : KW + 1]
    for k in range(KW):
        conv = conv + taps[KW - 1 - k : KW - k] * moved[k]
    gate = jax.nn.sigmoid(conv)
    active = conv * gate
    heads = heads_ref[...]
    raw = zx[:, 2 * INNER + 2 * N :] + heads[0:1]
    step = jnp.maximum(raw, 0.0) + jnp.log1p(jnp.exp(-jnp.abs(raw)))
    rate = step * heads[1:2]
    rows = lax.broadcasted_iota(jnp.int32, (SEQ, SEQ), 0)
    columns = lax.broadcasted_iota(jnp.int32, (SEQ, SEQ), 1)
    lower = (rows >= columns).astype(single)
    total = sharp(lower, rate, ((1,), (0,)))
    total_t = sharp(rate, lower, ((0,), (1,)))
    unit = (rows == columns).astype(single)
    step_t = sharp(step, unit, ((0,), (1,)))
    values = active[:, :INNER]
    in_state, out_state = active[:, INNER : INNER + N], active[:, INNER + N :]
    meeting = sharp(out_state, in_state, ((1,), (1,)))
    allowed = masks_ref[0]
    decays = []
    results = []
    for h in range(HEADS_HERE):
        fall = jnp.exp(jnp.minimum(total[:, h : h + 1] - total_t[h : h + 1], 0.0)) * allowed
        mixing = fall * meeting * step_t[h : h + 1]
        decays.append((fall, mixing))
        results.append(blunt(mixing, values[:, h * P_SIZE : (h + 1) * P_SIZE], ((1,), (0,))))
    result = jnp.concatenate(results, axis=1) + taps[5:6, :INNER] * values
    z = zx[:, :INNER]
    open_z = jax.nn.sigmoid(z)
    return (
        (zx, taps, same, moved, conv, gate, heads, raw, step, step_t, unit, lower),
        (values, in_state, out_state, meeting, decays, result, z, open_z),
    )


def mamba_forward_kernel(zx_ref, masks_ref, same_ref, taps_ref, heads_ref, part_ref, squares_ref):
    (_, taps, *_), (*_, result, z, open_z) = mamba_parts(
        zx_ref, masks_ref, same_ref, taps_ref, heads_ref
    )
    gated = result * (z * open_z)
    part_ref[0] = (gated * taps[6:7, :INNER]).astype(brain)
    sums = sharp(jnp.ones((8, INNER), single), gated * gated, ((1,), (1,)))
    squares_ref[0] = jnp.concatenate([sums, jnp.zeros((8, 128 - SEQ), single)], axis=1)


def mamba_backward_kernel(
    zx_ref, masks_ref, same_ref, taps_ref, heads_ref, d_yn_ref, scalars_ref, d_zx_ref, yn_ref, sums_ref
):
    first, second = mamba_parts(zx_ref, masks_ref, same_ref, taps_ref, heads_ref)
    (zx, taps, same, moved, conv, gate, heads, raw, step, step_t, unit, lower) = first
    (values, in_state, out_state, meeting, decays, result, z, open_z) = second
    scalars = sharp(unit, scalars_ref[0][:, :SEQ], ((1,), (1,)))
    inverse, along = scalars[:, 0:1], scalars[:, 1:2]
    gain, skip = taps[6:7, :INNER], taps[5:6, :INNER]
    d_yn = d_yn_ref[0]
    shut = z * open_z
    gated = result * shut
    scaled = gated * inverse
    yn_ref[0] = (scaled * gain).astype(brain)
    d_gain = jnp.sum(d_yn * scaled, axis=0, keepdims=True)
    d_gated = inverse * gain * d_yn - gated * along
    d_z = d_gated * result * (open_z * (1.0 + z * (1.0 - open_z)))
    d_result = d_gated * shut
    d_skip = jnp.sum(d_result * values, axis=0, keepdims=True)
    lanes = lax.broadcasted_iota(jnp.int32, (1, 128), 1)
    rows = lax.broadcasted_iota(jnp.int32, (128, 1), 0)
    d_meeting = jnp.zeros((SEQ, SEQ), single)
    by_row = jnp.zeros((SEQ, 128), single)
    by_column = jnp.zeros((128, SEQ), single)
    d_step_t = jnp.zeros((128, SEQ), single)
    d_values = []
    for h in range(HEADS_HERE):
        fall, mixing = decays[h]
        own = slice(h * P_SIZE, (h + 1) * P_SIZE)
        d_mixing = blunt(d_result[:, own], values[:, own], ((1,), (1,)))
        d_values.append(blunt(mixing, d_result[:, own], ((0,), (0,))))
        spread = d_mixing * fall
        d_meeting = d_meeting + spread * step_t[h : h + 1]
        spread = spread * meeting
        moving = spread * step_t[h : h + 1]
        by_row = by_row + jnp.sum(moving, axis=1, keepdims=True) * (lanes == h).astype(single)
        at = (rows == h).astype(single)
        by_column = by_column + at * jnp.sum(moving, axis=0, keepdims=True)
        d_step_t = d_step_t + at * jnp.sum(spread, axis=0, keepdims=True)
    d_total = by_row - sharp(unit, by_column, ((1,), (1,)))
    d_rate = sharp(lower, d_total, ((0,), (0,)))
    d_step = sharp(unit, d_step_t, ((1,), (1,))) + d_rate * heads[1:2]
    d_raw = d_step * jax.nn.sigmoid(raw)
    d_decay = jnp.sum(d_rate * step, axis=0, keepdims=True) * heads[1:2]
    d_active = jnp.concatenate(
        [
            jnp.concatenate(d_values, axis=1) + skip * d_result,
            sharp(d_meeting, out_state, ((0,), (0,))),
            sharp(d_meeting, in_state, ((1,), (0,))),
        ],
        axis=1,
    )
    d_conv = d_active * (gate * (1.0 + conv * (1.0 - gate)))
    d_taps = [jnp.sum(d_conv * moved[KW - 1 - k], axis=0, keepdims=True) for k in range(KW)]
    d_in = taps[KW - 1 : KW] * d_conv
    for k in range(1, KW):
        d_in = d_in + pltpu.roll(
            taps[KW - 1 - k : KW - k] * (d_conv * same[:, k : k + 1]), SEQ - k, 0
        )
    d_zx_ref[0] = jnp.concatenate([d_z, d_in, d_raw], axis=1).astype(brain)
    wide = INNER + 2 * N

    def widen(value):
        return jnp.concatenate(
            [value, jnp.zeros((1, wide - value.shape[1]), single)], axis=1
        )

    sums = jnp.concatenate(
        d_taps
        + [jnp.sum(d_conv, axis=0, keepdims=True), widen(d_skip), widen(d_gain)]
        + [widen(jnp.sum(d_raw, axis=0, keepdims=True)), widen(d_decay)]
        + [jnp.zeros((7, wide), single)],
        axis=0,
    )

    @pl.when(pl.program_id(0) == 0)
    def _():
        sums_ref[...] = jnp.zeros_like(sums_ref)

    sums_ref[...] += sums


def by_sequence(kernel, arrays, fixed, shapes, total_shapes, name):
    def whole(shape):
        return pl.BlockSpec(shape, lambda n: (0,) * len(shape))

    def one(shape):
        return pl.BlockSpec((1,) + shape[1:], lambda n: (n,) + (0,) * (len(shape) - 1))

    return pl.pallas_call(
        kernel,
        grid=(PARTS,),
        out_shape=shapes + total_shapes,
        in_specs=[
            whole(array.shape) if place in fixed else one(array.shape)
            for place, array in enumerate(arrays)
        ],
        out_specs=[one(s.shape) for s in shapes] + [whole(s.shape) for s in total_shapes],
        compiler_params=pltpu.CompilerParams(vmem_limit_bytes=32 << 20),
        name=name,
    )(*arrays)


def attend_scores(queries, keys, seg):
    scores = exact("nird,njd->nrij", queries, keys) * HEAD_SIZE ** (-0.5)
    scores = jnp.where(allowed_pairs(seg)[:, None], scores, -1e30)
    return jax.nn.softmax(scores, axis=-1)


def attend_mix(probs, values):
    return exact("nrij,njd->nird", probs, values)


def per_device(
    block_input,
    cotangent,
    segments,
    routes,
    in_proj,
    conv_taps,
    conv_bias,
    step_bias,
    decay_log,
    skip_weight,
    norm_gain,
    out_proj,
    query_proj,
    key_value_projection,
    attn_out_proj,
    norm_gains,
    router,
    shared_in,
    shared_out,
    experts_in,
    experts_out,
):
    phase = lax.axis_index("phase")
    first_phase = phase == 0
    zl = lax.axis_index("zl")
    team = phase * 4 + lax.axis_index("zh") * 2 + zl

    def mine(value):
        return lax.dynamic_index_in_dim(value, phase, 0, keepdims=False)

    start = mine(block_input)
    cot = mine(cotangent)
    seg = mine(segments)
    route_rows = mine(routes)

    both_ways = [(0, 1), (1, 0)]
    w_first, w_second = experts_in[0, 0], experts_out[0, 0]

    z_piece = in_proj[:, :DI].reshape(12, PARTS, INNER).transpose(1, 0, 2)
    x_piece = in_proj[:, DI : 2 * DI].reshape(12, PARTS, INNER).transpose(1, 0, 2)
    state_piece = jnp.broadcast_to(in_proj[None, :, 2 * DI : 2 * DI + 2 * N], (PARTS, 12, 2 * N))
    step_piece = in_proj[:, 2 * DI + 2 * N :].reshape(12, PARTS, HEADS_HERE).transpose(1, 0, 2)
    step_piece = jnp.pad(step_piece, ((0, 0), (0, 0), (0, 128 - HEADS_HERE)))
    q_piece = query_proj.reshape(12, 4, 384).transpose(1, 0, 2)
    kv_piece = key_value_projection.reshape(12, 2, 4, 128).transpose(2, 0, 1, 3).reshape(4, 12, 256)
    qkv_piece = jnp.repeat(jnp.concatenate([q_piece, kv_piece], axis=2), 2, axis=0)
    in_piece = pad_rows(jnp.concatenate([z_piece, x_piece, state_piece, step_piece], axis=2), 16)
    qkv_piece = pad_rows(qkv_piece, 16)
    sin_piece = shared_in[0].reshape(24, 2, 4, 256).transpose(2, 0, 1, 3).reshape(4, 24, 512)
    sin_piece = pad_rows(jnp.concatenate([sin_piece, sin_piece], axis=0), 32)
    sout_piece = jnp.broadcast_to(shared_out, (2, 16, WIDTH))
    attn_piece = jnp.broadcast_to(pad_rows(attn_out_proj, 16)[None], (2, 16, WIDTH))
    mixing = shuffle_matrix()
    rest = jnp.concatenate(
        [conv_taps.reshape(-1), conv_bias, norm_gain, norm_gains[0].reshape(-1)]
    )
    rest = jnp.pad(rest, (0, 512 - rest.shape[0])).reshape(4, 128)
    small = jnp.concatenate([router[0].reshape(12, 128), rest], axis=0)
    seg_piece = pad_to(seg, 8, 128)
    in_got, sin_got, sout_got, small_got, seg_got = exchange(
        [
            (in_piece, "swap"),
            (sin_piece, "swap"),
            (sout_piece, "phase"),
            (small, "gather"),
            (seg_piece, "gather"),
        ],
        TEAM,
        0,
        "team_start",
    )
    seg_all = seg_got[:, 0, :SEQ]
    sin_got = sin_got[:, :24].reshape(2, 96, 512)

    def to_other_phase(value):
        return lax.ppermute(value, "phase", both_ways)

    half = WIDTH // 2
    w_second_far = to_other_phase(w_second)
    in_rows, w_second_far = lax.optimization_barrier(
        (in_got[:, :12].reshape(96, IN_COLS), w_second_far)
    )
    w_first_far = [to_other_phase(after(w_first[:half], w_second_far))]
    w_in, small_all, w_out, start_all, qkv_got, attn_got = rank_gather(
        [in_rows, small_got.reshape(128, 128), pad_rows(out_proj, 32)],
        [(shuffle(start, mixing), "gather"), (qkv_piece, "swap"), (attn_piece, "zl")],
        1,
        "rank_weights",
    )
    w_in = w_in.reshape(WIDTH, IN_COLS)
    w_out = w_out[:, :24].reshape(INNER, WIDTH)
    later_wide = jnp.concatenate([qkv_got[:, :12].reshape(96, QKV_COLS), sin_got[1]], axis=1)
    later_tall = jnp.concatenate([attn_got[:, :12].reshape(24, WIDTH), sout_got[1]], axis=0)
    start_all, first_piece = lax.optimization_barrier((start_all, w_first_far[0]))
    w_first_far = [first_piece, to_other_phase(after(w_first[half:], first_piece))]
    later_wide = lax.all_gather(later_wide, RANK, axis=0)
    later_tall = lax.all_gather(later_tall, RANK, axis=0)
    w_qkv = later_wide[:, :, :QKV_COLS].reshape(WIDTH, QKV_COLS)
    w_attn = later_tall[:, :24].reshape(16, 2, 12, WIDTH).transpose(1, 0, 2, 3)
    w_attn = w_attn.reshape(384, WIDTH)

    def hidden_in(value):
        return value.reshape(16, 4, 24, 512).transpose(1, 0, 2, 3).reshape(WIDTH, 512)

    small_all = small_all.reshape(16, 2, 4, 16, 128)
    router_full = small_all[:, :, :, :12].reshape(16, 2, 4, 24, EXPERTS).transpose(1, 2, 0, 3, 4)
    router_full = router_full.reshape(2, WIDTH, EXPERTS)
    rest_all = small_all[:, :, :, 12:].reshape(16, 2, 4, 512)
    conv_full = rest_all[..., :130].reshape(16, 2, 4, 5, 26).transpose(3, 1, 2, 0, 4)
    conv_full = conv_full.reshape(5, CONVW).astype(single)
    gain_here = rest_all[..., 130:154].reshape(16, 8, 24)
    gain_here = lax.dynamic_index_in_dim(gain_here, team, 1, keepdims=False)
    gain_here = gain_here.reshape(INNER).astype(single)
    gains = rest_all[..., 154:202].reshape(16, 2, 4, 2, 24).transpose(1, 3, 2, 0, 4)
    gains = gains.reshape(2, 2, WIDTH).astype(single)
    conv_here = jnp.concatenate(
        [lax.dynamic_slice_in_dim(conv_full[:, :DI], team * INNER, INNER, 1), conv_full[:, DI:]],
        axis=1,
    )

    def heads_of(value):
        return lax.dynamic_slice_in_dim(value, team * HEADS_HERE, HEADS_HERE, 0)

    skip_wide = jnp.repeat(heads_of(skip_weight), P_SIZE)
    columns = jnp.stack([jnp.pad(skip_wide, (0, 2 * N)), jnp.pad(gain_here, (0, 2 * N))])
    taps_here = jnp.concatenate([conv_here, columns, jnp.zeros((1, INNER + 2 * N), single)], axis=0)
    heads_here = jnp.stack([heads_of(step_bias), -jnp.exp(heads_of(decay_log))])
    heads_here = pad_to(heads_here, 8, 128)
    allowed_all = allowed_pairs(seg_all).astype(single)
    same_all = [
        jnp.pad(seg_all[:, k:] == seg_all[:, : SEQ - k], ((0, 0), (k, 0))) for k in range(KW)
    ]
    same_all = jnp.pad(jnp.stack(same_all, axis=2).astype(single), ((0, 0), (0, 0), (0, 128 - KW)))

    expert_ids = jnp.arange(EXPERTS, dtype=jnp.int32)
    named = jnp.any(route_rows[:, :, None] == expert_ids, axis=1)
    position = jnp.arange(SEQ, dtype=jnp.int32)
    earlier = (position[:, None] > position[None, :]).astype(brain)
    slot = dot(earlier, named.astype(brain))
    slot = jnp.where(named, slot, -1.0).astype(brain)
    cell = jnp.arange(EXPERTS * SLOTS, dtype=jnp.int32)
    spread = (cell[None, :] // SLOTS == expert_ids[:, None]).astype(brain)
    taken = dot(slot, spread) == (cell % SLOTS).astype(single)
    taken_b = taken.astype(brain)

    def of_block(s):
        own = phase == s
        return (
            jnp.where(own, w_first, w_first_far),
            jnp.where(own, w_second, w_second_far),
        )

    def moe_open(s, hidden):
        normed = rms_scale(hidden, gains[s, 1]).astype(brain)
        logits = dot(normed, router_full[s])
        top = jnp.max(jnp.where(named, logits, -jnp.inf), axis=1, keepdims=True)
        weight = jnp.where(named, jnp.exp(logits - top), 0.0)
        gates = weight / jnp.sum(weight, axis=1, keepdims=True)
        gates_wide = jnp.where(taken, exact("ie,ec->ic", gates, spread.astype(single)), 0.0)
        return normed, gates, gates_wide, t_dot(taken_b, normed).astype(brain)

    def moe_experts(weights, rows_in):
        both = dot(rows_in, weights[0])
        hid = swiglu(both).astype(brain)
        return both, hid, dot(hid, weights[1]).astype(brain)

    def moe_shared(s, normed_all):
        both = dot(normed_all, sin_full[s])
        hid = swiglu(both).astype(brain)
        part = dot(hid, sout_full[s]).astype(brain)
        return both, hid, part.reshape(4, SEQ, WIDTH)

    def moe_join(hidden, gates_wide, back, shared_got):
        high = gates_wide.astype(brain)
        lower = (gates_wide - high.astype(single)).astype(brain)
        moe = dot(high, back) + dot(lower, back)
        return (hidden + moe + jnp.sum(shared_got.astype(single), axis=0)).astype(brain)

    def back_open(d_out, gates_wide):
        gate_cell = jnp.sum(gates_wide, axis=0)
        return (t_dot(taken_b, d_out) * gate_cell[:, None]).astype(brain)

    def back_experts(weights, d_answer, both):
        d_hid = dot_t(d_answer, weights[1])
        d_both = jax.vjp(swiglu, both)[1](d_hid)[0].astype(brain)
        return d_both, dot_t(d_both, weights[0]).astype(brain)

    def back_shared(s, d_out_all, normed_all, both, hid):
        d_hid = dot_t(d_out_all, sout_full[s])
        d_sout = t_dot(hid, d_out_all)
        d_both = jax.vjp(swiglu, both)[1](d_hid)[0].astype(brain)
        d_sin = t_dot(normed_all, d_both)
        d_part = dot_t(d_both, sin_full[s]).astype(brain).reshape(4, SEQ, WIDTH)
        return d_sin, d_sout, d_part

    def back_join(s, d_out, hidden, normed, gates, back, returned, d_shared_got):
        d_cells = jnp.where(taken, dot_t(d_out, back), 0.0)
        d_gates = exact("ic,ec->ie", d_cells, spread.astype(single))
        d_logits = gates * (d_gates - jnp.sum(gates * d_gates, axis=1, keepdims=True))
        d_normed = exact("ie,we->iw", d_logits, router_full[s].astype(single))
        d_router = exact("iw,ie->we", normed.astype(single), d_logits)
        d_normed = d_normed + dot(taken_b, returned) + jnp.sum(d_shared_got.astype(single), axis=0)
        d_hidden, d_gain = jax.vjp(rms_scale, hidden, gains[s, 1])[1](d_normed)
        return d_hidden + d_out.astype(single), d_gain, d_router

    def shared_in_parts(value):
        return value.astype(brain).reshape(4, 16, 24, 512).transpose(1, 0, 2, 3).reshape(16, 96, 512)

    u0 = start.astype(single)
    shuffled_gain = shuffle(gains[0, 0][None].astype(brain), mixing)[0].astype(single)
    n1_all = rms_scale(start_all.astype(single), shuffled_gain).astype(brain)
    n1_all = n1_all.reshape(PARTS * SEQ, WIDTH)
    zx = dot(n1_all, w_in).reshape(PARTS, SEQ, IN_COLS)

    core_inputs = [zx, allowed_all, same_all, taps_here, heads_here]
    part, squares = by_sequence(
        mamba_forward_kernel,
        core_inputs,
        (3, 4),
        [
            jax.ShapeDtypeStruct((PARTS, SEQ, INNER), brain),
            jax.ShapeDtypeStruct((PARTS, 8, 128), single),
        ],
        [],
        "mamba_forward",
    )
    part = dot(part.reshape(PARTS * SEQ, INNER), w_out)
    part = part.astype(brain).reshape(PARTS, SEQ, WIDTH)
    part, second_piece = lax.optimization_barrier((part, w_first_far[1]))
    w_first_far = jnp.concatenate([w_first_far[0], second_piece], axis=0)
    sin_all, sout_all, part_got, squares_got = rank_gather(
        [sin_got[0], sout_got[0]], [(part, "swap"), (squares, "swap")], 2, "team_mixed_0"
    )
    sin_full = (hidden_in(sin_all), hidden_in(later_wide[:, :, QKV_COLS:]))
    sout_full = (sout_all.reshape(256, WIDTH), later_tall[:, 24:].reshape(256, WIDTH))
    mean_square = jnp.sum(squares_got[:, 0, :SEQ], axis=0) / DI
    inverse = lax.rsqrt(mean_square + eps)
    mixed0 = jnp.sum(part_got.astype(single), axis=0) * inverse[:, None]
    hidden0 = u0 + mixed0
    normed0, gates0, gates_wide0, rows_out0 = moe_open(0, hidden0)
    rows_in0, normed_all0 = expert_exchange([rows_out0], [(normed0, "gather")], 3, "spread_0")
    normed_all0 = normed_all0.reshape(4 * SEQ, WIDTH)
    weights0 = of_block(0)
    sboth0, shid0, shared_part0 = moe_shared(0, normed_all0)
    both0, hid0, answer0 = moe_experts(weights0, rows_in0)
    back0, shared_got0 = expert_exchange([answer0], [(shared_part0, "swap")], 4, "collect_0")
    out0 = moe_join(hidden0, gates_wide0, back0, shared_got0)

    u1 = out0.astype(single)
    n1 = rms_scale(u1, gains[1, 0]).astype(brain)
    (n1_half,) = exchange([(shuffle(n1, mixing), "gather")], HALF, 5, "half_n1")
    n1_half = n1_half.reshape(4 * SEQ, WIDTH)
    seg_half = lax.dynamic_index_in_dim(seg_all.reshape(4, 2, SEQ), zl, 1, keepdims=False)
    qkv = dot(n1_half, w_qkv).astype(brain).astype(single).reshape(4, SEQ, QKV_COLS)
    queries = qkv[..., :384].reshape(4, SEQ, 3, HEAD_SIZE)
    keys, values = qkv[..., 384:512], qkv[..., 512:]
    probs, score_pull = jax.vjp(lambda q, k: attend_scores(q, k, seg_half), queries, keys)
    heads, mix_pull = jax.vjp(attend_mix, probs.astype(brain).astype(single), values)
    heads = heads.astype(brain).reshape(4 * SEQ, 384)
    part1 = dot(heads, w_attn).astype(brain).reshape(4, SEQ, WIDTH)
    (part1_got,) = exchange([(part1, "swap")], HALF, 6, "half_mixed")
    mixed1 = jnp.sum(part1_got.astype(single), axis=0)
    hidden1 = u1 + mixed1

    normed1, gates1, gates_wide1, rows_out1 = moe_open(1, hidden1)
    rows_in1, d_answer1, normed_all1, cot_all = expert_exchange(
        [rows_out1, back_open(cot, gates_wide1)],
        [(normed1, "gather"), (cot, "gather")],
        7,
        "spread_1",
    )
    normed_all1 = normed_all1.reshape(4 * SEQ, WIDTH)
    cot_all = cot_all.reshape(4 * SEQ, WIDTH)
    weights1 = of_block(1)
    sboth1, shid1, shared_part1 = moe_shared(1, normed_all1)
    d_sin1, d_sout1, d_shared1 = back_shared(1, cot_all, normed_all1, sboth1, shid1)
    both1, hid1, answer1 = moe_experts(weights1, rows_in1)
    d_both1, d_rows1 = back_experts(weights1, d_answer1, both1)
    back1, returned1, shared_got1, d_shared_got1 = expert_exchange(
        [answer1, d_rows1], [(shared_part1, "swap"), (d_shared1, "swap")], 8, "collect_1"
    )
    out1 = moe_join(hidden1, gates_wide1, back1, shared_got1)

    d_hid1, d_gain11, d_router1 = back_join(
        1, cot, hidden1, normed1, gates1, back1, returned1, d_shared_got1
    )
    (d_mixed1,) = exchange([(d_hid1.astype(brain), "gather")], HALF, 11, "half_dmixed")
    d_mixed1 = d_mixed1.reshape(4 * SEQ, WIDTH)
    d_heads = dot_t(d_mixed1, w_attn).reshape(4, SEQ, 3, HEAD_SIZE)
    d_attn = t_dot(heads, d_mixed1)
    d_probs, d_values = mix_pull(d_heads)
    d_queries, d_keys = score_pull(d_probs)
    d_qkv = jnp.concatenate([d_queries.reshape(4, SEQ, 384), d_keys, d_values], axis=2)
    d_qkv = d_qkv.astype(brain).reshape(4 * SEQ, QKV_COLS)
    d_w_qkv = t_dot(n1_half, d_qkv)
    d_n1_part = dot_t(d_qkv, w_qkv).astype(brain).reshape(4, SEQ, WIDTH)
    grads_wide = jnp.concatenate(
        [d_w_qkv.astype(brain).reshape(16, 96, QKV_COLS), shared_in_parts(d_sin1)], axis=2
    )
    attn_part = d_attn.astype(brain).reshape(2, 16, 12, WIDTH).transpose(1, 0, 2, 3)
    grads_tall = jnp.concatenate(
        [attn_part.reshape(16, 24, WIDTH), d_sout1.astype(brain).reshape(16, 16, WIDTH)], axis=1
    )
    grads_tall = jnp.pad(grads_tall.reshape(16, 40 * WIDTH), ((0, 0), (0, 54 * IN_COLS - 40 * WIDTH)))
    grads_later = jnp.concatenate([grads_wide, grads_tall.reshape(16, 54, IN_COLS)], axis=1)
    d_n1_part, grads_later = lax.optimization_barrier((d_n1_part, grads_later))
    grads_later = lax.psum_scatter(grads_later, RANK, scatter_dimension=0, tiled=True)[0]
    (d_n1_got,) = exchange([(d_n1_part, "swap")], HALF, 12, "half_dn1")
    d_n1 = unshuffle(jnp.sum(d_n1_got.astype(single), axis=0), mixing)
    d_u1, d_gain10 = jax.vjp(rms_scale, u1, gains[1, 0])[1](d_n1)
    d_u1 = (d_u1 + d_hid1).astype(brain)

    d_answer0, d_out0_all = expert_exchange(
        [back_open(d_u1, gates_wide0)], [(d_u1, "gather")], 13, "spread_back_0"
    )
    d_out0_all = d_out0_all.reshape(4 * SEQ, WIDTH)
    d_sin0, d_sout0, d_shared0 = back_shared(0, d_out0_all, normed_all0, sboth0, shid0)
    d_both0, d_rows0 = back_experts(weights0, d_answer0, both0)
    expert0 = (rows_in0, d_both0, hid0, d_answer0)
    expert1 = (rows_in1, d_both1, hid1, d_answer1)
    give_rows, give_both, give_hid, give_answer = (
        jnp.where(first_phase, b, a) for a, b in zip(expert0, expert1)
    )
    give_first = t_dot(give_rows, give_both).astype(brain)
    give_second = t_dot(give_hid, give_answer).astype(brain)
    d_rows0, give_first, give_second = lax.optimization_barrier((d_rows0, give_first, give_second))
    far_second = to_other_phase(give_second)
    returned0, d_shared_got0 = expert_exchange(
        [d_rows0], [(d_shared0, "swap")], 14, "collect_back_0"
    )
    d_hid0, d_gain01, d_router0 = back_join(
        0, d_u1, hidden0, normed0, gates0, back0, returned0, d_shared_got0
    )
    d_mixed0 = d_hid0.astype(brain)
    along = jnp.sum(d_mixed0.astype(single) * mixed0, axis=1)
    scalars = jnp.stack([inverse, inverse * inverse * along / DI])
    d_mixed0, far_second = lax.optimization_barrier((d_mixed0, far_second))
    sin_part0, sout_part0, d_mixed0, scalars_all = rank_sum(
        [shared_in_parts(d_sin0), d_sout0.astype(brain).reshape(16, 16, WIDTH)],
        [(d_mixed0, "gather"), (pad_to(scalars, 8, 128), "gather")],
        15,
        "team_dmixed",
    )
    far_first = [to_other_phase(after(give_first[:half], d_mixed0))]
    d_mixed0 = d_mixed0.reshape(PARTS * SEQ, WIDTH)
    d_yn = dot_t(d_mixed0, w_out).reshape(PARTS, SEQ, INNER)
    d_zx, yn, core_sums = by_sequence(
        mamba_backward_kernel,
        core_inputs + [d_yn, scalars_all],
        (3, 4),
        [
            jax.ShapeDtypeStruct((PARTS, SEQ, IN_COLS), brain),
            jax.ShapeDtypeStruct((PARTS, SEQ, INNER), brain),
        ],
        [jax.ShapeDtypeStruct((16, INNER + 2 * N), single)],
        "mamba_backward",
    )
    d_w_out = t_dot(yn.reshape(PARTS * SEQ, INNER), d_mixed0)
    d_zx = d_zx.reshape(PARTS * SEQ, IN_COLS)
    d_norm_gain = core_sums[6, :INNER]
    d_skip = jnp.sum(core_sums[5, :INNER].reshape(HEADS_HERE, P_SIZE), axis=1)
    d_step, d_decay = core_sums[7, :HEADS_HERE], core_sums[8, :HEADS_HERE]
    d_w_in = t_dot(n1_all, d_zx)
    d_n1_part0 = dot_t(d_zx, w_in).astype(brain)
    shuffled = start_all.astype(single)
    shuffled = shuffled * lax.rsqrt(jnp.mean(shuffled * shuffled, axis=-1, keepdims=True) + eps)
    d_gain00 = jnp.sum(
        shuffled.reshape(PARTS * SEQ, WIDTH) * d_n1_part0.astype(single), axis=0
    )
    d_gain00 = d_gain00.reshape(16, 8, 12).transpose(1, 0, 2).reshape(WIDTH)
    d_n1_part0 = d_n1_part0.reshape(PARTS, SEQ, WIDTH)
    d_n1_part0, grads_later, first_piece = lax.optimization_barrier(
        (d_n1_part0, grads_later, far_first[0])
    )
    far_first = [first_piece, to_other_phase(after(give_first[half:], first_piece))]

    qkv_part = grads_later[:96, :QKV_COLS].reshape(PARTS, 12, QKV_COLS)
    sin_part1 = grads_later[:96, QKV_COLS:].reshape(4, 24, 512)
    grads_tall = grads_later[96:].reshape(54 * IN_COLS)[: 40 * WIDTH].reshape(40, WIDTH)
    attn_part, sout_part1 = grads_tall[:24].reshape(2, 12, WIDTH), grads_tall[24:]

    conv_grads = core_sums[: KW + 1]
    conv_all = jnp.concatenate(
        [
            lax.dynamic_update_slice_in_dim(
                jnp.zeros((KW + 1, DI), single), conv_grads[:, :INNER], team * INNER, 1
            ),
            conv_grads[:, INNER:],
        ],
        axis=1,
    )
    conv_all = conv_all.reshape(5, 8, 16, 26).transpose(2, 1, 0, 3).reshape(16, 8, 130)
    head_all = lax.dynamic_update_slice_in_dim(
        jnp.zeros((3, H), single), jnp.stack([d_step, d_decay, d_skip]), team * HEADS_HERE, 1
    )
    head_all = jnp.broadcast_to(head_all.reshape(1, 1, 3 * H), (16, 8, 3 * H))
    gain_all = lax.dynamic_update_slice_in_dim(
        jnp.zeros((16, 8, 24), single), d_norm_gain.reshape(16, 1, 24), team, 1
    )
    d_gains = jnp.stack([jnp.stack([d_gain00, d_gain01]), jnp.stack([d_gain10, d_gain11])])
    d_gains = d_gains.reshape(2, 2, 4, 16, 24).transpose(3, 0, 2, 1, 4).reshape(16, 8, 48)
    d_router = jnp.stack([d_router0, d_router1]).reshape(2, 4, 16, 24 * EXPERTS)
    d_router = d_router.transpose(2, 0, 1, 3).reshape(16, 8, 24 * EXPERTS)
    small_grads = jnp.concatenate([d_router, conv_all, gain_all, d_gains, head_all], axis=2)
    small_grads = jnp.pad(small_grads, ((0, 0), (0, 0), (0, 2048 - small_grads.shape[2])))
    small_grads = small_grads.astype(brain).reshape(16, 128, 128)
    main_part, out_proj_grad, small_part, d_n1_got0, phase_outputs = rank_sum(
        [
            d_w_in.astype(brain).reshape(16, 96, IN_COLS),
            pad_rows(d_w_out.astype(brain).reshape(16, 24, WIDTH), 32),
            small_grads,
        ],
        [(d_n1_part0, "swap"), (jnp.stack([out0, out1]), "phase")],
        17,
        "rank_grads",
    )
    main_part = main_part.reshape(PARTS, 12, IN_COLS)
    sin_part0 = sin_part0.reshape(4, 24, 512)
    d_n1_0 = unshuffle(jnp.sum(d_n1_got0.astype(single), axis=0), mixing)
    (d_u0,) = jax.vjp(lambda value: rms_scale(value, gains[0, 0]), u0)[1](d_n1_0)
    d_u0 = d_u0 + d_hid0

    rows_kept, d_both_kept, hid_kept, d_answer_kept = (
        jnp.where(first_phase, a, b) for a, b in zip(expert0, expert1)
    )
    main_part, second_piece = lax.optimization_barrier((main_part, far_first[1]))
    far_first = jnp.concatenate([far_first[0], second_piece], axis=0)
    experts_in_grad = t_dot(rows_kept, d_both_kept) + far_first.astype(single)
    experts_out_grad = t_dot(hid_kept, d_answer_kept) + far_second.astype(single)

    main_end, qkv_end, sin_end, sout_end, attn_end, small_end, input_grads = exchange(
        [
            (pad_rows(main_part, 16), "swap"),
            (pad_rows(qkv_part, 16), "swap"),
            (pad_rows(jnp.concatenate([sin_part0, sin_part1], axis=0), 32), "swap"),
            (jnp.stack([sout_part0, sout_part1]), "phase"),
            (pad_rows(attn_part, 16), "zl"),
            (small_part.reshape(PARTS, 16, 128), "swap"),
            (jnp.stack([d_u0, d_u1.astype(single)]), "phase"),
        ],
        TEAM,
        18,
        "team_end",
    )
    rows_end = main_end[:, :12].astype(single)

    def side_by_side(value):
        return value.transpose(1, 0, 2).reshape(value.shape[1], -1)

    in_proj_grad = jnp.concatenate(
        [
            side_by_side(rows_end[:, :, :INNER]),
            side_by_side(rows_end[:, :, INNER : 2 * INNER]),
            jnp.sum(rows_end[:, :, 2 * INNER : 2 * INNER + 2 * N], axis=0),
            side_by_side(
                rows_end[:, :, 2 * INNER + 2 * N : 2 * INNER + 2 * N + HEADS_HERE]
            ),
        ],
        axis=1,
    )
    small_end = jnp.sum(small_end.astype(single), axis=0).reshape(2048)
    router_grad = small_end[: 24 * EXPERTS].reshape(1, 24, EXPERTS)
    at = 24 * EXPERTS
    conv_end = small_end[at : at + 130].reshape(5, 26)
    at += 130
    norm_gain_grad = small_end[at : at + 24]
    at += 24
    norm_gains_grad = small_end[at : at + 48].reshape(1, 2, 24)
    at += 48
    heads_end = small_end[at : at + 3 * H].reshape(3, H)
    qkv_end = qkv_end[:, :12].astype(single).reshape(4, 2, 12, QKV_COLS)
    qkv_end = jnp.sum(qkv_end, axis=1)
    query_grad = side_by_side(qkv_end[:, :, :384])
    kv_grad = qkv_end[:, :, 384:].reshape(4, 12, 2, 128).transpose(1, 2, 0, 3).reshape(12, 1024)
    sin_end = jnp.sum(sin_end[:, :24].astype(single).reshape(2, 4, 24, 2, 256), axis=0)
    shared_in_grad = sin_end.transpose(1, 2, 0, 3).reshape(1, 24, 2048)
    shared_out_grad = jnp.sum(sout_end.astype(single), axis=0)[None]
    attn_out_grad = jnp.sum(attn_end[:, :12].astype(single), axis=0)

    return (
        phase_outputs[None],
        input_grads[None],
        in_proj_grad,
        conv_end[:KW],
        conv_end[KW],
        heads_end[0],
        heads_end[1],
        heads_end[2],
        norm_gain_grad,
        out_proj_grad[:24].astype(single),
        query_grad,
        kv_grad,
        attn_out_grad,
        norm_gains_grad,
        router_grad,
        shared_in_grad,
        shared_out_grad,
        experts_in_grad[None, None],
        experts_out_grad[None, None],
    )


def solution(mesh):
    fine = Mesh(mesh.devices.reshape(tuple(SIZES.values())), ALL)
    in_specs = (
        P(None, DP, None),
        P(None, DP, None),
        P(None, DP, None),
        P(None, DP, None),
        P(ALL, None),
        P(None, ALL),
        P(ALL),
        P(),
        P(),
        P(),
        P(ALL),
        P(ALL, None),
        P(ALL, None),
        P(ALL, None),
        P(ALL, None),
        P("phase", None, DP),
        P("phase", DP, None),
        P("phase", DP, None),
        P("phase", DP, None),
        P("phase", DP, None, None),
        P("phase", DP, None, None),
    )
    out_specs = (
        P("phase", None, DP, None),
        P("phase", None, DP, None),
        P(ALL, None),
        P(None, ALL),
        P(ALL),
        P(),
        P(),
        P(),
        P(ALL),
        P(ALL, None),
        P(ALL, None),
        P(ALL, None),
        P(ALL, None),
        P("phase", None, DP),
        P("phase", DP, None),
        P("phase", DP, None),
        P("phase", DP, None),
        P("phase", DP, None, None),
        P("phase", DP, None, None),
    )
    return jax.shard_map(
        per_device, mesh=fine, in_specs=in_specs, out_specs=out_specs, check_vma=False
    )
```

```python
import functools

import jax
import jax.numpy as jnp
from jax import lax
from jax.experimental import pallas as pl
from jax.experimental.pallas import tpu as pltpu
from jax.sharding import Mesh
from jax.sharding import PartitionSpec as P

H = 48
P_SIZE = 64
N = 128
KW = 4
QUERY_HEADS = 12
KEY_VALUE_HEADS = 4
HEAD_SIZE = 128
DI = 3072
CONVW = 3328
WIDTH = 1536
SEQ = 64
EXPERTS = 64
SLOTS = 8
PARTS = 8
HEADS_HERE = H // PARTS
INNER = DI // PARTS
IN_COLS = 1152
QKV_COLS = 640

SIZES = {"phase": 2, "zh": 2, "zl": 2, "yh": 2, "x": 4, "core": 2}
TEAM = ("phase", "zh", "zl")
HALF = ("phase", "zh")
QUAD = ("zh", "zl")
RANK = ("yh", "x", "core")
DP = ("zh", "zl", "yh", "x", "core")
ALL = ("phase", "zh", "zl", "yh", "x", "core")
MESH_ID = pl.DeviceIdType.MESH

eps = 1e-05
single = jnp.float32
brain = jnp.bfloat16


def place_of(axes, index):
    out = {}
    for name in reversed(axes):
        out[name] = lax.rem(index, SIZES[name])
        index = lax.div(index, SIZES[name])
    return out


def size_of(axes):
    total = 1
    for name in axes:
        total *= SIZES[name]
    return total


def my_place(axes):
    me = jnp.int32(0)
    for name in axes:
        me = me * SIZES[name] + lax.axis_index(name)
    return me


def greet(barrier, device):
    pl.semaphore_signal(barrier, inc=1, device_id=device, device_id_type=MESH_ID)


def send(source, target, send_sem, recv_sem, device):
    copy = pltpu.make_async_remote_copy(
        src_ref=source,
        dst_ref=target,
        send_sem=send_sem,
        recv_sem=recv_sem,
        device_id=device,
        device_id_type=MESH_ID,
    )
    copy.start()
    return copy


def team_copies(axes, modes, sources, targets, send_sem, recv_sem, own_sem):
    n = size_of(axes)
    me = my_place(axes)
    copies = []
    for k in range(1, n):
        peer = lax.rem(me + k, n)
        device = place_of(axes, peer)
        for item, mode in enumerate(modes):
            if mode in SIZES:
                continue
            source = sources[item].at[peer] if mode == "swap" else sources[item]
            copies.append(
                send(
                    source,
                    targets[item].at[me],
                    send_sem.at[item, k],
                    recv_sem.at[item, k],
                    device,
                )
            )
    for item, mode in enumerate(modes):
        slot = me
        source = sources[item] if mode == "gather" else sources[item].at[me]
        if mode in SIZES:
            slot = lax.axis_index(mode)
            source = sources[item].at[slot]
            copies.append(
                send(
                    sources[item].at[1 - slot],
                    targets[item].at[slot],
                    send_sem.at[item, 0],
                    recv_sem.at[item, 0],
                    {mode: 1 - slot},
                )
            )
        copy = pltpu.make_async_copy(source, targets[item].at[slot], own_sem.at[item])
        copy.start()
        copies.append(copy)
    return copies


def greet_team(barrier, axes):
    n = size_of(axes)
    me = my_place(axes)
    for k in range(1, n):
        greet(barrier, place_of(axes, lax.rem(me + k, n)))
    return n - 1


def exchange_kernel(axes, modes, *refs):
    count = len(modes)
    barrier = pltpu.get_barrier_semaphore()
    pl.semaphore_wait(barrier, greet_team(barrier, axes))
    copies = team_copies(axes, modes, refs[:count], refs[count : 2 * count], *refs[2 * count :])
    for copy in copies:
        copy.wait()


def received(axes, items):
    n = size_of(axes)
    return [
        jax.ShapeDtypeStruct(((n,) if mode == "gather" else ()) + array.shape, array.dtype)
        for array, mode in items
    ]


def call(kernel, arrays, shapes, scratch, number, name, microseconds):
    moved = sum(s.size * s.dtype.itemsize for s in shapes)
    return pl.pallas_call(
        kernel,
        out_shape=shapes,
        in_specs=[pl.BlockSpec(memory_space=pltpu.VMEM)] * len(arrays),
        out_specs=[pl.BlockSpec(memory_space=pltpu.VMEM)] * len(shapes),
        scratch_shapes=scratch,
        compiler_params=pltpu.CompilerParams(
            collective_id=number, has_side_effects=True, vmem_limit_bytes=48 << 20
        ),
        cost_estimate=pl.CostEstimate(
            flops=microseconds * 10**9, bytes_accessed=2 * moved, transcendentals=0
        ),
        name=name,
    )(*arrays)


def team_semaphores(axes, items):
    return [
        pltpu.SemaphoreType.DMA((len(items), size_of(axes))),
        pltpu.SemaphoreType.DMA((len(items), size_of(axes))),
        pltpu.SemaphoreType.DMA((len(items),)),
    ]


def exchange(items, axes, number, name):
    return call(
        functools.partial(exchange_kernel, axes, tuple(mode for _, mode in items)),
        [array for array, _ in items],
        received(axes, items),
        team_semaphores(axes, items),
        number,
        name,
        20,
    )


def rank_devices():
    yh, x, core = lax.axis_index("yh"), lax.axis_index("x"), lax.axis_index("core")
    across = [lax.rem(x + k, 4) for k in range(4)]
    out = []
    for dy in range(2):
        for dx in range(4):
            for dc in range(2):
                y_at = 1 - yh if dy else yh
                c_at = 1 - core if dc else core
                device = {"yh": y_at, "x": across[dx], "core": c_at}
                out.append((device, y_at * 8 + across[dx] * 2 + c_at))
    return out


def for_each_expert_place(action):
    z = lax.axis_index("zh") * 2 + lax.axis_index("zl")
    rank = rank_devices()

    def of_layer(layer, own):
        high, low = lax.div(layer, 2), lax.rem(layer, 2)
        for k, (device, at) in enumerate(rank):
            action(dict(device, zh=high, zl=low), layer * 16 + at, own and k == 0)

    of_layer(z, True)

    def step(k, carry):
        of_layer(lax.rem(z + k, 4), False)
        return carry

    lax.fori_loop(1, 4, step, 0)


def expert_exchange_kernel(count, modes, *refs):
    every = count + len(modes)
    sources, targets = refs[:every], refs[every : 2 * every]
    send_sem, recv_sem, own_sem, rows_sent, rows_got = refs[2 * every :]
    mine = my_place(DP)
    barrier = pltpu.get_barrier_semaphore()

    def welcome(device, at, own):
        if not own:
            greet(barrier, device)

    for_each_expert_place(welcome)
    pl.semaphore_wait(barrier, 63)
    team = team_copies(
        QUAD, modes, sources[count:], targets[count:], send_sem, recv_sem, own_sem
    )

    def give(device, at, own):
        for item in range(count):
            source, target = sources[item].at[at], targets[item].at[mine]
            if own:
                pltpu.make_async_copy(source, target, rows_got.at[item]).start()
            else:
                send(source, target, rows_sent.at[item], rows_got.at[item], device)

    for_each_expert_place(give)
    for item in range(count):
        sent = sources[item].at[pl.ds(0, 63)]
        pltpu.make_async_copy(sent, sent, rows_sent.at[item]).wait()
        pltpu.make_async_copy(targets[item], targets[item], rows_got.at[item]).wait()
    for copy in team:
        copy.wait()


def expert_exchange(rows, items, number, name):
    rows = [value.reshape(EXPERTS, SLOTS, WIDTH) for value in rows]
    count = len(rows)
    out = call(
        functools.partial(expert_exchange_kernel, count, tuple(mode for _, mode in items)),
        rows + [array for array, _ in items],
        [jax.ShapeDtypeStruct(value.shape, brain) for value in rows] + received(QUAD, items),
        team_semaphores(QUAD, items)
        + [pltpu.SemaphoreType.DMA((count,)), pltpu.SemaphoreType.DMA((count,))],
        number,
        name,
        40 * count,
    )
    rows_got = [value.reshape(EXPERTS * SLOTS, WIDTH) for value in out[:count]]
    return rows_got + list(out[count:])


def rank_gather_kernel(count, modes, *refs):
    every = count + len(modes)
    sources, targets = refs[:count], refs[every : every + count]
    team_sources, team_targets = refs[count:every], refs[every + count : 2 * every]
    send_sem, recv_sem, own_sem, *team_sems = refs[2 * every :]
    yh, x, core = lax.axis_index("yh"), lax.axis_index("x"), lax.axis_index("core")
    right, left, far = lax.rem(x + 1, 4), lax.rem(x + 3, 4), lax.rem(x + 2, 4)
    other = 1 - yh
    to_y, to_right, to_left, to_core = {"yh": other}, {"x": right}, {"x": left}, {"core": 1 - core}
    barrier = pltpu.get_barrier_semaphore()
    for device in (to_y, to_right, to_left, to_core):
        greet(barrier, device)
    pl.semaphore_wait(barrier, 4 + greet_team(barrier, TEAM))

    def slot(y_at, x_at):
        return y_at * 8 + x_at * 2 + core

    sent = []

    def pass_on(item, at, kind, device, source=None):
        target = targets[item].at[at]
        copy = send(
            target if source is None else source,
            target,
            send_sem.at[item, kind],
            recv_sem.at[item, kind],
            device,
        )
        sent.append(copy)
        return copy

    def arrived(item, kind):
        pltpu.make_async_copy(sources[item], sources[item], recv_sem.at[item, kind]).wait()

    items = range(count)
    me = slot(yh, x)
    own = []
    for item in items:
        pass_on(item, me, 0, to_y, sources[item])
        pass_on(item, me, 1, to_right, sources[item])
        pass_on(item, me, 2, to_left, sources[item])
        pass_on(item, me, 7, to_core, sources[item])
        copy = pltpu.make_async_copy(sources[item], targets[item].at[me], own_sem.at[item])
        copy.start()
        own.append(copy)
    team = team_copies(TEAM, modes, team_sources, team_targets, *team_sems)
    steps = (
        (1, slot(yh, left), ((5, to_right), (8, to_core))),
        (0, slot(other, x), ((3, to_right), (4, to_left), (9, to_core))),
        (2, slot(yh, right), ((10, to_core),)),
        (4, slot(other, right), ((6, to_left), (11, to_core))),
        (3, slot(other, left), ((12, to_core),)),
        (5, slot(yh, far), ((13, to_core),)),
        (6, slot(other, far), ((14, to_core),)),
    )
    for kind, at, onward in steps:
        for item in items:
            arrived(item, kind)
            for next_kind, device in onward:
                pass_on(item, at, next_kind, device)
    for item in items:
        for kind in range(7, 15):
            arrived(item, kind)
    for copy in own:
        copy.wait()
    for copy in sent:
        copy.wait_send()
    for copy in team:
        copy.wait()


def rank_gather(arrays, items, number, name):
    count = len(arrays)
    return call(
        functools.partial(rank_gather_kernel, count, tuple(mode for _, mode in items)),
        arrays + [array for array, _ in items],
        [jax.ShapeDtypeStruct((16,) + array.shape, array.dtype) for array in arrays]
        + received(TEAM, items),
        [
            pltpu.SemaphoreType.DMA((count, 15)),
            pltpu.SemaphoreType.DMA((count, 15)),
            pltpu.SemaphoreType.DMA((count,)),
        ]
        + team_semaphores(TEAM, items),
        number,
        name,
        40,
    )


def rank_sum_kernel(count, modes, *refs):
    every = count + len(modes)
    sources, team_sources = refs[:count], refs[count:every]
    targets, team_targets = refs[every : every + count], refs[every + count : 2 * every]
    refs = refs[2 * every :]
    from_core, totals, arrivals = (refs[k * count : (k + 1) * count] for k in range(3))
    send_sem, recv_sem, *team_sems = refs[3 * count :]
    yh, x, core = lax.axis_index("yh"), lax.axis_index("x"), lax.axis_index("core")
    right, left, far = lax.rem(x + 1, 4), lax.rem(x + 3, 4), lax.rem(x + 2, 4)
    other = 1 - yh
    to_y, to_right, to_left, to_core = {"yh": other}, {"x": right}, {"x": left}, {"core": 1 - core}
    barrier = pltpu.get_barrier_semaphore()
    for device in (to_y, to_right, to_left, to_core):
        greet(barrier, device)
    pl.semaphore_wait(barrier, 4 + greet_team(barrier, TEAM))
    items = range(count)
    sent = []

    def pass_on(item, at, kind, device):
        copy = send(
            totals[item].at[at],
            arrivals[item].at[kind],
            send_sem.at[item, kind],
            recv_sem.at[item, kind],
            device,
        )
        sent.append(copy)

    def arrived(item, kind):
        landed = arrivals[item].at[kind]
        pltpu.make_async_copy(landed, landed, recv_sem.at[item, kind]).wait()
        return arrivals[item][kind].astype(single)

    def slot(y_at, x_at):
        return y_at * 4 + x_at

    for item in items:
        sent.append(
            send(
                sources[item].at[:, 1 - core],
                from_core[item],
                send_sem.at[item, 7],
                recv_sem.at[item, 7],
                to_core,
            )
        )
    team = team_copies(TEAM, modes, team_sources, team_targets, *team_sems)
    for item in items:
        landed = from_core[item]
        pltpu.make_async_copy(landed, landed, recv_sem.at[item, 7]).wait()

        def add(at):
            value = sources[item][at, core].astype(single) + from_core[item][at].astype(single)
            totals[item][at] = value.astype(brain)

        add(slot(yh, far))
        pass_on(item, slot(yh, far), 0, to_right)
        add(slot(other, far))
        pass_on(item, slot(other, far), 1, to_left)
        add(slot(other, right))
        pass_on(item, slot(other, right), 3, to_right)
        add(slot(yh, left))
        pass_on(item, slot(yh, left), 5, to_left)
        for at in (slot(yh, right), slot(other, left), slot(yh, x), slot(other, x)):
            add(at)
    for item in items:
        at = slot(yh, right)
        totals[item][at] = (totals[item][at].astype(single) + arrived(item, 0)).astype(brain)
        pass_on(item, at, 2, to_right)
        at = slot(other, left)
        totals[item][at] = (totals[item][at].astype(single) + arrived(item, 1)).astype(brain)
        pass_on(item, at, 4, to_left)
    for item in items:
        at = slot(other, x)
        value = totals[item][at].astype(single) + arrived(item, 3)
        totals[item][at] = (value + arrived(item, 4)).astype(brain)
        pass_on(item, at, 6, to_y)
    for item in items:
        value = totals[item][slot(yh, x)].astype(single) + arrived(item, 5)
        value = value + arrived(item, 2)
        targets[item][...] = (value + arrived(item, 6)).astype(targets[item].dtype)
    for copy in sent:
        copy.wait_send()
    for copy in team:
        copy.wait()


def rank_sum(arrays, items, number, name):
    count = len(arrays)
    arrays = [array.reshape((8, 2) + array.shape[1:]) for array in arrays]
    pieces = [array.shape[2:] for array in arrays]
    scratch = [pltpu.VMEM((8,) + piece, brain) for piece in pieces]
    scratch += [pltpu.VMEM((8,) + piece, brain) for piece in pieces]
    scratch += [pltpu.VMEM((7,) + piece, brain) for piece in pieces]
    scratch += [pltpu.SemaphoreType.DMA((count, 8)), pltpu.SemaphoreType.DMA((count, 8))]
    return call(
        functools.partial(rank_sum_kernel, count, tuple(mode for _, mode in items)),
        arrays + [array for array, _ in items],
        [jax.ShapeDtypeStruct(piece, brain) for piece in pieces] + received(TEAM, items),
        scratch + team_semaphores(TEAM, items),
        number,
        name,
        45,
    )


def dot(left, right):
    return jnp.dot(left, right, preferred_element_type=single)


def dot_t(left, right):
    return lax.dot_general(left, right, (((1,), (1,)), ((), ())), preferred_element_type=single)


def t_dot(left, right):
    return lax.dot_general(left, right, (((0,), (0,)), ((), ())), preferred_element_type=single)


def exact(spec, left, right):
    return jnp.einsum(
        spec, left, right, precision=lax.Precision.HIGHEST, preferred_element_type=single
    )


def rms_scale(value, gain):
    return value * lax.rsqrt(jnp.mean(value * value, axis=-1, keepdims=True) + eps) * gain


def swiglu(value):
    half = value.shape[-1] // 2
    return jax.nn.silu(value[..., :half]) * value[..., half:]


def shuffle_matrix():
    to = jnp.arange(WIDTH, dtype=jnp.int32)
    origin = to // 12 % 8 * 192 + to // 96 * 12 + to % 12
    return (jnp.arange(WIDTH, dtype=jnp.int32)[:, None] == origin[None, :]).astype(brain)


def shuffle(value, matrix):
    return dot(value, matrix).astype(brain)


def unshuffle(value, matrix):
    high = value.astype(brain)
    lower = (value - high.astype(single)).astype(brain)
    both = dot_t(jnp.concatenate([high, lower], axis=0), matrix)
    return both[: value.shape[0]] + both[value.shape[0] :]


def after(values, first):
    return lax.optimization_barrier((values, first))[0]


def pad_rows(value, rows):
    return jnp.pad(value, [(0, 0)] * (value.ndim - 2) + [(0, rows - value.shape[-2]), (0, 0)])


def pad_to(value, rows, columns):
    return jnp.pad(value, ((0, rows - value.shape[0]), (0, columns - value.shape[1])))


def allowed_pairs(seg):
    position = jnp.arange(SEQ, dtype=jnp.int32)
    return (position[:, None] >= position[None, :]) & (seg[..., :, None] == seg[..., None, :])


def product(left, right, dims, precision=None):
    return lax.dot_general(
        left, right, (dims, ((), ())), precision=precision, preferred_element_type=single
    )


def sharp(left, right, dims):
    return product(left, right, dims, lax.Precision.HIGHEST)


def blunt(left, right, dims):
    return product(left.astype(brain), right.astype(brain), dims)


def mamba_parts(zx_ref, masks_ref, same_ref, taps_ref, heads_ref):
    zx = zx_ref[0]
    conv_in = zx[:, INNER : 2 * INNER + 2 * N]
    taps = taps_ref[...]
    same = same_ref[0]
    moved = [conv_in]
    for k in range(1, KW):
        moved.append(pltpu.roll(conv_in, k, 0) * same[:, k : k + 1])
    conv = taps[KW : KW + 1]
    for k in range(KW):
        conv = conv + taps[KW - 1 - k : KW - k] * moved[k]
    gate = jax.nn.sigmoid(conv)
    active = conv * gate
    heads = heads_ref[...]
    raw = zx[:, 2 * INNER + 2 * N :] + heads[0:1]
    step = jnp.maximum(raw, 0.0) + jnp.log1p(jnp.exp(-jnp.abs(raw)))
    rate = step * heads[1:2]
    rows = lax.broadcasted_iota(jnp.int32, (SEQ, SEQ), 0)
    columns = lax.broadcasted_iota(jnp.int32, (SEQ, SEQ), 1)
    lower = (rows >= columns).astype(single)
    total = sharp(lower, rate, ((1,), (0,)))
    total_t = sharp(rate, lower, ((0,), (1,)))
    unit = (rows == columns).astype(single)
    step_t = sharp(step, unit, ((0,), (1,)))
    values = active[:, :INNER]
    in_state, out_state = active[:, INNER : INNER + N], active[:, INNER + N :]
    meeting = sharp(out_state, in_state, ((1,), (1,)))
    allowed = masks_ref[0]
    decays = []
    results = []
    for h in range(HEADS_HERE):
        fall = jnp.exp(jnp.minimum(total[:, h : h + 1] - total_t[h : h + 1], 0.0)) * allowed
        mixing = fall * meeting * step_t[h : h + 1]
        decays.append((fall, mixing))
        results.append(blunt(mixing, values[:, h * P_SIZE : (h + 1) * P_SIZE], ((1,), (0,))))
    result = jnp.concatenate(results, axis=1) + taps[5:6, :INNER] * values
    z = zx[:, :INNER]
    open_z = jax.nn.sigmoid(z)
    return (
        (zx, taps, same, moved, conv, gate, heads, raw, step, step_t, unit, lower),
        (values, in_state, out_state, meeting, decays, result, z, open_z),
    )


def mamba_forward_kernel(zx_ref, masks_ref, same_ref, taps_ref, heads_ref, part_ref, squares_ref):
    (_, taps, *_), (*_, result, z, open_z) = mamba_parts(
        zx_ref, masks_ref, same_ref, taps_ref, heads_ref
    )
    gated = result * (z * open_z)
    part_ref[0] = (gated * taps[6:7, :INNER]).astype(brain)
    sums = sharp(jnp.ones((8, INNER), single), gated * gated, ((1,), (1,)))
    squares_ref[0] = jnp.concatenate([sums, jnp.zeros((8, 128 - SEQ), single)], axis=1)


def mamba_backward_kernel(
    zx_ref, masks_ref, same_ref, taps_ref, heads_ref, d_yn_ref, scalars_ref, d_zx_ref, yn_ref, sums_ref
):
    first, second = mamba_parts(zx_ref, masks_ref, same_ref, taps_ref, heads_ref)
    (zx, taps, same, moved, conv, gate, heads, raw, step, step_t, unit, lower) = first
    (values, in_state, out_state, meeting, decays, result, z, open_z) = second
    scalars = sharp(unit, scalars_ref[0][:, :SEQ], ((1,), (1,)))
    inverse, along = scalars[:, 0:1], scalars[:, 1:2]
    gain, skip = taps[6:7, :INNER], taps[5:6, :INNER]
    d_yn = d_yn_ref[0]
    shut = z * open_z
    gated = result * shut
    scaled = gated * inverse
    yn_ref[0] = (scaled * gain).astype(brain)
    d_gain = jnp.sum(d_yn * scaled, axis=0, keepdims=True)
    d_gated = inverse * gain * d_yn - gated * along
    d_z = d_gated * result * (open_z * (1.0 + z * (1.0 - open_z)))
    d_result = d_gated * shut
    d_skip = jnp.sum(d_result * values, axis=0, keepdims=True)
    lanes = lax.broadcasted_iota(jnp.int32, (1, 128), 1)
    rows = lax.broadcasted_iota(jnp.int32, (128, 1), 0)
    d_meeting = jnp.zeros((SEQ, SEQ), single)
    by_row = jnp.zeros((SEQ, 128), single)
    by_column = jnp.zeros((128, SEQ), single)
    d_step_t = jnp.zeros((128, SEQ), single)
    d_values = []
    for h in range(HEADS_HERE):
        fall, mixing = decays[h]
        own = slice(h * P_SIZE, (h + 1) * P_SIZE)
        d_mixing = blunt(d_result[:, own], values[:, own], ((1,), (1,)))
        d_values.append(blunt(mixing, d_result[:, own], ((0,), (0,))))
        spread = d_mixing * fall
        d_meeting = d_meeting + spread * step_t[h : h + 1]
        spread = spread * meeting
        moving = spread * step_t[h : h + 1]
        by_row = by_row + jnp.sum(moving, axis=1, keepdims=True) * (lanes == h).astype(single)
        at = (rows == h).astype(single)
        by_column = by_column + at * jnp.sum(moving, axis=0, keepdims=True)
        d_step_t = d_step_t + at * jnp.sum(spread, axis=0, keepdims=True)
    d_total = by_row - sharp(unit, by_column, ((1,), (1,)))
    d_rate = sharp(lower, d_total, ((0,), (0,)))
    d_step = sharp(unit, d_step_t, ((1,), (1,))) + d_rate * heads[1:2]
    d_raw = d_step * jax.nn.sigmoid(raw)
    d_decay = jnp.sum(d_rate * step, axis=0, keepdims=True) * heads[1:2]
    d_active = jnp.concatenate(
        [
            jnp.concatenate(d_values, axis=1) + skip * d_result,
            sharp(d_meeting, out_state, ((0,), (0,))),
            sharp(d_meeting, in_state, ((1,), (0,))),
        ],
        axis=1,
    )
    d_conv = d_active * (gate * (1.0 + conv * (1.0 - gate)))
    d_taps = [jnp.sum(d_conv * moved[KW - 1 - k], axis=0, keepdims=True) for k in range(KW)]
    d_in = taps[KW - 1 : KW] * d_conv
    for k in range(1, KW):
        d_in = d_in + pltpu.roll(
            taps[KW - 1 - k : KW - k] * (d_conv * same[:, k : k + 1]), SEQ - k, 0
        )
    d_zx_ref[0] = jnp.concatenate([d_z, d_in, d_raw], axis=1).astype(brain)
    wide = INNER + 2 * N

    def widen(value):
        return jnp.concatenate(
            [value, jnp.zeros((1, wide - value.shape[1]), single)], axis=1
        )

    sums = jnp.concatenate(
        d_taps
        + [jnp.sum(d_conv, axis=0, keepdims=True), widen(d_skip), widen(d_gain)]
        + [widen(jnp.sum(d_raw, axis=0, keepdims=True)), widen(d_decay)]
        + [jnp.zeros((7, wide), single)],
        axis=0,
    )

    @pl.when(pl.program_id(0) == 0)
    def _():
        sums_ref[...] = jnp.zeros_like(sums_ref)

    sums_ref[...] += sums


def by_sequence(kernel, arrays, fixed, shapes, total_shapes, name):
    def whole(shape):
        return pl.BlockSpec(shape, lambda n: (0,) * len(shape))

    def one(shape):
        return pl.BlockSpec((1,) + shape[1:], lambda n: (n,) + (0,) * (len(shape) - 1))

    return pl.pallas_call(
        kernel,
        grid=(PARTS,),
        out_shape=shapes + total_shapes,
        in_specs=[
            whole(array.shape) if place in fixed else one(array.shape)
            for place, array in enumerate(arrays)
        ],
        out_specs=[one(s.shape) for s in shapes] + [whole(s.shape) for s in total_shapes],
        compiler_params=pltpu.CompilerParams(vmem_limit_bytes=32 << 20),
        name=name,
    )(*arrays)


def attend_scores(queries, keys, seg):
    scores = exact("nird,njd->nrij", queries, keys) * HEAD_SIZE ** (-0.5)
    scores = jnp.where(allowed_pairs(seg)[:, None], scores, -1e30)
    return jax.nn.softmax(scores, axis=-1)


def attend_mix(probs, values):
    return exact("nrij,njd->nird", probs, values)


def per_device(
    block_input,
    cotangent,
    segments,
    routes,
    in_proj,
    conv_taps,
    conv_bias,
    step_bias,
    decay_log,
    skip_weight,
    norm_gain,
    out_proj,
    query_proj,
    key_value_projection,
    attn_out_proj,
    norm_gains,
    router,
    shared_in,
    shared_out,
    experts_in,
    experts_out,
):
    phase = lax.axis_index("phase")
    first_phase = phase == 0
    zl = lax.axis_index("zl")
    team = phase * 4 + lax.axis_index("zh") * 2 + zl

    def mine(value):
        return lax.dynamic_index_in_dim(value, phase, 0, keepdims=False)

    start = mine(block_input)
    cot = mine(cotangent)
    seg = mine(segments)
    route_rows = mine(routes)

    both_ways = [(0, 1), (1, 0)]
    w_first, w_second = experts_in[0, 0], experts_out[0, 0]

    z_piece = in_proj[:, :DI].reshape(12, PARTS, INNER).transpose(1, 0, 2)
    x_piece = in_proj[:, DI : 2 * DI].reshape(12, PARTS, INNER).transpose(1, 0, 2)
    state_piece = jnp.broadcast_to(in_proj[None, :, 2 * DI : 2 * DI + 2 * N], (PARTS, 12, 2 * N))
    step_piece = in_proj[:, 2 * DI + 2 * N :].reshape(12, PARTS, HEADS_HERE).transpose(1, 0, 2)
    step_piece = jnp.pad(step_piece, ((0, 0), (0, 0), (0, 128 - HEADS_HERE)))
    q_piece = query_proj.reshape(12, 4, 384).transpose(1, 0, 2)
    kv_piece = key_value_projection.reshape(12, 2, 4, 128).transpose(2, 0, 1, 3).reshape(4, 12, 256)
    qkv_piece = jnp.repeat(jnp.concatenate([q_piece, kv_piece], axis=2), 2, axis=0)
    in_piece = pad_rows(jnp.concatenate([z_piece, x_piece, state_piece, step_piece], axis=2), 16)
    qkv_piece = pad_rows(qkv_piece, 16)
    sin_piece = shared_in[0].reshape(24, 2, 4, 256).transpose(2, 0, 1, 3).reshape(4, 24, 512)
    sin_piece = pad_rows(jnp.concatenate([sin_piece, sin_piece], axis=0), 32)
    sout_piece = jnp.broadcast_to(shared_out, (2, 16, WIDTH))
    attn_piece = jnp.broadcast_to(pad_rows(attn_out_proj, 16)[None], (2, 16, WIDTH))
    mixing = shuffle_matrix()
    rest = jnp.concatenate(
        [conv_taps.reshape(-1), conv_bias, norm_gain, norm_gains[0].reshape(-1)]
    )
    rest = jnp.pad(rest, (0, 512 - rest.shape[0])).reshape(4, 128)
    small = jnp.concatenate([router[0].reshape(12, 128), rest], axis=0)
    seg_piece = pad_to(seg, 8, 128)
    in_got, sin_got, sout_got, small_got, seg_got = exchange(
        [
            (in_piece, "swap"),
            (sin_piece, "swap"),
            (sout_piece, "phase"),
            (small, "gather"),
            (seg_piece, "gather"),
        ],
        TEAM,
        0,
        "team_start",
    )
    seg_all = seg_got[:, 0, :SEQ]
    sin_got = sin_got[:, :24].reshape(2, 96, 512)

    def to_other_phase(value):
        return lax.ppermute(value, "phase", both_ways)

    half = WIDTH // 2
    w_second_far = to_other_phase(w_second)
    in_rows, w_second_far = lax.optimization_barrier(
        (in_got[:, :12].reshape(96, IN_COLS), w_second_far)
    )
    w_first_far = [to_other_phase(after(w_first[:half], w_second_far))]
    w_in, small_all, w_out, start_all, qkv_got, attn_got = rank_gather(
        [in_rows, small_got.reshape(128, 128), pad_rows(out_proj, 32)],
        [(shuffle(start, mixing), "gather"), (qkv_piece, "swap"), (attn_piece, "zl")],
        1,
        "rank_weights",
    )
    w_in = w_in.reshape(WIDTH, IN_COLS)
    w_out = w_out[:, :24].reshape(INNER, WIDTH)
    later_wide = jnp.concatenate([qkv_got[:, :12].reshape(96, QKV_COLS), sin_got[1]], axis=1)
    later_tall = jnp.concatenate([attn_got[:, :12].reshape(24, WIDTH), sout_got[1]], axis=0)
    start_all, first_piece = lax.optimization_barrier((start_all, w_first_far[0]))
    w_first_far = [first_piece, to_other_phase(after(w_first[half:], first_piece))]
    later_wide = lax.all_gather(later_wide, RANK, axis=0)
    later_tall = lax.all_gather(later_tall, RANK, axis=0)
    w_qkv = later_wide[:, :, :QKV_COLS].reshape(WIDTH, QKV_COLS)
    w_attn = later_tall[:, :24].reshape(16, 2, 12, WIDTH).transpose(1, 0, 2, 3)
    w_attn = w_attn.reshape(384, WIDTH)

    def hidden_in(value):
        return value.reshape(16, 4, 24, 512).transpose(1, 0, 2, 3).reshape(WIDTH, 512)

    small_all = small_all.reshape(16, 2, 4, 16, 128)
    router_full = small_all[:, :, :, :12].reshape(16, 2, 4, 24, EXPERTS).transpose(1, 2, 0, 3, 4)
    router_full = router_full.reshape(2, WIDTH, EXPERTS)
    rest_all = small_all[:, :, :, 12:].reshape(16, 2, 4, 512)
    conv_full = rest_all[..., :130].reshape(16, 2, 4, 5, 26).transpose(3, 1, 2, 0, 4)
    conv_full = conv_full.reshape(5, CONVW).astype(single)
    gain_here = rest_all[..., 130:154].reshape(16, 8, 24)
    gain_here = lax.dynamic_index_in_dim(gain_here, team, 1, keepdims=False)
    gain_here = gain_here.reshape(INNER).astype(single)
    gains = rest_all[..., 154:202].reshape(16, 2, 4, 2, 24).transpose(1, 3, 2, 0, 4)
    gains = gains.reshape(2, 2, WIDTH).astype(single)
    conv_here = jnp.concatenate(
        [lax.dynamic_slice_in_dim(conv_full[:, :DI], team * INNER, INNER, 1), conv_full[:, DI:]],
        axis=1,
    )

    def heads_of(value):
        return lax.dynamic_slice_in_dim(value, team * HEADS_HERE, HEADS_HERE, 0)

    skip_wide = jnp.repeat(heads_of(skip_weight), P_SIZE)
    columns = jnp.stack([jnp.pad(skip_wide, (0, 2 * N)), jnp.pad(gain_here, (0, 2 * N))])
    taps_here = jnp.concatenate([conv_here, columns, jnp.zeros((1, INNER + 2 * N), single)], axis=0)
    heads_here = jnp.stack([heads_of(step_bias), -jnp.exp(heads_of(decay_log))])
    heads_here = pad_to(heads_here, 8, 128)
    allowed_all = allowed_pairs(seg_all).astype(single)
    same_all = [
        jnp.pad(seg_all[:, k:] == seg_all[:, : SEQ - k], ((0, 0), (k, 0))) for k in range(KW)
    ]
    same_all = jnp.pad(jnp.stack(same_all, axis=2).astype(single), ((0, 0), (0, 0), (0, 128 - KW)))

    expert_ids = jnp.arange(EXPERTS, dtype=jnp.int32)
    named = jnp.any(route_rows[:, :, None] == expert_ids, axis=1)
    position = jnp.arange(SEQ, dtype=jnp.int32)
    earlier = (position[:, None] > position[None, :]).astype(brain)
    slot = dot(earlier, named.astype(brain))
    slot = jnp.where(named, slot, -1.0).astype(brain)
    cell = jnp.arange(EXPERTS * SLOTS, dtype=jnp.int32)
    spread = (cell[None, :] // SLOTS == expert_ids[:, None]).astype(brain)
    taken = dot(slot, spread) == (cell % SLOTS).astype(single)
    taken_b = taken.astype(brain)

    def of_block(s):
        own = phase == s
        return (
            jnp.where(own, w_first, w_first_far),
            jnp.where(own, w_second, w_second_far),
        )

    def moe_open(s, hidden):
        normed = rms_scale(hidden, gains[s, 1]).astype(brain)
        logits = dot(normed, router_full[s])
        top = jnp.max(jnp.where(named, logits, -jnp.inf), axis=1, keepdims=True)
        weight = jnp.where(named, jnp.exp(logits - top), 0.0)
        gates = weight / jnp.sum(weight, axis=1, keepdims=True)
        gates_wide = jnp.where(taken, exact("ie,ec->ic", gates, spread.astype(single)), 0.0)
        return normed, gates, gates_wide, t_dot(taken_b, normed).astype(brain)

    def moe_experts(weights, rows_in):
        both = dot(rows_in, weights[0])
        hid = swiglu(both).astype(brain)
        return both, hid, dot(hid, weights[1]).astype(brain)

    def moe_shared(s, normed_all):
        both = dot(normed_all, sin_full[s])
        hid = swiglu(both).astype(brain)
        part = dot(hid, sout_full[s]).astype(brain)
        return both, hid, part.reshape(4, SEQ, WIDTH)

    def moe_join(hidden, gates_wide, back, shared_got):
        high = gates_wide.astype(brain)
        lower = (gates_wide - high.astype(single)).astype(brain)
        moe = dot(high, back) + dot(lower, back)
        return (hidden + moe + jnp.sum(shared_got.astype(single), axis=0)).astype(brain)

    def back_open(d_out, gates_wide):
        gate_cell = jnp.sum(gates_wide, axis=0)
        return (t_dot(taken_b, d_out) * gate_cell[:, None]).astype(brain)

    def back_experts(weights, d_answer, both):
        d_hid = dot_t(d_answer, weights[1])
        d_both = jax.vjp(swiglu, both)[1](d_hid)[0].astype(brain)
        return d_both, dot_t(d_both, weights[0]).astype(brain)

    def back_shared(s, d_out_all, normed_all, both, hid):
        d_hid = dot_t(d_out_all, sout_full[s])
        d_sout = t_dot(hid, d_out_all)
        d_both = jax.vjp(swiglu, both)[1](d_hid)[0].astype(brain)
        d_sin = t_dot(normed_all, d_both)
        d_part = dot_t(d_both, sin_full[s]).astype(brain).reshape(4, SEQ, WIDTH)
        return d_sin, d_sout, d_part

    def back_join(s, d_out, hidden, normed, gates, back, returned, d_shared_got):
        d_cells = jnp.where(taken, dot_t(d_out, back), 0.0)
        d_gates = exact("ic,ec->ie", d_cells, spread.astype(single))
        d_logits = gates * (d_gates - jnp.sum(gates * d_gates, axis=1, keepdims=True))
        d_normed = exact("ie,we->iw", d_logits, router_full[s].astype(single))
        d_router = exact("iw,ie->we", normed.astype(single), d_logits)
        d_normed = d_normed + dot(taken_b, returned) + jnp.sum(d_shared_got.astype(single), axis=0)
        d_hidden, d_gain = jax.vjp(rms_scale, hidden, gains[s, 1])[1](d_normed)
        return d_hidden + d_out.astype(single), d_gain, d_router

    def shared_in_parts(value):
        return value.astype(brain).reshape(4, 16, 24, 512).transpose(1, 0, 2, 3).reshape(16, 96, 512)

    u0 = start.astype(single)
    shuffled_gain = shuffle(gains[0, 0][None].astype(brain), mixing)[0].astype(single)
    n1_all = rms_scale(start_all.astype(single), shuffled_gain).astype(brain)
    n1_all = n1_all.reshape(PARTS * SEQ, WIDTH)
    zx = dot(n1_all, w_in).reshape(PARTS, SEQ, IN_COLS)

    core_inputs = [zx, allowed_all, same_all, taps_here, heads_here]
    part, squares = by_sequence(
        mamba_forward_kernel,
        core_inputs,
        (3, 4),
        [
            jax.ShapeDtypeStruct((PARTS, SEQ, INNER), brain),
            jax.ShapeDtypeStruct((PARTS, 8, 128), single),
        ],
        [],
        "mamba_forward",
    )
    part = dot(part.reshape(PARTS * SEQ, INNER), w_out)
    part = part.astype(brain).reshape(PARTS, SEQ, WIDTH)
    part, second_piece = lax.optimization_barrier((part, w_first_far[1]))
    w_first_far = jnp.concatenate([w_first_far[0], second_piece], axis=0)
    sin_all, sout_all, part_got, squares_got = rank_gather(
        [sin_got[0], sout_got[0]], [(part, "swap"), (squares, "swap")], 2, "team_mixed_0"
    )
    sin_full = (hidden_in(sin_all), hidden_in(later_wide[:, :, QKV_COLS:]))
    sout_full = (sout_all.reshape(256, WIDTH), later_tall[:, 24:].reshape(256, WIDTH))
    mean_square = jnp.sum(squares_got[:, 0, :SEQ], axis=0) / DI
    inverse = lax.rsqrt(mean_square + eps)
    mixed0 = jnp.sum(part_got.astype(single), axis=0) * inverse[:, None]
    hidden0 = u0 + mixed0
    normed0, gates0, gates_wide0, rows_out0 = moe_open(0, hidden0)
    rows_in0, normed_all0 = expert_exchange([rows_out0], [(normed0, "gather")], 3, "spread_0")
    normed_all0 = normed_all0.reshape(4 * SEQ, WIDTH)
    weights0 = of_block(0)
    sboth0, shid0, shared_part0 = moe_shared(0, normed_all0)
    both0, hid0, answer0 = moe_experts(weights0, rows_in0)
    back0, shared_got0 = expert_exchange([answer0], [(shared_part0, "swap")], 4, "collect_0")
    out0 = moe_join(hidden0, gates_wide0, back0, shared_got0)

    u1 = out0.astype(single)
    n1 = rms_scale(u1, gains[1, 0]).astype(brain)
    (n1_half,) = exchange([(shuffle(n1, mixing), "gather")], HALF, 5, "half_n1")
    n1_half = n1_half.reshape(4 * SEQ, WIDTH)
    seg_half = lax.dynamic_index_in_dim(seg_all.reshape(4, 2, SEQ), zl, 1, keepdims=False)
    qkv = dot(n1_half, w_qkv).astype(brain).astype(single).reshape(4, SEQ, QKV_COLS)
    queries = qkv[..., :384].reshape(4, SEQ, 3, HEAD_SIZE)
    keys, values = qkv[..., 384:512], qkv[..., 512:]
    probs, score_pull = jax.vjp(lambda q, k: attend_scores(q, k, seg_half), queries, keys)
    heads, mix_pull = jax.vjp(attend_mix, probs.astype(brain).astype(single), values)
    heads = heads.astype(brain).reshape(4 * SEQ, 384)
    part1 = dot(heads, w_attn).astype(brain).reshape(4, SEQ, WIDTH)
    (part1_got,) = exchange([(part1, "swap")], HALF, 6, "half_mixed")
    mixed1 = jnp.sum(part1_got.astype(single), axis=0)
    hidden1 = u1 + mixed1

    normed1, gates1, gates_wide1, rows_out1 = moe_open(1, hidden1)
    rows_in1, d_answer1, normed_all1, cot_all = expert_exchange(
        [rows_out1, back_open(cot, gates_wide1)],
        [(normed1, "gather"), (cot, "gather")],
        7,
        "spread_1",
    )
    normed_all1 = normed_all1.reshape(4 * SEQ, WIDTH)
    cot_all = cot_all.reshape(4 * SEQ, WIDTH)
    weights1 = of_block(1)
    sboth1, shid1, shared_part1 = moe_shared(1, normed_all1)
    d_sin1, d_sout1, d_shared1 = back_shared(1, cot_all, normed_all1, sboth1, shid1)
    both1, hid1, answer1 = moe_experts(weights1, rows_in1)
    d_both1, d_rows1 = back_experts(weights1, d_answer1, both1)
    back1, returned1, shared_got1, d_shared_got1 = expert_exchange(
        [answer1, d_rows1], [(shared_part1, "swap"), (d_shared1, "swap")], 8, "collect_1"
    )
    out1 = moe_join(hidden1, gates_wide1, back1, shared_got1)

    d_hid1, d_gain11, d_router1 = back_join(
        1, cot, hidden1, normed1, gates1, back1, returned1, d_shared_got1
    )
    (d_mixed1,) = exchange([(d_hid1.astype(brain), "gather")], HALF, 11, "half_dmixed")
    d_mixed1 = d_mixed1.reshape(4 * SEQ, WIDTH)
    d_heads = dot_t(d_mixed1, w_attn).reshape(4, SEQ, 3, HEAD_SIZE)
    d_attn = t_dot(heads, d_mixed1)
    d_probs, d_values = mix_pull(d_heads)
    d_queries, d_keys = score_pull(d_probs)
    d_qkv = jnp.concatenate([d_queries.reshape(4, SEQ, 384), d_keys, d_values], axis=2)
    d_qkv = d_qkv.astype(brain).reshape(4 * SEQ, QKV_COLS)
    d_w_qkv = t_dot(n1_half, d_qkv)
    d_n1_part = dot_t(d_qkv, w_qkv).astype(brain).reshape(4, SEQ, WIDTH)
    grads_wide = jnp.concatenate(
        [d_w_qkv.astype(brain).reshape(16, 96, QKV_COLS), shared_in_parts(d_sin1)], axis=2
    )
    attn_part = d_attn.astype(brain).reshape(2, 16, 12, WIDTH).transpose(1, 0, 2, 3)
    grads_tall = jnp.concatenate(
        [
            attn_part.reshape(16, 24, WIDTH),
            d_sout1.astype(brain).reshape(16, 16, WIDTH),
            jnp.zeros((16, 8, WIDTH), brain),
        ],
        axis=1,
    )
    d_n1_part, grads_wide = lax.optimization_barrier((d_n1_part, grads_wide))
    grads_wide = lax.psum_scatter(grads_wide, RANK, scatter_dimension=0, tiled=True)[0]
    (d_n1_got,) = exchange([(d_n1_part, "swap")], HALF, 12, "half_dn1")
    d_n1 = unshuffle(jnp.sum(d_n1_got.astype(single), axis=0), mixing)
    d_u1, d_gain10 = jax.vjp(rms_scale, u1, gains[1, 0])[1](d_n1)
    d_u1 = (d_u1 + d_hid1).astype(brain)

    d_answer0, d_out0_all = expert_exchange(
        [back_open(d_u1, gates_wide0)], [(d_u1, "gather")], 13, "spread_back_0"
    )
    d_out0_all = d_out0_all.reshape(4 * SEQ, WIDTH)
    d_sin0, d_sout0, d_shared0 = back_shared(0, d_out0_all, normed_all0, sboth0, shid0)
    d_both0, d_rows0 = back_experts(weights0, d_answer0, both0)
    expert0 = (rows_in0, d_both0, hid0, d_answer0)
    expert1 = (rows_in1, d_both1, hid1, d_answer1)
    give_rows, give_both, give_hid, give_answer = (
        jnp.where(first_phase, b, a) for a, b in zip(expert0, expert1)
    )
    give_first = t_dot(give_rows, give_both).astype(brain)
    give_second = t_dot(give_hid, give_answer).astype(brain)
    d_rows0, give_first, give_second = lax.optimization_barrier((d_rows0, give_first, give_second))
    far_second = to_other_phase(give_second)
    returned0, d_shared_got0 = expert_exchange(
        [d_rows0], [(d_shared0, "swap")], 14, "collect_back_0"
    )
    d_hid0, d_gain01, d_router0 = back_join(
        0, d_u1, hidden0, normed0, gates0, back0, returned0, d_shared_got0
    )
    d_mixed0 = d_hid0.astype(brain)
    along = jnp.sum(d_mixed0.astype(single) * mixed0, axis=1)
    scalars = jnp.stack([inverse, inverse * inverse * along / DI])
    d_mixed0, far_second = lax.optimization_barrier((d_mixed0, far_second))
    grads_tall, sin_part0, sout_part0, d_mixed0, scalars_all = rank_sum(
        [grads_tall, shared_in_parts(d_sin0), d_sout0.astype(brain).reshape(16, 16, WIDTH)],
        [(d_mixed0, "gather"), (pad_to(scalars, 8, 128), "gather")],
        15,
        "team_dmixed",
    )
    far_first = [to_other_phase(after(give_first[:half], d_mixed0))]
    d_mixed0 = d_mixed0.reshape(PARTS * SEQ, WIDTH)
    d_yn = dot_t(d_mixed0, w_out).reshape(PARTS, SEQ, INNER)
    d_zx, yn, core_sums = by_sequence(
        mamba_backward_kernel,
        core_inputs + [d_yn, scalars_all],
        (3, 4),
        [
            jax.ShapeDtypeStruct((PARTS, SEQ, IN_COLS), brain),
            jax.ShapeDtypeStruct((PARTS, SEQ, INNER), brain),
        ],
        [jax.ShapeDtypeStruct((16, INNER + 2 * N), single)],
        "mamba_backward",
    )
    d_w_out = t_dot(yn.reshape(PARTS * SEQ, INNER), d_mixed0)
    d_zx = d_zx.reshape(PARTS * SEQ, IN_COLS)
    d_norm_gain = core_sums[6, :INNER]
    d_skip = jnp.sum(core_sums[5, :INNER].reshape(HEADS_HERE, P_SIZE), axis=1)
    d_step, d_decay = core_sums[7, :HEADS_HERE], core_sums[8, :HEADS_HERE]
    d_w_in = t_dot(n1_all, d_zx)
    d_n1_part0 = dot_t(d_zx, w_in).astype(brain)
    shuffled = start_all.astype(single)
    shuffled = shuffled * lax.rsqrt(jnp.mean(shuffled * shuffled, axis=-1, keepdims=True) + eps)
    d_gain00 = jnp.sum(
        shuffled.reshape(PARTS * SEQ, WIDTH) * d_n1_part0.astype(single), axis=0
    )
    d_gain00 = d_gain00.reshape(16, 8, 12).transpose(1, 0, 2).reshape(WIDTH)
    d_n1_part0 = d_n1_part0.reshape(PARTS, SEQ, WIDTH)
    d_n1_part0, grads_wide, first_piece = lax.optimization_barrier(
        (d_n1_part0, grads_wide, far_first[0])
    )

    qkv_part = grads_wide[:, :QKV_COLS].reshape(PARTS, 12, QKV_COLS)
    sin_part1 = grads_wide[:, QKV_COLS:].reshape(4, 24, 512)
    attn_part, sout_part1 = grads_tall[:24].reshape(2, 12, WIDTH), grads_tall[24:40]

    conv_grads = core_sums[: KW + 1]
    conv_all = jnp.concatenate(
        [
            lax.dynamic_update_slice_in_dim(
                jnp.zeros((KW + 1, DI), single), conv_grads[:, :INNER], team * INNER, 1
            ),
            conv_grads[:, INNER:],
        ],
        axis=1,
    )
    conv_all = conv_all.reshape(5, 8, 16, 26).transpose(2, 1, 0, 3).reshape(16, 8, 130)
    head_all = lax.dynamic_update_slice_in_dim(
        jnp.zeros((3, H), single), jnp.stack([d_step, d_decay, d_skip]), team * HEADS_HERE, 1
    )
    head_all = jnp.broadcast_to(head_all.reshape(1, 1, 3 * H), (16, 8, 3 * H))
    gain_all = lax.dynamic_update_slice_in_dim(
        jnp.zeros((16, 8, 24), single), d_norm_gain.reshape(16, 1, 24), team, 1
    )
    d_gains = jnp.stack([jnp.stack([d_gain00, d_gain01]), jnp.stack([d_gain10, d_gain11])])
    d_gains = d_gains.reshape(2, 2, 4, 16, 24).transpose(3, 0, 2, 1, 4).reshape(16, 8, 48)
    d_router = jnp.stack([d_router0, d_router1]).reshape(2, 4, 16, 24 * EXPERTS)
    d_router = d_router.transpose(2, 0, 1, 3).reshape(16, 8, 24 * EXPERTS)
    small_grads = jnp.concatenate([d_router, conv_all, gain_all, d_gains, head_all], axis=2)
    small_grads = jnp.pad(small_grads, ((0, 0), (0, 0), (0, 2048 - small_grads.shape[2])))
    small_grads = small_grads.astype(brain).reshape(16, 128, 128)
    main_part, out_proj_grad, small_part, d_n1_got0, phase_outputs = rank_sum(
        [
            d_w_in.astype(brain).reshape(16, 96, IN_COLS),
            pad_rows(d_w_out.astype(brain).reshape(16, 24, WIDTH), 32),
            small_grads,
        ],
        [(d_n1_part0, "swap"), (jnp.stack([out0, out1]), "phase")],
        17,
        "rank_grads",
    )
    main_part = main_part.reshape(PARTS, 12, IN_COLS)
    sin_part0 = sin_part0.reshape(4, 24, 512)
    d_n1_0 = unshuffle(jnp.sum(d_n1_got0.astype(single), axis=0), mixing)
    (d_u0,) = jax.vjp(lambda value: rms_scale(value, gains[0, 0]), u0)[1](d_n1_0)
    d_u0 = d_u0 + d_hid0

    rows_kept, d_both_kept, hid_kept, d_answer_kept = (
        jnp.where(first_phase, a, b) for a, b in zip(expert0, expert1)
    )
    second_piece = to_other_phase(after(give_first[half:], main_part))
    far_first = jnp.concatenate([first_piece, second_piece], axis=0)
    experts_in_grad = t_dot(rows_kept, d_both_kept) + far_first.astype(single)
    experts_out_grad = t_dot(hid_kept, d_answer_kept) + far_second.astype(single)

    main_end, qkv_end, sin_end, sout_end, attn_end, small_end, input_grads = exchange(
        [
            (pad_rows(main_part, 16), "swap"),
            (pad_rows(qkv_part, 16), "swap"),
            (pad_rows(jnp.concatenate([sin_part0, sin_part1], axis=0), 32), "swap"),
            (jnp.stack([sout_part0, sout_part1]), "phase"),
            (pad_rows(attn_part, 16), "zl"),
            (small_part.reshape(PARTS, 16, 128), "swap"),
            (jnp.stack([d_u0, d_u1.astype(single)]), "phase"),
        ],
        TEAM,
        18,
        "team_end",
    )
    rows_end = main_end[:, :12].astype(single)

    def side_by_side(value):
        return value.transpose(1, 0, 2).reshape(value.shape[1], -1)

    in_proj_grad = jnp.concatenate(
        [
            side_by_side(rows_end[:, :, :INNER]),
            side_by_side(rows_end[:, :, INNER : 2 * INNER]),
            jnp.sum(rows_end[:, :, 2 * INNER : 2 * INNER + 2 * N], axis=0),
            side_by_side(
                rows_end[:, :, 2 * INNER + 2 * N : 2 * INNER + 2 * N + HEADS_HERE]
            ),
        ],
        axis=1,
    )
    small_end = jnp.sum(small_end.astype(single), axis=0).reshape(2048)
    router_grad = small_end[: 24 * EXPERTS].reshape(1, 24, EXPERTS)
    at = 24 * EXPERTS
    conv_end = small_end[at : at + 130].reshape(5, 26)
    at += 130
    norm_gain_grad = small_end[at : at + 24]
    at += 24
    norm_gains_grad = small_end[at : at + 48].reshape(1, 2, 24)
    at += 48
    heads_end = small_end[at : at + 3 * H].reshape(3, H)
    qkv_end = qkv_end[:, :12].astype(single).reshape(4, 2, 12, QKV_COLS)
    qkv_end = jnp.sum(qkv_end, axis=1)
    query_grad = side_by_side(qkv_end[:, :, :384])
    kv_grad = qkv_end[:, :, 384:].reshape(4, 12, 2, 128).transpose(1, 2, 0, 3).reshape(12, 1024)
    sin_end = jnp.sum(sin_end[:, :24].astype(single).reshape(2, 4, 24, 2, 256), axis=0)
    shared_in_grad = sin_end.transpose(1, 2, 0, 3).reshape(1, 24, 2048)
    shared_out_grad = jnp.sum(sout_end.astype(single), axis=0)[None]
    attn_out_grad = jnp.sum(attn_end[:, :12].astype(single), axis=0)

    return (
        phase_outputs[None],
        input_grads[None],
        in_proj_grad,
        conv_end[:KW],
        conv_end[KW],
        heads_end[0],
        heads_end[1],
        heads_end[2],
        norm_gain_grad,
        out_proj_grad[:24].astype(single),
        query_grad,
        kv_grad,
        attn_out_grad,
        norm_gains_grad,
        router_grad,
        shared_in_grad,
        shared_out_grad,
        experts_in_grad[None, None],
        experts_out_grad[None, None],
    )


def solution(mesh):
    fine = Mesh(mesh.devices.reshape(tuple(SIZES.values())), ALL)
    in_specs = (
        P(None, DP, None),
        P(None, DP, None),
        P(None, DP, None),
        P(None, DP, None),
        P(ALL, None),
        P(None, ALL),
        P(ALL),
        P(),
        P(),
        P(),
        P(ALL),
        P(ALL, None),
        P(ALL, None),
        P(ALL, None),
        P(ALL, None),
        P("phase", None, DP),
        P("phase", DP, None),
        P("phase", DP, None),
        P("phase", DP, None),
        P("phase", DP, None, None),
        P("phase", DP, None, None),
    )
    out_specs = (
        P("phase", None, DP, None),
        P("phase", None, DP, None),
        P(ALL, None),
        P(None, ALL),
        P(ALL),
        P(),
        P(),
        P(),
        P(ALL),
        P(ALL, None),
        P(ALL, None),
        P(ALL, None),
        P(ALL, None),
        P("phase", None, DP),
        P("phase", DP, None),
        P("phase", DP, None),
        P("phase", DP, None),
        P("phase", DP, None, None),
        P("phase", DP, None, None),
    )
    return jax.shard_map(
        per_device, mesh=fine, in_specs=in_specs, out_specs=out_specs, check_vma=False
    )
```

```python
import functools

import jax
import jax.numpy as jnp
from jax import lax
from jax.experimental import pallas as pl
from jax.experimental.pallas import tpu as pltpu
from jax.sharding import Mesh
from jax.sharding import PartitionSpec as P

H = 48
P_SIZE = 64
N = 128
KW = 4
QUERY_HEADS = 12
KEY_VALUE_HEADS = 4
HEAD_SIZE = 128
DI = 3072
CONVW = 3328
WIDTH = 1536
SEQ = 64
EXPERTS = 64
SLOTS = 8
PARTS = 8
HEADS_HERE = H // PARTS
INNER = DI // PARTS
IN_COLS = 1152
QKV_COLS = 640

SIZES = {"phase": 2, "zh": 2, "zl": 2, "yh": 2, "x": 4, "core": 2}
TEAM = ("phase", "zh", "zl")
HALF = ("phase", "zh")
QUAD = ("zh", "zl")
RANK = ("yh", "x", "core")
DP = ("zh", "zl", "yh", "x", "core")
ALL = ("phase", "zh", "zl", "yh", "x", "core")
MESH_ID = pl.DeviceIdType.MESH

eps = 1e-05
single = jnp.float32
brain = jnp.bfloat16


def place_of(axes, index):
    out = {}
    for name in reversed(axes):
        out[name] = lax.rem(index, SIZES[name])
        index = lax.div(index, SIZES[name])
    return out


def size_of(axes):
    total = 1
    for name in axes:
        total *= SIZES[name]
    return total


def my_place(axes):
    me = jnp.int32(0)
    for name in axes:
        me = me * SIZES[name] + lax.axis_index(name)
    return me


def greet(barrier, device):
    pl.semaphore_signal(barrier, inc=1, device_id=device, device_id_type=MESH_ID)


def send(source, target, send_sem, recv_sem, device):
    copy = pltpu.make_async_remote_copy(
        src_ref=source,
        dst_ref=target,
        send_sem=send_sem,
        recv_sem=recv_sem,
        device_id=device,
        device_id_type=MESH_ID,
    )
    copy.start()
    return copy


def team_copies(axes, modes, sources, targets, send_sem, recv_sem, own_sem):
    n = size_of(axes)
    me = my_place(axes)
    copies = []
    for k in range(1, n):
        peer = lax.rem(me + k, n)
        device = place_of(axes, peer)
        for item, mode in enumerate(modes):
            if mode in SIZES:
                continue
            source = sources[item].at[peer] if mode == "swap" else sources[item]
            copies.append(
                send(
                    source,
                    targets[item].at[me],
                    send_sem.at[item, k],
                    recv_sem.at[item, k],
                    device,
                )
            )
    for item, mode in enumerate(modes):
        slot = me
        source = sources[item] if mode == "gather" else sources[item].at[me]
        if mode in SIZES:
            slot = lax.axis_index(mode)
            source = sources[item].at[slot]
            copies.append(
                send(
                    sources[item].at[1 - slot],
                    targets[item].at[slot],
                    send_sem.at[item, 0],
                    recv_sem.at[item, 0],
                    {mode: 1 - slot},
                )
            )
        copy = pltpu.make_async_copy(source, targets[item].at[slot], own_sem.at[item])
        copy.start()
        copies.append(copy)
    return copies


def greet_team(barrier, axes):
    n = size_of(axes)
    me = my_place(axes)
    for k in range(1, n):
        greet(barrier, place_of(axes, lax.rem(me + k, n)))
    return n - 1


def exchange_kernel(axes, modes, *refs):
    count = len(modes)
    barrier = pltpu.get_barrier_semaphore()
    pl.semaphore_wait(barrier, greet_team(barrier, axes))
    copies = team_copies(axes, modes, refs[:count], refs[count : 2 * count], *refs[2 * count :])
    for copy in copies:
        copy.wait()


def received(axes, items):
    n = size_of(axes)
    return [
        jax.ShapeDtypeStruct(((n,) if mode == "gather" else ()) + array.shape, array.dtype)
        for array, mode in items
    ]


def call(kernel, arrays, shapes, scratch, number, name, microseconds):
    moved = sum(s.size * s.dtype.itemsize for s in shapes)
    return pl.pallas_call(
        kernel,
        out_shape=shapes,
        in_specs=[pl.BlockSpec(memory_space=pltpu.VMEM)] * len(arrays),
        out_specs=[pl.BlockSpec(memory_space=pltpu.VMEM)] * len(shapes),
        scratch_shapes=scratch,
        compiler_params=pltpu.CompilerParams(
            collective_id=number, has_side_effects=True, vmem_limit_bytes=48 << 20
        ),
        cost_estimate=pl.CostEstimate(
            flops=microseconds * 10**9, bytes_accessed=2 * moved, transcendentals=0
        ),
        name=name,
    )(*arrays)


def team_semaphores(axes, items):
    return [
        pltpu.SemaphoreType.DMA((len(items), size_of(axes))),
        pltpu.SemaphoreType.DMA((len(items), size_of(axes))),
        pltpu.SemaphoreType.DMA((len(items),)),
    ]


def exchange(items, axes, number, name):
    return call(
        functools.partial(exchange_kernel, axes, tuple(mode for _, mode in items)),
        [array for array, _ in items],
        received(axes, items),
        team_semaphores(axes, items),
        number,
        name,
        20,
    )


def rank_devices():
    yh, x, core = lax.axis_index("yh"), lax.axis_index("x"), lax.axis_index("core")
    across = [lax.rem(x + k, 4) for k in range(4)]
    out = []
    for dy in range(2):
        for dx in range(4):
            for dc in range(2):
                y_at = 1 - yh if dy else yh
                c_at = 1 - core if dc else core
                device = {"yh": y_at, "x": across[dx], "core": c_at}
                out.append((device, y_at * 8 + across[dx] * 2 + c_at))
    return out


def for_each_expert_place(action):
    z = lax.axis_index("zh") * 2 + lax.axis_index("zl")
    rank = rank_devices()

    def of_layer(layer, own):
        high, low = lax.div(layer, 2), lax.rem(layer, 2)
        for k, (device, at) in enumerate(rank):
            action(dict(device, zh=high, zl=low), layer * 16 + at, own and k == 0)

    of_layer(z, True)

    def step(k, carry):
        of_layer(lax.rem(z + k, 4), False)
        return carry

    lax.fori_loop(1, 4, step, 0)


def expert_exchange_kernel(count, modes, *refs):
    every = count + len(modes)
    sources, targets = refs[:every], refs[every : 2 * every]
    send_sem, recv_sem, own_sem, rows_sent, rows_got = refs[2 * every :]
    mine = my_place(DP)
    barrier = pltpu.get_barrier_semaphore()

    def welcome(device, at, own):
        if not own:
            greet(barrier, device)

    for_each_expert_place(welcome)
    pl.semaphore_wait(barrier, 63)
    team = team_copies(
        QUAD, modes, sources[count:], targets[count:], send_sem, recv_sem, own_sem
    )

    def give(device, at, own):
        for item in range(count):
            source, target = sources[item].at[at], targets[item].at[mine]
            if own:
                pltpu.make_async_copy(source, target, rows_got.at[item]).start()
            else:
                send(source, target, rows_sent.at[item], rows_got.at[item], device)

    for_each_expert_place(give)
    for item in range(count):
        sent = sources[item].at[pl.ds(0, 63)]
        pltpu.make_async_copy(sent, sent, rows_sent.at[item]).wait()
        pltpu.make_async_copy(targets[item], targets[item], rows_got.at[item]).wait()
    for copy in team:
        copy.wait()


def expert_exchange(rows, items, number, name):
    rows = [value.reshape(EXPERTS, SLOTS, WIDTH) for value in rows]
    count = len(rows)
    out = call(
        functools.partial(expert_exchange_kernel, count, tuple(mode for _, mode in items)),
        rows + [array for array, _ in items],
        [jax.ShapeDtypeStruct(value.shape, brain) for value in rows] + received(QUAD, items),
        team_semaphores(QUAD, items)
        + [pltpu.SemaphoreType.DMA((count,)), pltpu.SemaphoreType.DMA((count,))],
        number,
        name,
        40 * count,
    )
    rows_got = [value.reshape(EXPERTS * SLOTS, WIDTH) for value in out[:count]]
    return rows_got + list(out[count:])


def rank_gather_kernel(count, modes, *refs):
    every = count + len(modes)
    sources, targets = refs[:count], refs[every : every + count]
    team_sources, team_targets = refs[count:every], refs[every + count : 2 * every]
    send_sem, recv_sem, own_sem, *team_sems = refs[2 * every :]
    yh, x, core = lax.axis_index("yh"), lax.axis_index("x"), lax.axis_index("core")
    right, left, far = lax.rem(x + 1, 4), lax.rem(x + 3, 4), lax.rem(x + 2, 4)
    other = 1 - yh
    to_y, to_right, to_left, to_core = {"yh": other}, {"x": right}, {"x": left}, {"core": 1 - core}
    barrier = pltpu.get_barrier_semaphore()
    for device in (to_y, to_right, to_left, to_core):
        greet(barrier, device)
    pl.semaphore_wait(barrier, 4 + greet_team(barrier, TEAM))

    def slot(y_at, x_at):
        return y_at * 8 + x_at * 2 + core

    sent = []

    def pass_on(item, at, kind, device, source=None):
        target = targets[item].at[at]
        copy = send(
            target if source is None else source,
            target,
            send_sem.at[item, kind],
            recv_sem.at[item, kind],
            device,
        )
        sent.append(copy)
        return copy

    def arrived(item, kind):
        pltpu.make_async_copy(sources[item], sources[item], recv_sem.at[item, kind]).wait()

    items = range(count)
    me = slot(yh, x)
    own = []
    for item in items:
        pass_on(item, me, 0, to_y, sources[item])
        pass_on(item, me, 1, to_right, sources[item])
        pass_on(item, me, 2, to_left, sources[item])
        pass_on(item, me, 7, to_core, sources[item])
        copy = pltpu.make_async_copy(sources[item], targets[item].at[me], own_sem.at[item])
        copy.start()
        own.append(copy)
    team = team_copies(TEAM, modes, team_sources, team_targets, *team_sems)
    steps = (
        (1, slot(yh, left), ((5, to_right), (8, to_core))),
        (0, slot(other, x), ((3, to_right), (4, to_left), (9, to_core))),
        (2, slot(yh, right), ((10, to_core),)),
        (4, slot(other, right), ((6, to_left), (11, to_core))),
        (3, slot(other, left), ((12, to_core),)),
        (5, slot(yh, far), ((13, to_core),)),
        (6, slot(other, far), ((14, to_core),)),
    )
    for kind, at, onward in steps:
        for item in items:
            arrived(item, kind)
            for next_kind, device in onward:
                pass_on(item, at, next_kind, device)
    for item in items:
        for kind in range(7, 15):
            arrived(item, kind)
    for copy in own:
        copy.wait()
    for copy in sent:
        copy.wait_send()
    for copy in team:
        copy.wait()


def rank_gather(arrays, items, number, name):
    count = len(arrays)
    return call(
        functools.partial(rank_gather_kernel, count, tuple(mode for _, mode in items)),
        arrays + [array for array, _ in items],
        [jax.ShapeDtypeStruct((16,) + array.shape, array.dtype) for array in arrays]
        + received(TEAM, items),
        [
            pltpu.SemaphoreType.DMA((count, 15)),
            pltpu.SemaphoreType.DMA((count, 15)),
            pltpu.SemaphoreType.DMA((count,)),
        ]
        + team_semaphores(TEAM, items),
        number,
        name,
        40,
    )


def rank_sum_kernel(count, modes, *refs):
    every = count + len(modes)
    sources, team_sources = refs[:count], refs[count:every]
    targets, team_targets = refs[every : every + count], refs[every + count : 2 * every]
    refs = refs[2 * every :]
    from_core, totals, arrivals = (refs[k * count : (k + 1) * count] for k in range(3))
    send_sem, recv_sem, *team_sems = refs[3 * count :]
    yh, x, core = lax.axis_index("yh"), lax.axis_index("x"), lax.axis_index("core")
    right, left, far = lax.rem(x + 1, 4), lax.rem(x + 3, 4), lax.rem(x + 2, 4)
    other = 1 - yh
    to_y, to_right, to_left, to_core = {"yh": other}, {"x": right}, {"x": left}, {"core": 1 - core}
    barrier = pltpu.get_barrier_semaphore()
    for device in (to_y, to_right, to_left, to_core):
        greet(barrier, device)
    pl.semaphore_wait(barrier, 4 + greet_team(barrier, TEAM))
    items = range(count)
    sent = []

    def pass_on(item, at, kind, device):
        copy = send(
            totals[item].at[at],
            arrivals[item].at[kind],
            send_sem.at[item, kind],
            recv_sem.at[item, kind],
            device,
        )
        sent.append(copy)

    def arrived(item, kind):
        landed = arrivals[item].at[kind]
        pltpu.make_async_copy(landed, landed, recv_sem.at[item, kind]).wait()
        return arrivals[item][kind].astype(single)

    def slot(y_at, x_at):
        return y_at * 4 + x_at

    for item in items:
        sent.append(
            send(
                sources[item].at[:, 1 - core],
                from_core[item],
                send_sem.at[item, 7],
                recv_sem.at[item, 7],
                to_core,
            )
        )
    team = team_copies(TEAM, modes, team_sources, team_targets, *team_sems)
    for item in items:
        landed = from_core[item]
        pltpu.make_async_copy(landed, landed, recv_sem.at[item, 7]).wait()

        def add(at):
            value = sources[item][at, core].astype(single) + from_core[item][at].astype(single)
            totals[item][at] = value.astype(brain)

        add(slot(yh, far))
        pass_on(item, slot(yh, far), 0, to_right)
        add(slot(other, far))
        pass_on(item, slot(other, far), 1, to_left)
        add(slot(other, right))
        pass_on(item, slot(other, right), 3, to_right)
        add(slot(yh, left))
        pass_on(item, slot(yh, left), 5, to_left)
        for at in (slot(yh, right), slot(other, left), slot(yh, x), slot(other, x)):
            add(at)
    for item in items:
        at = slot(yh, right)
        totals[item][at] = (totals[item][at].astype(single) + arrived(item, 0)).astype(brain)
        pass_on(item, at, 2, to_right)
        at = slot(other, left)
        totals[item][at] = (totals[item][at].astype(single) + arrived(item, 1)).astype(brain)
        pass_on(item, at, 4, to_left)
    for item in items:
        at = slot(other, x)
        value = totals[item][at].astype(single) + arrived(item, 3)
        totals[item][at] = (value + arrived(item, 4)).astype(brain)
        pass_on(item, at, 6, to_y)
    for item in items:
        value = totals[item][slot(yh, x)].astype(single) + arrived(item, 5)
        value = value + arrived(item, 2)
        targets[item][...] = (value + arrived(item, 6)).astype(targets[item].dtype)
    for copy in sent:
        copy.wait_send()
    for copy in team:
        copy.wait()


def rank_sum(arrays, items, number, name):
    count = len(arrays)
    arrays = [array.reshape((8, 2) + array.shape[1:]) for array in arrays]
    pieces = [array.shape[2:] for array in arrays]
    scratch = [pltpu.VMEM((8,) + piece, brain) for piece in pieces]
    scratch += [pltpu.VMEM((8,) + piece, brain) for piece in pieces]
    scratch += [pltpu.VMEM((7,) + piece, brain) for piece in pieces]
    scratch += [pltpu.SemaphoreType.DMA((count, 8)), pltpu.SemaphoreType.DMA((count, 8))]
    return call(
        functools.partial(rank_sum_kernel, count, tuple(mode for _, mode in items)),
        arrays + [array for array, _ in items],
        [jax.ShapeDtypeStruct(piece, brain) for piece in pieces] + received(TEAM, items),
        scratch + team_semaphores(TEAM, items),
        number,
        name,
        45,
    )


def dot(left, right):
    return jnp.dot(left, right, preferred_element_type=single)


def dot_t(left, right):
    return lax.dot_general(left, right, (((1,), (1,)), ((), ())), preferred_element_type=single)


def t_dot(left, right):
    return lax.dot_general(left, right, (((0,), (0,)), ((), ())), preferred_element_type=single)


def exact(spec, left, right):
    return jnp.einsum(
        spec, left, right, precision=lax.Precision.HIGHEST, preferred_element_type=single
    )


def rms_scale(value, gain):
    return value * lax.rsqrt(jnp.mean(value * value, axis=-1, keepdims=True) + eps) * gain


def swiglu(value):
    half = value.shape[-1] // 2
    return jax.nn.silu(value[..., :half]) * value[..., half:]


def shuffle_matrix():
    to = jnp.arange(WIDTH, dtype=jnp.int32)
    origin = to // 12 % 8 * 192 + to // 96 * 12 + to % 12
    return (jnp.arange(WIDTH, dtype=jnp.int32)[:, None] == origin[None, :]).astype(brain)


def shuffle(value, matrix):
    return dot(value, matrix).astype(brain)


def unshuffle(value, matrix):
    high = value.astype(brain)
    lower = (value - high.astype(single)).astype(brain)
    both = dot_t(jnp.concatenate([high, lower], axis=0), matrix)
    return both[: value.shape[0]] + both[value.shape[0] :]


def after(values, first):
    return lax.optimization_barrier((values, first))[0]


def pad_rows(value, rows):
    return jnp.pad(value, [(0, 0)] * (value.ndim - 2) + [(0, rows - value.shape[-2]), (0, 0)])


def pad_to(value, rows, columns):
    return jnp.pad(value, ((0, rows - value.shape[0]), (0, columns - value.shape[1])))


def allowed_pairs(seg):
    position = jnp.arange(SEQ, dtype=jnp.int32)
    return (position[:, None] >= position[None, :]) & (seg[..., :, None] == seg[..., None, :])


def product(left, right, dims, precision=None):
    return lax.dot_general(
        left, right, (dims, ((), ())), precision=precision, preferred_element_type=single
    )


def sharp(left, right, dims):
    return product(left, right, dims, lax.Precision.HIGHEST)


def blunt(left, right, dims):
    return product(left.astype(brain), right.astype(brain), dims)


def mamba_parts(zx_ref, masks_ref, same_ref, taps_ref, heads_ref):
    zx = zx_ref[0]
    conv_in = zx[:, INNER : 2 * INNER + 2 * N]
    taps = taps_ref[...]
    same = same_ref[0]
    moved = [conv_in]
    for k in range(1, KW):
        moved.append(pltpu.roll(conv_in, k, 0) * same[:, k : k + 1])
    conv = taps[KW : KW + 1]
    for k in range(KW):
        conv = conv + taps[KW - 1 - k : KW - k] * moved[k]
    gate = jax.nn.sigmoid(conv)
    active = conv * gate
    heads = heads_ref[...]
    raw = zx[:, 2 * INNER + 2 * N :] + heads[0:1]
    step = jnp.maximum(raw, 0.0) + jnp.log1p(jnp.exp(-jnp.abs(raw)))
    rate = step * heads[1:2]
    rows = lax.broadcasted_iota(jnp.int32, (SEQ, SEQ), 0)
    columns = lax.broadcasted_iota(jnp.int32, (SEQ, SEQ), 1)
    lower = (rows >= columns).astype(single)
    total = sharp(lower, rate, ((1,), (0,)))
    total_t = sharp(rate, lower, ((0,), (1,)))
    unit = (rows == columns).astype(single)
    step_t = sharp(step, unit, ((0,), (1,)))
    values = active[:, :INNER]
    in_state, out_state = active[:, INNER : INNER + N], active[:, INNER + N :]
    meeting = sharp(out_state, in_state, ((1,), (1,)))
    allowed = masks_ref[0]
    decays = []
    results = []
    for h in range(HEADS_HERE):
        fall = jnp.exp(jnp.minimum(total[:, h : h + 1] - total_t[h : h + 1], 0.0)) * allowed
        mixing = fall * meeting * step_t[h : h + 1]
        decays.append((fall, mixing))
        results.append(blunt(mixing, values[:, h * P_SIZE : (h + 1) * P_SIZE], ((1,), (0,))))
    result = jnp.concatenate(results, axis=1) + taps[5:6, :INNER] * values
    z = zx[:, :INNER]
    open_z = jax.nn.sigmoid(z)
    return (
        (zx, taps, same, moved, conv, gate, heads, raw, step, step_t, unit, lower),
        (values, in_state, out_state, meeting, decays, result, z, open_z),
    )


def mamba_forward_kernel(zx_ref, masks_ref, same_ref, taps_ref, heads_ref, part_ref, squares_ref):
    (_, taps, *_), (*_, result, z, open_z) = mamba_parts(
        zx_ref, masks_ref, same_ref, taps_ref, heads_ref
    )
    gated = result * (z * open_z)
    part_ref[0] = (gated * taps[6:7, :INNER]).astype(brain)
    sums = sharp(jnp.ones((8, INNER), single), gated * gated, ((1,), (1,)))
    squares_ref[0] = jnp.concatenate([sums, jnp.zeros((8, 128 - SEQ), single)], axis=1)


def mamba_backward_kernel(
    zx_ref, masks_ref, same_ref, taps_ref, heads_ref, d_yn_ref, scalars_ref, d_zx_ref, yn_ref, sums_ref
):
    first, second = mamba_parts(zx_ref, masks_ref, same_ref, taps_ref, heads_ref)
    (zx, taps, same, moved, conv, gate, heads, raw, step, step_t, unit, lower) = first
    (values, in_state, out_state, meeting, decays, result, z, open_z) = second
    scalars = sharp(unit, scalars_ref[0][:, :SEQ], ((1,), (1,)))
    inverse, along = scalars[:, 0:1], scalars[:, 1:2]
    gain, skip = taps[6:7, :INNER], taps[5:6, :INNER]
    d_yn = d_yn_ref[0]
    shut = z * open_z
    gated = result * shut
    scaled = gated * inverse
    yn_ref[0] = (scaled * gain).astype(brain)
    d_gain = jnp.sum(d_yn * scaled, axis=0, keepdims=True)
    d_gated = inverse * gain * d_yn - gated * along
    d_z = d_gated * result * (open_z * (1.0 + z * (1.0 - open_z)))
    d_result = d_gated * shut
    d_skip = jnp.sum(d_result * values, axis=0, keepdims=True)
    lanes = lax.broadcasted_iota(jnp.int32, (1, 128), 1)
    rows = lax.broadcasted_iota(jnp.int32, (128, 1), 0)
    d_meeting = jnp.zeros((SEQ, SEQ), single)
    by_row = jnp.zeros((SEQ, 128), single)
    by_column = jnp.zeros((128, SEQ), single)
    d_step_t = jnp.zeros((128, SEQ), single)
    d_values = []
    for h in range(HEADS_HERE):
        fall, mixing = decays[h]
        own = slice(h * P_SIZE, (h + 1) * P_SIZE)
        d_mixing = blunt(d_result[:, own], values[:, own], ((1,), (1,)))
        d_values.append(blunt(mixing, d_result[:, own], ((0,), (0,))))
        spread = d_mixing * fall
        d_meeting = d_meeting + spread * step_t[h : h + 1]
        spread = spread * meeting
        moving = spread * step_t[h : h + 1]
        by_row = by_row + jnp.sum(moving, axis=1, keepdims=True) * (lanes == h).astype(single)
        at = (rows == h).astype(single)
        by_column = by_column + at * jnp.sum(moving, axis=0, keepdims=True)
        d_step_t = d_step_t + at * jnp.sum(spread, axis=0, keepdims=True)
    d_total = by_row - sharp(unit, by_column, ((1,), (1,)))
    d_rate = sharp(lower, d_total, ((0,), (0,)))
    d_step = sharp(unit, d_step_t, ((1,), (1,))) + d_rate * heads[1:2]
    d_raw = d_step * jax.nn.sigmoid(raw)
    d_decay = jnp.sum(d_rate * step, axis=0, keepdims=True) * heads[1:2]
    d_active = jnp.concatenate(
        [
            jnp.concatenate(d_values, axis=1) + skip * d_result,
            sharp(d_meeting, out_state, ((0,), (0,))),
            sharp(d_meeting, in_state, ((1,), (0,))),
        ],
        axis=1,
    )
    d_conv = d_active * (gate * (1.0 + conv * (1.0 - gate)))
    d_taps = [jnp.sum(d_conv * moved[KW - 1 - k], axis=0, keepdims=True) for k in range(KW)]
    d_in = taps[KW - 1 : KW] * d_conv
    for k in range(1, KW):
        d_in = d_in + pltpu.roll(
            taps[KW - 1 - k : KW - k] * (d_conv * same[:, k : k + 1]), SEQ - k, 0
        )
    d_zx_ref[0] = jnp.concatenate([d_z, d_in, d_raw], axis=1).astype(brain)
    wide = INNER + 2 * N

    def widen(value):
        return jnp.concatenate(
            [value, jnp.zeros((1, wide - value.shape[1]), single)], axis=1
        )

    sums = jnp.concatenate(
        d_taps
        + [jnp.sum(d_conv, axis=0, keepdims=True), widen(d_skip), widen(d_gain)]
        + [widen(jnp.sum(d_raw, axis=0, keepdims=True)), widen(d_decay)]
        + [jnp.zeros((7, wide), single)],
        axis=0,
    )

    @pl.when(pl.program_id(0) == 0)
    def _():
        sums_ref[...] = jnp.zeros_like(sums_ref)

    sums_ref[...] += sums


def by_sequence(kernel, arrays, fixed, shapes, total_shapes, name):
    def whole(shape):
        return pl.BlockSpec(shape, lambda n: (0,) * len(shape))

    def one(shape):
        return pl.BlockSpec((1,) + shape[1:], lambda n: (n,) + (0,) * (len(shape) - 1))

    return pl.pallas_call(
        kernel,
        grid=(PARTS,),
        out_shape=shapes + total_shapes,
        in_specs=[
            whole(array.shape) if place in fixed else one(array.shape)
            for place, array in enumerate(arrays)
        ],
        out_specs=[one(s.shape) for s in shapes] + [whole(s.shape) for s in total_shapes],
        compiler_params=pltpu.CompilerParams(vmem_limit_bytes=32 << 20),
        name=name,
    )(*arrays)


def attend_scores(queries, keys, seg):
    scores = exact("nird,njd->nrij", queries, keys) * HEAD_SIZE ** (-0.5)
    scores = jnp.where(allowed_pairs(seg)[:, None], scores, -1e30)
    return jax.nn.softmax(scores, axis=-1)


def attend_mix(probs, values):
    return exact("nrij,njd->nird", probs, values)


def per_device(
    block_input,
    cotangent,
    segments,
    routes,
    in_proj,
    conv_taps,
    conv_bias,
    step_bias,
    decay_log,
    skip_weight,
    norm_gain,
    out_proj,
    query_proj,
    key_value_projection,
    attn_out_proj,
    norm_gains,
    router,
    shared_in,
    shared_out,
    experts_in,
    experts_out,
):
    phase = lax.axis_index("phase")
    first_phase = phase == 0
    zl = lax.axis_index("zl")
    team = phase * 4 + lax.axis_index("zh") * 2 + zl

    def mine(value):
        return lax.dynamic_index_in_dim(value, phase, 0, keepdims=False)

    start = mine(block_input)
    cot = mine(cotangent)
    seg = mine(segments)
    route_rows = mine(routes)

    both_ways = [(0, 1), (1, 0)]
    w_first, w_second = experts_in[0, 0], experts_out[0, 0]

    z_piece = in_proj[:, :DI].reshape(12, PARTS, INNER).transpose(1, 0, 2)
    x_piece = in_proj[:, DI : 2 * DI].reshape(12, PARTS, INNER).transpose(1, 0, 2)
    state_piece = jnp.broadcast_to(in_proj[None, :, 2 * DI : 2 * DI + 2 * N], (PARTS, 12, 2 * N))
    step_piece = in_proj[:, 2 * DI + 2 * N :].reshape(12, PARTS, HEADS_HERE).transpose(1, 0, 2)
    step_piece = jnp.pad(step_piece, ((0, 0), (0, 0), (0, 128 - HEADS_HERE)))
    q_piece = query_proj.reshape(12, 4, 384).transpose(1, 0, 2)
    kv_piece = key_value_projection.reshape(12, 2, 4, 128).transpose(2, 0, 1, 3).reshape(4, 12, 256)
    qkv_piece = jnp.repeat(jnp.concatenate([q_piece, kv_piece], axis=2), 2, axis=0)
    in_piece = pad_rows(jnp.concatenate([z_piece, x_piece, state_piece, step_piece], axis=2), 16)
    qkv_piece = pad_rows(qkv_piece, 16)
    sin_piece = shared_in[0].reshape(24, 2, 4, 256).transpose(2, 0, 1, 3).reshape(4, 24, 512)
    sin_piece = pad_rows(jnp.concatenate([sin_piece, sin_piece], axis=0), 32)
    sout_piece = jnp.broadcast_to(shared_out, (2, 16, WIDTH))
    attn_piece = jnp.broadcast_to(pad_rows(attn_out_proj, 16)[None], (2, 16, WIDTH))
    mixing = shuffle_matrix()
    rest = jnp.concatenate(
        [conv_taps.reshape(-1), conv_bias, norm_gain, norm_gains[0].reshape(-1)]
    )
    rest = jnp.pad(rest, (0, 512 - rest.shape[0])).reshape(4, 128)
    small = jnp.concatenate([router[0].reshape(12, 128), rest], axis=0)
    seg_piece = pad_to(seg, 8, 128)
    in_got, sin_got, sout_got, small_got, seg_got = exchange(
        [
            (in_piece, "swap"),
            (sin_piece, "swap"),
            (sout_piece, "phase"),
            (small, "gather"),
            (seg_piece, "gather"),
        ],
        TEAM,
        0,
        "team_start",
    )
    seg_all = seg_got[:, 0, :SEQ]
    sin_got = sin_got[:, :24].reshape(2, 96, 512)

    def to_other_phase(value):
        return lax.ppermute(value, "phase", both_ways)

    def in_turn(value, count=3):
        pieces = []
        for piece in jnp.split(value, count, axis=0):
            pieces.append(to_other_phase(after(piece, pieces[-1]) if pieces else piece))
        return pieces

    half = WIDTH // 2
    w_second_far = to_other_phase(w_second)
    in_rows, w_second_far = lax.optimization_barrier(
        (in_got[:, :12].reshape(96, IN_COLS), w_second_far)
    )
    first_pieces = in_turn(after(w_first[:half], w_second_far))
    w_in, small_all, w_out, start_all, qkv_got, attn_got = rank_gather(
        [in_rows, small_got.reshape(128, 128), pad_rows(out_proj, 32)],
        [(shuffle(start, mixing), "gather"), (qkv_piece, "swap"), (attn_piece, "zl")],
        1,
        "rank_weights",
    )
    w_in = w_in.reshape(WIDTH, IN_COLS)
    w_out = w_out[:, :24].reshape(INNER, WIDTH)
    later_wide = jnp.concatenate([qkv_got[:, :12].reshape(96, QKV_COLS), sin_got[1]], axis=1)
    later_tall = jnp.concatenate([attn_got[:, :12].reshape(24, WIDTH), sout_got[1]], axis=0)
    start_all, first_pieces = lax.optimization_barrier((start_all, first_pieces))
    second_pieces = in_turn(after(w_first[half:], first_pieces[-1]))
    later_wide = lax.all_gather(later_wide, RANK, axis=0)
    later_tall = lax.all_gather(later_tall, RANK, axis=0)
    w_qkv = later_wide[:, :, :QKV_COLS].reshape(WIDTH, QKV_COLS)
    w_attn = later_tall[:, :24].reshape(16, 2, 12, WIDTH).transpose(1, 0, 2, 3)
    w_attn = w_attn.reshape(384, WIDTH)

    def hidden_in(value):
        return value.reshape(16, 4, 24, 512).transpose(1, 0, 2, 3).reshape(WIDTH, 512)

    small_all = small_all.reshape(16, 2, 4, 16, 128)
    router_full = small_all[:, :, :, :12].reshape(16, 2, 4, 24, EXPERTS).transpose(1, 2, 0, 3, 4)
    router_full = router_full.reshape(2, WIDTH, EXPERTS)
    rest_all = small_all[:, :, :, 12:].reshape(16, 2, 4, 512)
    conv_full = rest_all[..., :130].reshape(16, 2, 4, 5, 26).transpose(3, 1, 2, 0, 4)
    conv_full = conv_full.reshape(5, CONVW).astype(single)
    gain_here = rest_all[..., 130:154].reshape(16, 8, 24)
    gain_here = lax.dynamic_index_in_dim(gain_here, team, 1, keepdims=False)
    gain_here = gain_here.reshape(INNER).astype(single)
    gains = rest_all[..., 154:202].reshape(16, 2, 4, 2, 24).transpose(1, 3, 2, 0, 4)
    gains = gains.reshape(2, 2, WIDTH).astype(single)
    conv_here = jnp.concatenate(
        [lax.dynamic_slice_in_dim(conv_full[:, :DI], team * INNER, INNER, 1), conv_full[:, DI:]],
        axis=1,
    )

    def heads_of(value):
        return lax.dynamic_slice_in_dim(value, team * HEADS_HERE, HEADS_HERE, 0)

    skip_wide = jnp.repeat(heads_of(skip_weight), P_SIZE)
    columns = jnp.stack([jnp.pad(skip_wide, (0, 2 * N)), jnp.pad(gain_here, (0, 2 * N))])
    taps_here = jnp.concatenate([conv_here, columns, jnp.zeros((1, INNER + 2 * N), single)], axis=0)
    heads_here = jnp.stack([heads_of(step_bias), -jnp.exp(heads_of(decay_log))])
    heads_here = pad_to(heads_here, 8, 128)
    allowed_all = allowed_pairs(seg_all).astype(single)
    same_all = [
        jnp.pad(seg_all[:, k:] == seg_all[:, : SEQ - k], ((0, 0), (k, 0))) for k in range(KW)
    ]
    same_all = jnp.pad(jnp.stack(same_all, axis=2).astype(single), ((0, 0), (0, 0), (0, 128 - KW)))

    expert_ids = jnp.arange(EXPERTS, dtype=jnp.int32)
    named = jnp.any(route_rows[:, :, None] == expert_ids, axis=1)
    position = jnp.arange(SEQ, dtype=jnp.int32)
    earlier = (position[:, None] > position[None, :]).astype(brain)
    slot = dot(earlier, named.astype(brain))
    slot = jnp.where(named, slot, -1.0).astype(brain)
    cell = jnp.arange(EXPERTS * SLOTS, dtype=jnp.int32)
    spread = (cell[None, :] // SLOTS == expert_ids[:, None]).astype(brain)
    taken = dot(slot, spread) == (cell % SLOTS).astype(single)
    taken_b = taken.astype(brain)

    def of_block(s):
        own = phase == s
        return (
            jnp.where(own, w_first, w_first_far),
            jnp.where(own, w_second, w_second_far),
        )

    def moe_open(s, hidden):
        normed = rms_scale(hidden, gains[s, 1]).astype(brain)
        logits = dot(normed, router_full[s])
        top = jnp.max(jnp.where(named, logits, -jnp.inf), axis=1, keepdims=True)
        weight = jnp.where(named, jnp.exp(logits - top), 0.0)
        gates = weight / jnp.sum(weight, axis=1, keepdims=True)
        gates_wide = jnp.where(taken, exact("ie,ec->ic", gates, spread.astype(single)), 0.0)
        return normed, gates, gates_wide, t_dot(taken_b, normed).astype(brain)

    def moe_experts(weights, rows_in):
        both = dot(rows_in, weights[0])
        hid = swiglu(both).astype(brain)
        return both, hid, dot(hid, weights[1]).astype(brain)

    def moe_shared(s, normed_all):
        both = dot(normed_all, sin_full[s])
        hid = swiglu(both).astype(brain)
        part = dot(hid, sout_full[s]).astype(brain)
        return both, hid, part.reshape(4, SEQ, WIDTH)

    def moe_join(hidden, gates_wide, back, shared_got):
        high = gates_wide.astype(brain)
        lower = (gates_wide - high.astype(single)).astype(brain)
        moe = dot(high, back) + dot(lower, back)
        return (hidden + moe + jnp.sum(shared_got.astype(single), axis=0)).astype(brain)

    def back_open(d_out, gates_wide):
        gate_cell = jnp.sum(gates_wide, axis=0)
        return (t_dot(taken_b, d_out) * gate_cell[:, None]).astype(brain)

    def back_experts(weights, d_answer, both):
        d_hid = dot_t(d_answer, weights[1])
        d_both = jax.vjp(swiglu, both)[1](d_hid)[0].astype(brain)
        return d_both, dot_t(d_both, weights[0]).astype(brain)

    def back_shared(s, d_out_all, normed_all, both, hid):
        d_hid = dot_t(d_out_all, sout_full[s])
        d_sout = t_dot(hid, d_out_all)
        d_both = jax.vjp(swiglu, both)[1](d_hid)[0].astype(brain)
        d_sin = t_dot(normed_all, d_both)
        d_part = dot_t(d_both, sin_full[s]).astype(brain).reshape(4, SEQ, WIDTH)
        return d_sin, d_sout, d_part

    def back_join(s, d_out, hidden, normed, gates, back, returned, d_shared_got):
        d_cells = jnp.where(taken, dot_t(d_out, back), 0.0)
        d_gates = exact("ic,ec->ie", d_cells, spread.astype(single))
        d_logits = gates * (d_gates - jnp.sum(gates * d_gates, axis=1, keepdims=True))
        d_normed = exact("ie,we->iw", d_logits, router_full[s].astype(single))
        d_router = exact("iw,ie->we", normed.astype(single), d_logits)
        d_normed = d_normed + dot(taken_b, returned) + jnp.sum(d_shared_got.astype(single), axis=0)
        d_hidden, d_gain = jax.vjp(rms_scale, hidden, gains[s, 1])[1](d_normed)
        return d_hidden + d_out.astype(single), d_gain, d_router

    def shared_in_parts(value):
        return value.astype(brain).reshape(4, 16, 24, 512).transpose(1, 0, 2, 3).reshape(16, 96, 512)

    u0 = start.astype(single)
    shuffled_gain = shuffle(gains[0, 0][None].astype(brain), mixing)[0].astype(single)
    n1_all = rms_scale(start_all.astype(single), shuffled_gain).astype(brain)
    n1_all = n1_all.reshape(PARTS * SEQ, WIDTH)
    zx = dot(n1_all, w_in).reshape(PARTS, SEQ, IN_COLS)

    core_inputs = [zx, allowed_all, same_all, taps_here, heads_here]
    part, squares = by_sequence(
        mamba_forward_kernel,
        core_inputs,
        (3, 4),
        [
            jax.ShapeDtypeStruct((PARTS, SEQ, INNER), brain),
            jax.ShapeDtypeStruct((PARTS, 8, 128), single),
        ],
        [],
        "mamba_forward",
    )
    part = dot(part.reshape(PARTS * SEQ, INNER), w_out)
    part = part.astype(brain).reshape(PARTS, SEQ, WIDTH)
    part, second_pieces = lax.optimization_barrier((part, second_pieces))
    w_first_far = jnp.concatenate(first_pieces + second_pieces, axis=0)
    sin_all, sout_all, part_got, squares_got = rank_gather(
        [sin_got[0], sout_got[0]], [(part, "swap"), (squares, "swap")], 2, "team_mixed_0"
    )
    sin_full = (hidden_in(sin_all), hidden_in(later_wide[:, :, QKV_COLS:]))
    sout_full = (sout_all.reshape(256, WIDTH), later_tall[:, 24:].reshape(256, WIDTH))
    mean_square = jnp.sum(squares_got[:, 0, :SEQ], axis=0) / DI
    inverse = lax.rsqrt(mean_square + eps)
    mixed0 = jnp.sum(part_got.astype(single), axis=0) * inverse[:, None]
    hidden0 = u0 + mixed0
    normed0, gates0, gates_wide0, rows_out0 = moe_open(0, hidden0)
    rows_in0, normed_all0 = expert_exchange([rows_out0], [(normed0, "gather")], 3, "spread_0")
    normed_all0 = normed_all0.reshape(4 * SEQ, WIDTH)
    weights0 = of_block(0)
    sboth0, shid0, shared_part0 = moe_shared(0, normed_all0)
    both0, hid0, answer0 = moe_experts(weights0, rows_in0)
    back0, shared_got0 = expert_exchange([answer0], [(shared_part0, "swap")], 4, "collect_0")
    out0 = moe_join(hidden0, gates_wide0, back0, shared_got0)

    u1 = out0.astype(single)
    n1 = rms_scale(u1, gains[1, 0]).astype(brain)
    (n1_half,) = exchange([(shuffle(n1, mixing), "gather")], HALF, 5, "half_n1")
    n1_half = n1_half.reshape(4 * SEQ, WIDTH)
    seg_half = lax.dynamic_index_in_dim(seg_all.reshape(4, 2, SEQ), zl, 1, keepdims=False)
    qkv = dot(n1_half, w_qkv).astype(brain).astype(single).reshape(4, SEQ, QKV_COLS)
    queries = qkv[..., :384].reshape(4, SEQ, 3, HEAD_SIZE)
    keys, values = qkv[..., 384:512], qkv[..., 512:]
    probs, score_pull = jax.vjp(lambda q, k: attend_scores(q, k, seg_half), queries, keys)
    heads, mix_pull = jax.vjp(attend_mix, probs.astype(brain).astype(single), values)
    heads = heads.astype(brain).reshape(4 * SEQ, 384)
    part1 = dot(heads, w_attn).astype(brain).reshape(4, SEQ, WIDTH)
    (part1_got,) = exchange([(part1, "swap")], HALF, 6, "half_mixed")
    mixed1 = jnp.sum(part1_got.astype(single), axis=0)
    hidden1 = u1 + mixed1

    normed1, gates1, gates_wide1, rows_out1 = moe_open(1, hidden1)
    rows_in1, d_answer1, normed_all1, cot_all = expert_exchange(
        [rows_out1, back_open(cot, gates_wide1)],
        [(normed1, "gather"), (cot, "gather")],
        7,
        "spread_1",
    )
    normed_all1 = normed_all1.reshape(4 * SEQ, WIDTH)
    cot_all = cot_all.reshape(4 * SEQ, WIDTH)
    weights1 = of_block(1)
    sboth1, shid1, shared_part1 = moe_shared(1, normed_all1)
    d_sin1, d_sout1, d_shared1 = back_shared(1, cot_all, normed_all1, sboth1, shid1)
    both1, hid1, answer1 = moe_experts(weights1, rows_in1)
    d_both1, d_rows1 = back_experts(weights1, d_answer1, both1)
    back1, returned1, shared_got1, d_shared_got1 = expert_exchange(
        [answer1, d_rows1], [(shared_part1, "swap"), (d_shared1, "swap")], 8, "collect_1"
    )
    out1 = moe_join(hidden1, gates_wide1, back1, shared_got1)

    d_hid1, d_gain11, d_router1 = back_join(
        1, cot, hidden1, normed1, gates1, back1, returned1, d_shared_got1
    )
    (d_mixed1,) = exchange([(d_hid1.astype(brain), "gather")], HALF, 11, "half_dmixed")
    d_mixed1 = d_mixed1.reshape(4 * SEQ, WIDTH)
    d_heads = dot_t(d_mixed1, w_attn).reshape(4, SEQ, 3, HEAD_SIZE)
    d_attn = t_dot(heads, d_mixed1)
    d_probs, d_values = mix_pull(d_heads)
    d_queries, d_keys = score_pull(d_probs)
    d_qkv = jnp.concatenate([d_queries.reshape(4, SEQ, 384), d_keys, d_values], axis=2)
    d_qkv = d_qkv.astype(brain).reshape(4 * SEQ, QKV_COLS)
    d_w_qkv = t_dot(n1_half, d_qkv)
    d_n1_part = dot_t(d_qkv, w_qkv).astype(brain).reshape(4, SEQ, WIDTH)
    grads_wide = jnp.concatenate(
        [d_w_qkv.astype(brain).reshape(16, 96, QKV_COLS), shared_in_parts(d_sin1)], axis=2
    )
    attn_part = d_attn.astype(brain).reshape(2, 16, 12, WIDTH).transpose(1, 0, 2, 3)
    grads_tall = jnp.concatenate(
        [attn_part.reshape(16, 24, WIDTH), d_sout1.astype(brain).reshape(16, 16, WIDTH)], axis=1
    )
    grads_tall = jnp.pad(grads_tall.reshape(16, 40 * WIDTH), ((0, 0), (0, 54 * IN_COLS - 40 * WIDTH)))
    grads_later = jnp.concatenate([grads_wide, grads_tall.reshape(16, 54, IN_COLS)], axis=1)
    d_n1_part, grads_later = lax.optimization_barrier((d_n1_part, grads_later))
    grads_later = lax.psum_scatter(grads_later, RANK, scatter_dimension=0, tiled=True)[0]
    (d_n1_got,) = exchange([(d_n1_part, "swap")], HALF, 12, "half_dn1")
    d_n1 = unshuffle(jnp.sum(d_n1_got.astype(single), axis=0), mixing)
    d_u1, d_gain10 = jax.vjp(rms_scale, u1, gains[1, 0])[1](d_n1)
    d_u1 = (d_u1 + d_hid1).astype(brain)

    d_answer0, d_out0_all = expert_exchange(
        [back_open(d_u1, gates_wide0)], [(d_u1, "gather")], 13, "spread_back_0"
    )
    d_out0_all = d_out0_all.reshape(4 * SEQ, WIDTH)
    d_sin0, d_sout0, d_shared0 = back_shared(0, d_out0_all, normed_all0, sboth0, shid0)
    d_both0, d_rows0 = back_experts(weights0, d_answer0, both0)
    expert0 = (rows_in0, d_both0, hid0, d_answer0)
    expert1 = (rows_in1, d_both1, hid1, d_answer1)
    give_rows, give_both, give_hid, give_answer = (
        jnp.where(first_phase, b, a) for a, b in zip(expert0, expert1)
    )
    give_first = t_dot(give_rows, give_both).astype(brain)
    give_second = t_dot(give_hid, give_answer).astype(brain)
    d_rows0, give_first, give_second = lax.optimization_barrier((d_rows0, give_first, give_second))
    far_second = to_other_phase(give_second)
    returned0, d_shared_got0 = expert_exchange(
        [d_rows0], [(d_shared0, "swap")], 14, "collect_back_0"
    )
    d_hid0, d_gain01, d_router0 = back_join(
        0, d_u1, hidden0, normed0, gates0, back0, returned0, d_shared_got0
    )
    d_mixed0 = d_hid0.astype(brain)
    along = jnp.sum(d_mixed0.astype(single) * mixed0, axis=1)
    scalars = jnp.stack([inverse, inverse * inverse * along / DI])
    d_mixed0, far_second = lax.optimization_barrier((d_mixed0, far_second))
    sin_part0, sout_part0, d_mixed0, scalars_all = rank_sum(
        [shared_in_parts(d_sin0), d_sout0.astype(brain).reshape(16, 16, WIDTH)],
        [(d_mixed0, "gather"), (pad_to(scalars, 8, 128), "gather")],
        15,
        "team_dmixed",
    )
    far_first = in_turn(after(give_first[:half], d_mixed0))
    d_mixed0 = d_mixed0.reshape(PARTS * SEQ, WIDTH)
    d_yn = dot_t(d_mixed0, w_out).reshape(PARTS, SEQ, INNER)
    d_zx, yn, core_sums = by_sequence(
        mamba_backward_kernel,
        core_inputs + [d_yn, scalars_all],
        (3, 4),
        [
            jax.ShapeDtypeStruct((PARTS, SEQ, IN_COLS), brain),
            jax.ShapeDtypeStruct((PARTS, SEQ, INNER), brain),
        ],
        [jax.ShapeDtypeStruct((16, INNER + 2 * N), single)],
        "mamba_backward",
    )
    d_w_out = t_dot(yn.reshape(PARTS * SEQ, INNER), d_mixed0)
    d_zx = d_zx.reshape(PARTS * SEQ, IN_COLS)
    d_norm_gain = core_sums[6, :INNER]
    d_skip = jnp.sum(core_sums[5, :INNER].reshape(HEADS_HERE, P_SIZE), axis=1)
    d_step, d_decay = core_sums[7, :HEADS_HERE], core_sums[8, :HEADS_HERE]
    d_w_in = t_dot(n1_all, d_zx)
    d_n1_part0 = dot_t(d_zx, w_in).astype(brain)
    shuffled = start_all.astype(single)
    shuffled = shuffled * lax.rsqrt(jnp.mean(shuffled * shuffled, axis=-1, keepdims=True) + eps)
    d_gain00 = jnp.sum(
        shuffled.reshape(PARTS * SEQ, WIDTH) * d_n1_part0.astype(single), axis=0
    )
    d_gain00 = d_gain00.reshape(16, 8, 12).transpose(1, 0, 2).reshape(WIDTH)
    d_n1_part0 = d_n1_part0.reshape(PARTS, SEQ, WIDTH)
    d_n1_part0, grads_later, first_pieces = lax.optimization_barrier(
        (d_n1_part0, grads_later, far_first)
    )
    second_piece = to_other_phase(after(give_first[half:], first_pieces[-1]))

    qkv_part = grads_later[:96, :QKV_COLS].reshape(PARTS, 12, QKV_COLS)
    sin_part1 = grads_later[:96, QKV_COLS:].reshape(4, 24, 512)
    grads_tall = grads_later[96:].reshape(54 * IN_COLS)[: 40 * WIDTH].reshape(40, WIDTH)
    attn_part, sout_part1 = grads_tall[:24].reshape(2, 12, WIDTH), grads_tall[24:]

    conv_grads = core_sums[: KW + 1]
    conv_all = jnp.concatenate(
        [
            lax.dynamic_update_slice_in_dim(
                jnp.zeros((KW + 1, DI), single), conv_grads[:, :INNER], team * INNER, 1
            ),
            conv_grads[:, INNER:],
        ],
        axis=1,
    )
    conv_all = conv_all.reshape(5, 8, 16, 26).transpose(2, 1, 0, 3).reshape(16, 8, 130)
    head_all = lax.dynamic_update_slice_in_dim(
        jnp.zeros((3, H), single), jnp.stack([d_step, d_decay, d_skip]), team * HEADS_HERE, 1
    )
    head_all = jnp.broadcast_to(head_all.reshape(1, 1, 3 * H), (16, 8, 3 * H))
    gain_all = lax.dynamic_update_slice_in_dim(
        jnp.zeros((16, 8, 24), single), d_norm_gain.reshape(16, 1, 24), team, 1
    )
    d_gains = jnp.stack([jnp.stack([d_gain00, d_gain01]), jnp.stack([d_gain10, d_gain11])])
    d_gains = d_gains.reshape(2, 2, 4, 16, 24).transpose(3, 0, 2, 1, 4).reshape(16, 8, 48)
    d_router = jnp.stack([d_router0, d_router1]).reshape(2, 4, 16, 24 * EXPERTS)
    d_router = d_router.transpose(2, 0, 1, 3).reshape(16, 8, 24 * EXPERTS)
    small_grads = jnp.concatenate([d_router, conv_all, gain_all, d_gains, head_all], axis=2)
    small_grads = jnp.pad(small_grads, ((0, 0), (0, 0), (0, 2048 - small_grads.shape[2])))
    small_grads = small_grads.astype(brain).reshape(16, 128, 128)
    main_part, out_proj_grad, small_part, d_n1_got0, phase_outputs = rank_sum(
        [
            d_w_in.astype(brain).reshape(16, 96, IN_COLS),
            pad_rows(d_w_out.astype(brain).reshape(16, 24, WIDTH), 32),
            small_grads,
        ],
        [(d_n1_part0, "swap"), (jnp.stack([out0, out1]), "phase")],
        17,
        "rank_grads",
    )
    main_part = main_part.reshape(PARTS, 12, IN_COLS)
    sin_part0 = sin_part0.reshape(4, 24, 512)
    d_n1_0 = unshuffle(jnp.sum(d_n1_got0.astype(single), axis=0), mixing)
    (d_u0,) = jax.vjp(lambda value: rms_scale(value, gains[0, 0]), u0)[1](d_n1_0)
    d_u0 = d_u0 + d_hid0

    rows_kept, d_both_kept, hid_kept, d_answer_kept = (
        jnp.where(first_phase, a, b) for a, b in zip(expert0, expert1)
    )
    main_part, second_piece = lax.optimization_barrier((main_part, second_piece))
    far_first = jnp.concatenate(first_pieces + [second_piece], axis=0)
    experts_in_grad = t_dot(rows_kept, d_both_kept) + far_first.astype(single)
    experts_out_grad = t_dot(hid_kept, d_answer_kept) + far_second.astype(single)

    main_end, qkv_end, sin_end, sout_end, attn_end, small_end, input_grads = exchange(
        [
            (pad_rows(main_part, 16), "swap"),
            (pad_rows(qkv_part, 16), "swap"),
            (pad_rows(jnp.concatenate([sin_part0, sin_part1], axis=0), 32), "swap"),
            (jnp.stack([sout_part0, sout_part1]), "phase"),
            (pad_rows(attn_part, 16), "zl"),
            (small_part.reshape(PARTS, 16, 128), "swap"),
            (jnp.stack([d_u0, d_u1.astype(single)]), "phase"),
        ],
        TEAM,
        18,
        "team_end",
    )
    rows_end = main_end[:, :12].astype(single)

    def side_by_side(value):
        return value.transpose(1, 0, 2).reshape(value.shape[1], -1)

    in_proj_grad = jnp.concatenate(
        [
            side_by_side(rows_end[:, :, :INNER]),
            side_by_side(rows_end[:, :, INNER : 2 * INNER]),
            jnp.sum(rows_end[:, :, 2 * INNER : 2 * INNER + 2 * N], axis=0),
            side_by_side(
                rows_end[:, :, 2 * INNER + 2 * N : 2 * INNER + 2 * N + HEADS_HERE]
            ),
        ],
        axis=1,
    )
    small_end = jnp.sum(small_end.astype(single), axis=0).reshape(2048)
    router_grad = small_end[: 24 * EXPERTS].reshape(1, 24, EXPERTS)
    at = 24 * EXPERTS
    conv_end = small_end[at : at + 130].reshape(5, 26)
    at += 130
    norm_gain_grad = small_end[at : at + 24]
    at += 24
    norm_gains_grad = small_end[at : at + 48].reshape(1, 2, 24)
    at += 48
    heads_end = small_end[at : at + 3 * H].reshape(3, H)
    qkv_end = qkv_end[:, :12].astype(single).reshape(4, 2, 12, QKV_COLS)
    qkv_end = jnp.sum(qkv_end, axis=1)
    query_grad = side_by_side(qkv_end[:, :, :384])
    kv_grad = qkv_end[:, :, 384:].reshape(4, 12, 2, 128).transpose(1, 2, 0, 3).reshape(12, 1024)
    sin_end = jnp.sum(sin_end[:, :24].astype(single).reshape(2, 4, 24, 2, 256), axis=0)
    shared_in_grad = sin_end.transpose(1, 2, 0, 3).reshape(1, 24, 2048)
    shared_out_grad = jnp.sum(sout_end.astype(single), axis=0)[None]
    attn_out_grad = jnp.sum(attn_end[:, :12].astype(single), axis=0)

    return (
        phase_outputs[None],
        input_grads[None],
        in_proj_grad,
        conv_end[:KW],
        conv_end[KW],
        heads_end[0],
        heads_end[1],
        heads_end[2],
        norm_gain_grad,
        out_proj_grad[:24].astype(single),
        query_grad,
        kv_grad,
        attn_out_grad,
        norm_gains_grad,
        router_grad,
        shared_in_grad,
        shared_out_grad,
        experts_in_grad[None, None],
        experts_out_grad[None, None],
    )


def solution(mesh):
    fine = Mesh(mesh.devices.reshape(tuple(SIZES.values())), ALL)
    in_specs = (
        P(None, DP, None),
        P(None, DP, None),
        P(None, DP, None),
        P(None, DP, None),
        P(ALL, None),
        P(None, ALL),
        P(ALL),
        P(),
        P(),
        P(),
        P(ALL),
        P(ALL, None),
        P(ALL, None),
        P(ALL, None),
        P(ALL, None),
        P("phase", None, DP),
        P("phase", DP, None),
        P("phase", DP, None),
        P("phase", DP, None),
        P("phase", DP, None, None),
        P("phase", DP, None, None),
    )
    out_specs = (
        P("phase", None, DP, None),
        P("phase", None, DP, None),
        P(ALL, None),
        P(None, ALL),
        P(ALL),
        P(),
        P(),
        P(),
        P(ALL),
        P(ALL, None),
        P(ALL, None),
        P(ALL, None),
        P(ALL, None),
        P("phase", None, DP),
        P("phase", DP, None),
        P("phase", DP, None),
        P("phase", DP, None),
        P("phase", DP, None, None),
        P("phase", DP, None, None),
    )
    return jax.shard_map(
        per_device, mesh=fine, in_specs=in_specs, out_specs=out_specs, check_vma=False
    )
```
